32 devices in a mesh: fsdp: 2 (over x), ctx: 4 (over y, core), tp: 4 (over z).
Axes of the slice: x: 2, y: 2, z: 4, core: 2. Of those that a mesh axis runs over, the one named last changes fastest.
Arguments:
- stream_in: bfloat16 [8192, 2048], P(('fsdp', 'ctx', 'tp')), may hold values from -6 to 6
- stream_grad: bfloat16 [8192, 2048], P(('fsdp', 'ctx', 'tp')), may hold values from -6 to 6
- segments: int32 [8192], P('fsdp'), may hold values from 0 to 8, as said below
- positions: int32 [8192], P('fsdp'), may hold values from 0 to 2431, as said below
- first_gain: float32 [2048], replicated, may hold values from 0.5 to 1.5
- first_shift: float32 [2048], replicated, may hold values from -3 to 3
- second_gain: float32 [2048], replicated, may hold values from 0.5 to 1.5
- second_shift: float32 [2048], replicated, may hold values from -3 to 3
- attend_weight: bfloat16 [2048, 8, 768], P(('fsdp', 'ctx'), 'tp'), may hold values from -0.125 to 0.125
- attend_bias: float32 [8, 768], P('tp'), may hold values from -3 to 3
- output_weight: bfloat16 [2048, 2048], P(('fsdp', 'ctx'), 'tp'), may hold values from -1 to 1
- expand_weight: bfloat16 [2048, 8192], P(('fsdp', 'ctx'), 'tp'), may hold values from -0.125 to 0.125
- expand_bias: float32 [8192], P('tp'), may hold values from -3 to 3
- contract_weight: bfloat16 [2048, 8192], P(('fsdp', 'ctx'), 'tp'), may hold values from -0.0625 to 0.0625
- output_bias: float32 [2048], replicated, may hold values from -3 to 3
Outputs:
- stream_out: bfloat16 [8192, 2048], P(('fsdp', 'ctx', 'tp'))
- input_grad: float32 [8192, 2048], P(('fsdp', 'ctx', 'tp'))
- first_gain_grad: float32 [2048], replicated
- first_shift_grad: float32 [2048], replicated
- second_gain_grad: float32 [2048], replicated
- second_shift_grad: float32 [2048], replicated
- attend_weight_grad: float32 [2048, 8, 768], P(('fsdp', 'ctx'), 'tp')
- attend_bias_grad: float32 [8, 768], P('tp')
- output_weight_grad: float32 [2048, 2048], P(('fsdp', 'ctx'), 'tp')
- expand_weight_grad: float32 [2048, 8192], P(('fsdp', 'ctx'), 'tp')
- expand_bias_grad: float32 [8192], P('tp')
- contract_weight_grad: float32 [2048, 8192], P(('fsdp', 'ctx'), 'tp')
- output_bias_grad: float32 [2048], replicated
The draws below stay inside these ranges and needn't reach their ends.
Inputs may be any that keep to these rules, and one draw needn't show every extreme that they name: `segments`: each group's 4096 tokens form 4 runs of 1024; a run begins with 512 prompt tokens (id 0) and then holds 2 continuations, consecutive pairs of them 256 + o and 256 - o tokens long with 1 <= o <= 128; the first pair of each group's first run has o = 128; ids 1 to 8 each name one continuation of a group. The prompt tokens of a run hold positions k * 512 to k * 512 + 511 in order, each k once in a group; a continuation's tokens hold 2048, 2049 and so on in order.
All inputs are finite; a program needn't handle non-finite values.
Results may differ from the reference program's by a relative error of at most 0.012.
Values may be sent and summed in bfloat16 or wider, within the bound.
A program may use at most 256 MiB of HBM per device.

```python
import math
import jax
import jax.numpy as jnp
from jax import lax

D = 2048
H = 8
HD = 256
FF = 8192
ROT = 64
PROMPT = 2048
CL = 256
CONT_DEV = 2
PC = 512
GROUPS = 2
GROUP_TOK = 4096
CONTS = 8
TOKENS = 8192


def stretch_order(single_key):
    return jax.random.permutation(single_key, PROMPT // PC).astype(jnp.int32)


def label_order(single_key):
    return jax.random.permutation(single_key, CONTS).astype(jnp.int32)


def layout(key):
    holders = PROMPT // PC
    pairs = CONT_DEV // 2
    orders = jax.vmap(stretch_order)(jax.random.split(jax.random.fold_in(key, 11), GROUPS))
    labels = jax.vmap(label_order)(jax.random.split(jax.random.fold_in(key, 12), GROUPS)) + 1
    offsets = jax.random.randint(jax.random.fold_in(key, 13), (GROUPS, holders, pairs), 1, CL // 2 + 1).astype(jnp.int32)
    offsets = offsets.at[:, 0, 0].set(CL // 2)
    prompt_pos = orders[:, :, None] * PC + jnp.arange(PC, dtype=jnp.int32)[None, None, :]
    slot = jnp.arange(2 * CL, dtype=jnp.int32)[None, None, None, :]
    cut = CL + offsets[..., None]
    second = (slot >= cut).astype(jnp.int32)
    follow_pos = PROMPT + slot - second * cut
    follow_pos = follow_pos.reshape(GROUPS, holders, CONT_DEV * CL)
    pair_index = jnp.arange(pairs, dtype=jnp.int32)[None, None, :, None]
    which = (2 * pair_index + second).reshape(GROUPS, holders, CONT_DEV * CL)
    run_labels = labels.reshape(GROUPS, holders, CONT_DEV)
    follow_seg = jnp.take_along_axis(run_labels, which, 2)
    where_at = jnp.concatenate([prompt_pos, follow_pos], 2).reshape(-1)
    seg_ids = jnp.concatenate([jnp.zeros((GROUPS, holders, PC), jnp.int32), follow_seg], 2).reshape(-1)
    return (seg_ids.astype(jnp.int32), where_at.astype(jnp.int32))


def draw_segments(key, part):
    return layout(key)[0]


def draw_positions(key, part):
    return layout(key)[1]


def block_scale(rng, extent, cuts, smallest, top_value):
    def one(axis_at, shards_of):
        heights = jax.random.uniform(jax.random.fold_in(jax.random.fold_in(rng, 6), axis_at), (shards_of,), jnp.float32, smallest / len(cuts), top_value / len(cuts))
        return jnp.repeat(jnp.exp(heights), extent[axis_at] // shards_of).reshape((-1,) + (1,) * (len(extent) - axis_at - 1))

    loudness = one(*cuts[0])
    for cut in cuts[1:]:
        loudness = loudness * one(*cut)
    return loudness


def noise(key, dims, scale, bound, shards=(), kind=jnp.bfloat16):
    values = scale * jax.random.normal(key, dims, jnp.float32)
    if shards:
        values = values * block_scale(key, dims, shards, -0.22, 0.18)
    return jnp.clip(values, -bound, bound).astype(kind)


def setup_inputs(seed: int = 0) -> dict:
    seeds = jax.random.split(jax.random.key(seed), 16)
    stream_in = noise(seeds[0], (TOKENS, D), 1.0, 6.0, ((0, 32),))
    stream_grad = noise(seeds[1], (TOKENS, D), 1.0, 6.0, ((0, 32),))
    segments = draw_segments(jax.random.fold_in(seeds[15], 71), 0)
    positions = draw_positions(jax.random.fold_in(seeds[15], 71), 0)
    first_gain = jnp.clip(1.0 + 0.1 * jax.random.normal(seeds[4], (D,), jnp.float32), 0.5, 1.5)
    first_shift = noise(seeds[5], (D,), 0.3, 3.0, (), jnp.float32)
    second_gain = jnp.clip(1.0 + 0.1 * jax.random.normal(seeds[6], (D,), jnp.float32), 0.5, 1.5)
    second_shift = noise(seeds[7], (D,), 0.3, 3.0, (), jnp.float32)
    attend_weight = noise(seeds[8], (D, H, 3 * HD), D ** -0.5, 0.125, ((0, 8), (1, 4)))
    attend_bias = noise(seeds[9], (H, 3 * HD), 0.3, 3.0, ((0, 4),), jnp.float32)
    output_weight = noise(seeds[10], (D, D), (D // 64) ** -0.5, 1.0, ((0, 8), (1, 4)))
    expand_weight = noise(seeds[11], (D, FF), D ** -0.5, 0.125, ((0, 8), (1, 4)))
    expand_bias = noise(seeds[12], (FF,), 0.3, 3.0, ((0, 4),), jnp.float32)
    contract_weight = noise(seeds[13], (D, FF), FF ** -0.5, 0.0625, ((0, 8), (1, 4)))
    output_bias = noise(seeds[14], (D,), 0.3, 3.0, (), jnp.float32)
    return {"stream_in": stream_in, "stream_grad": stream_grad, "segments": segments, "positions": positions, "first_gain": first_gain, "first_shift": first_shift, "second_gain": second_gain, "second_shift": second_shift, "attend_weight": attend_weight, "attend_bias": attend_bias, "output_weight": output_weight, "expand_weight": expand_weight, "expand_bias": expand_bias, "contract_weight": contract_weight, "output_bias": output_bias}


EPS = 1e-05
HIGH = lax.Precision.HIGHEST

@jax.custom_vjp
def low(v):
    return lax.optimization_barrier(v.astype(jnp.bfloat16)).astype(jnp.float32)

@jax.custom_vjp
def low_back(v):
    return v

def low_keep(v):
    return (low(v), None)

def low_pass(kept, grad):
    return (grad,)

def back_keep(v):
    return (v, None)

def back_low(kept, grad):
    return (low(grad),)
low.defvjp(low_keep, low_pass)
low_back.defvjp(back_keep, back_low)

def layer_norm(values, gain_row, shift_row):
    center = values - lax.optimization_barrier(jnp.mean(values, -1, keepdims=True))
    spread = lax.optimization_barrier(jnp.mean(center * center, -1, keepdims=True))
    return center * lax.rsqrt(spread + EPS) * gain_row + shift_row

def rotate(values, where_at):
    half_rot = ROT // 2
    frequency = jnp.exp(jnp.arange(half_rot, dtype=jnp.float32) * (-2.0 * math.log(10000.0) / ROT))
    angles = where_at.astype(jnp.float32)[:, None] * frequency[None, :]
    cosine = jnp.concatenate([jnp.cos(angles), jnp.cos(angles)], -1)[:, None, :]
    sine_rows = jnp.concatenate([jnp.sin(angles), jnp.sin(angles)], -1)[:, None, :]
    rotated_part = values[..., :ROT]
    turned = jnp.concatenate([-rotated_part[..., half_rot:], rotated_part[..., :half_rot]], -1)
    return jnp.concatenate([rotated_part * cosine + turned * sine_rows, values[..., ROT:]], -1)

def forward(inputs, seg_rows, pos_rows, params):
    first_gain, first_shift, second_gain, second_shift, attend_weight, attend_bias, output_weight, expand_weight, expand_bias, contract_weight, output_bias = params
    row_count = inputs.shape[0]
    first_norm = low(layer_norm(inputs, first_gain, first_shift))
    second_norm = low(layer_norm(inputs, second_gain, second_shift))
    projected = jnp.dot(first_norm, attend_weight.reshape(D, -1), precision=HIGH)
    projected = low_back(projected.reshape(row_count, H, 3 * HD) + attend_bias)
    queries = low(rotate(projected[..., :HD], pos_rows))
    key_heads = low(rotate(projected[..., HD:2 * HD], pos_rows))
    value_heads = low(projected[..., 2 * HD:])
    block_rows = math.gcd(row_count, 512)
    score_scale = 1.0 / math.sqrt(HD)

    def attend_block(pieces):
        query_block, seg_block, pos_block = pieces
        scores = jnp.einsum('qhd,khd->hqk', query_block, key_heads, precision=HIGH) * score_scale
        scores = low_back(scores)
        allowed = ((seg_rows[None, :] == 0) | (seg_rows[None, :] == seg_block[:, None])) & (pos_rows[None, :] <= pos_block[:, None])
        scores = jnp.where(allowed[None], scores, -1e+30)
        row_top = lax.optimization_barrier(jnp.max(scores, -1, keepdims=True))
        exponent = jnp.exp(scores - row_top)
        probability = exponent / lax.optimization_barrier(jnp.sum(exponent, -1, keepdims=True))
        attended = jnp.einsum('hqk,khd->qhd', low(probability), value_heads, precision=HIGH)
        return low(low_back(attended))
    blocks = row_count // block_rows
    attended = lax.map(jax.checkpoint(attend_block), (queries.reshape(blocks, block_rows, H, HD), seg_rows.reshape(blocks, block_rows), pos_rows.reshape(blocks, block_rows)))
    attended = attended.reshape(row_count, D)
    pre_gelu = low_back(jnp.dot(second_norm, expand_weight, precision=HIGH) + expand_bias)
    activated = low(jax.nn.gelu(pre_gelu, approximate=False))
    mixed = jnp.dot(attended, output_weight.T, precision=HIGH) + jnp.dot(activated, contract_weight.T, precision=HIGH)
    return inputs + mixed + output_bias

def reference(stream_in, stream_grad, segments, positions, first_gain, first_shift, second_gain, second_shift, attend_weight, attend_bias, output_weight, expand_weight, expand_bias, contract_weight, output_bias):
    params = jax.tree.map(lambda member: member.astype(jnp.float32), (first_gain, first_shift, second_gain, second_shift, attend_weight, attend_bias, output_weight, expand_weight, expand_bias, contract_weight, output_bias))
    inputs = stream_in.astype(jnp.float32).reshape(GROUPS, GROUP_TOK, D)
    grads_in = stream_grad.astype(jnp.float32).reshape(GROUPS, GROUP_TOK, D)
    group_seg = segments.reshape(GROUPS, GROUP_TOK)
    group_pos = positions.reshape(GROUPS, GROUP_TOK)

    def scan_group(totals, pieces):
        group_rows, row_grads, seg_rows, pos_rows = pieces

        def run_layer(values, weights):
            return forward(values, seg_rows, pos_rows, weights)
        result, backward = jax.vjp(run_layer, group_rows, params)
        input_part, weight_parts = backward(row_grads)
        return (jax.tree.map(jnp.add, totals, weight_parts), (result, input_part))
    zero_grads = jax.tree.map(jnp.zeros_like, params)
    totals, (results, input_parts) = lax.scan(scan_group, zero_grads, (inputs, grads_in, group_seg, group_pos))
    return (results.reshape(TOKENS, D).astype(jnp.bfloat16), input_parts.reshape(TOKENS, D), totals[0], totals[1], totals[2], totals[3], totals[4], totals[5], totals[6], totals[7], totals[8], totals[9], totals[10])
```

```python
from functools import partial
import math

import jax
import jax.numpy as jnp
from jax import lax
from jax.sharding import PartitionSpec as P

ROT = 64
PROMPT = 2048
EPS = 1e-05
F32 = jnp.float32
BF16 = jnp.bfloat16


def dot(left, right):
    return jnp.dot(left, right, preferred_element_type=F32)


def row_product(left, right):
    return jnp.einsum("tf,df->td", left, right, preferred_element_type=F32)


def column_product(left, right):
    return jnp.einsum("tc,tk->ck", left, right, preferred_element_type=F32)


def rotate(values, where_at):
    half_rot = ROT // 2
    frequency = jnp.exp(jnp.arange(half_rot, dtype=F32) * (-2.0 * math.log(10000.0) / ROT))
    angles = where_at.astype(F32)[:, None] * frequency[None, :]
    cosine = jnp.concatenate([jnp.cos(angles), jnp.cos(angles)], -1)[:, None, :]
    sine_rows = jnp.concatenate([jnp.sin(angles), jnp.sin(angles)], -1)[:, None, :]
    rotated_part = values[..., :ROT]
    turned = jnp.concatenate([-rotated_part[..., half_rot:], rotated_part[..., :half_rot]], -1)
    return jnp.concatenate([rotated_part * cosine + turned * sine_rows, values[..., ROT:]], -1)


class SquareLinks:
    blocks = 8
    order = ((0, 0, 0), (1, 0, 0), (0, 1, 0), (1, 1, 0), (0, 0, 1), (1, 0, 1), (0, 1, 1), (1, 1, 1))

    def __init__(self):
        self.f = lax.axis_index("fsdp")
        c = lax.axis_index("ctx")
        self.y, self.c = c // 2, c % 2

    def x_hop(self, v):
        return lax.ppermute(v, "fsdp", [(0, 1), (1, 0)])

    def y_hop(self, v):
        return lax.ppermute(v, "ctx", [(0, 2), (2, 0), (1, 3), (3, 1)])

    def core_hop(self, v):
        return lax.ppermute(v, "ctx", [(0, 1), (1, 0), (2, 3), (3, 2)])

    def place(self, bits):
        a, b, d = bits
        return ((self.f ^ a) * 2 + (self.y ^ b)) * 2 + (self.c ^ d)

    def to_relative(self, v, axis):
        size = v.shape[axis] // self.blocks
        return jnp.concatenate(
            [lax.dynamic_slice_in_dim(v, self.place(bits) * size, size, axis) for bits in self.order], axis
        )

    def to_whole(self, v, axis):
        size = v.shape[axis] // self.blocks
        where = {bits: i for i, bits in enumerate(self.order)}
        table = jnp.array([where[(p // 4, p // 2 % 2, p % 2)] for p in range(8)], jnp.int32)
        return jnp.concatenate(
            [
                lax.dynamic_slice_in_dim(v, table[self.place((p // 4, p // 2 % 2, p % 2))] * size, size, axis)
                for p in range(8)
            ],
            axis,
        )

    def gather(self, block):
        rows = block.shape[0]
        half = rows // 2
        from_x, from_y = self.x_hop(block), self.y_hop(block)
        corner = (self.x_hop(from_y[:half]), self.y_hop(from_x[half:]))
        near = jnp.concatenate([block, from_x, from_y, *corner], 0)
        return jnp.concatenate([near, self.core_hop(near)], 0)

    def scatter(self, near, far):
        near = near.astype(F32) + self.core_hop(far.astype(BF16)).astype(F32)
        rows = near.shape[0] // 4
        half = rows // 2
        own, to_x, to_y, corner = (near[i * rows : (i + 1) * rows] for i in range(4))
        corner = corner.astype(BF16)
        via_x, via_y = self.x_hop(corner[:half]), self.y_hop(corner[half:])
        to_y = jnp.concatenate([to_y[:half] + via_x.astype(F32), to_y[half:]], 0).astype(BF16)
        to_x = jnp.concatenate([to_x[:half], to_x[half:] + via_y.astype(F32)], 0).astype(BF16)
        return own + self.x_hop(to_x).astype(F32) + self.y_hop(to_y).astype(F32)

    def ctx_order(self, v):
        size = v.shape[0] // 4
        return jnp.concatenate(
            [
                lax.dynamic_slice_in_dim(v, ((self.y ^ b) * 2 + (self.c ^ d)) * size, size, 0)
                for b, d in ((0, 0), (1, 0), (0, 1), (1, 1))
            ],
            0,
        )

    def gather_ctx(self, block):
        near = jnp.concatenate([block, self.y_hop(block)], 0)
        return jnp.concatenate([near, self.core_hop(near)], 0)

    def scatter_ctx(self, parts):
        half = parts.shape[0] // 2
        near = parts[:half] + self.core_hop(parts[half:].astype(BF16)).astype(F32)
        rows = half // 2
        return near[:rows] + self.y_hop(near[rows:].astype(BF16)).astype(F32)

    def sum_rows(self, v):
        v = v + self.core_hop(v)
        v = v + self.x_hop(v)
        return v + self.y_hop(v)


class AnyLinks:
    def to_relative(self, v, axis):
        return v

    def to_whole(self, v, axis):
        return v

    def gather(self, block):
        return lax.all_gather(block, ("fsdp", "ctx"), axis=0, tiled=True)

    def scatter(self, near, far):
        whole = jnp.concatenate([near, far], 0).astype(BF16)
        return lax.psum_scatter(whole, ("fsdp", "ctx"), scatter_dimension=0, tiled=True).astype(F32)

    def ctx_order(self, v):
        return v

    def gather_ctx(self, block):
        return lax.all_gather(block, "ctx", axis=0, tiled=True)

    def scatter_ctx(self, parts):
        return lax.psum_scatter(parts, "ctx", scatter_dimension=0, tiled=True)

    def sum_rows(self, v):
        return lax.psum(v, ("fsdp", "ctx"))


def sum_tp(v):
    size = lax.axis_size("tp")
    if size & (size - 1):
        return lax.psum(v, "tp")
    step = 1
    while step < size:
        v = v + lax.ppermute(v, "tp", [(i, i ^ step) for i in range(size)])
        step *= 2
    return v


def attention_probs(query_heads, key_heads, allowed):
    score_scale = 1.0 / math.sqrt(query_heads.shape[-1])
    scores = jnp.einsum("qhd,khd->hqk", query_heads, key_heads, preferred_element_type=F32) * score_scale
    scores = jnp.where(allowed[None], scores, -1e30)
    row_top = jnp.max(scores, -1, keepdims=True)
    exponent = jnp.exp(scores - row_top)
    return exponent / jnp.sum(exponent, -1, keepdims=True)


def shards(
    stream_in,
    stream_grad,
    segments,
    positions,
    first_gain,
    first_shift,
    second_gain,
    second_shift,
    attend_weight,
    attend_bias,
    output_weight,
    expand_weight,
    expand_bias,
    contract_weight,
    output_bias,
):
    square = lax.axis_size("fsdp") == 2 and lax.axis_size("ctx") == 4
    links = SquareLinks() if square else AnyLinks()
    local_rows = attend_weight.shape[0]
    heads_here = attend_bias.shape[0]
    head_size = attend_bias.shape[1] // 3
    hidden_here = expand_bias.shape[0]
    score_scale = 1.0 / math.sqrt(head_size)
    holders = lax.axis_size("ctx")
    holder = lax.axis_index("ctx")
    prompt_here = PROMPT // holders

    in_part = links.to_relative(stream_in, 1)
    grad_part = links.to_relative(stream_grad, 1)
    gains = links.to_relative(jnp.stack([first_gain, first_shift, second_gain, second_shift]), 1)
    full_rows = lax.all_gather(in_part, "tp", axis=0, tiled=True)
    grad_part_late, full_rows = lax.optimization_barrier((grad_part, full_rows))
    grad_rows = lax.all_gather(grad_part_late, "tp", axis=0, tiled=True)
    row_count = full_rows.shape[0]

    attend_all = links.gather(attend_weight.reshape(local_rows, -1))
    expand_all = links.gather(expand_weight)
    contract_all = links.gather(contract_weight)
    output_all = links.gather(output_weight)
    width = attend_all.shape[0]

    row_pos = lax.dynamic_slice_in_dim(positions, holder * row_count, row_count)
    row_seg = lax.dynamic_slice_in_dim(segments, holder * row_count, row_count)
    prompt_pos = links.ctx_order(positions.reshape(holders, row_count)[:, :prompt_here].reshape(-1))
    key_pos = jnp.concatenate([prompt_pos, row_pos[prompt_here:]])
    key_seg = jnp.concatenate([jnp.zeros_like(prompt_pos), row_seg[prompt_here:]])
    allowed = ((key_seg[None, :] == 0) | (key_seg[None, :] == row_seg[:, None])) & (
        key_pos[None, :] <= row_pos[:, None]
    )

    inputs = full_rows.astype(F32)
    center = inputs - jnp.mean(inputs, -1, keepdims=True)
    scale = lax.rsqrt(jnp.mean(center * center, -1, keepdims=True) + EPS)
    unit = center * scale
    first_norm = (unit * gains[0] + gains[1]).astype(BF16)
    second_norm = (unit * gains[2] + gains[3]).astype(BF16)

    projected = dot(first_norm, attend_all).reshape(row_count, heads_here, 3 * head_size) + attend_bias
    query_heads = rotate(projected[..., :head_size], row_pos).astype(BF16)
    key_heads = rotate(projected[..., head_size : 2 * head_size], row_pos).astype(BF16)
    value_heads = projected[..., 2 * head_size :].astype(BF16)
    prompt_pairs = jnp.concatenate([key_heads[:prompt_here], value_heads[:prompt_here]], -1)
    gathered = links.gather_ctx(prompt_pairs)
    all_keys = jnp.concatenate([gathered[..., :head_size], key_heads[prompt_here:]], 0)
    all_values = jnp.concatenate([gathered[..., head_size:], value_heads[prompt_here:]], 0)

    pre_gelu = dot(second_norm, expand_all) + expand_bias
    activated = jax.nn.gelu(pre_gelu, approximate=False).astype(BF16)

    probability = attention_probs(query_heads, all_keys, allowed)
    prob_low = probability.astype(BF16)
    attended = jnp.einsum("hqk,khd->qhd", prob_low, all_values, preferred_element_type=F32)
    attended = attended.astype(BF16).reshape(row_count, heads_here * head_size)
    mixed = (row_product(attended, output_all) + row_product(activated, contract_all)).astype(BF16)
    branch_total = lax.psum_scatter(mixed, "tp", scatter_dimension=0, tiled=True)
    local_inputs = in_part.astype(F32)
    stream_out = links.to_whole(branch_total.astype(F32) + local_inputs, 1) + output_bias
    stream_out = stream_out.astype(BF16)

    grad_attended = dot(grad_rows, output_all).astype(BF16).reshape(row_count, heads_here, head_size)
    grad_activated = dot(grad_rows, contract_all)
    gelu_back = jax.vjp(partial(jax.nn.gelu, approximate=False), pre_gelu)[1]
    grad_pre = gelu_back(grad_activated)[0].astype(BF16)

    grad_prob = jnp.einsum("qhd,khd->hqk", grad_attended, all_values, preferred_element_type=F32)
    inner = jnp.sum(probability * grad_prob, -1, keepdims=True)
    grad_scores = (probability * (grad_prob - inner)).astype(BF16)
    grad_queries = (
        jnp.einsum("hqk,khd->qhd", grad_scores, all_keys, preferred_element_type=F32) * score_scale
    )
    grad_keys = (
        jnp.einsum("hqk,qhd->khd", grad_scores, query_heads, preferred_element_type=F32) * score_scale
    )
    grad_values = jnp.einsum("hqk,qhd->khd", prob_low, grad_attended, preferred_element_type=F32)
    pair_grads = jnp.concatenate([grad_keys, grad_values], -1)
    prompt_grad = links.scatter_ctx(pair_grads[:PROMPT])
    pair_rows = jnp.concatenate([prompt_grad, pair_grads[PROMPT:]], 0)

    def rotate_rows(values):
        return rotate(values, row_pos)

    rotate_back = jax.vjp(rotate_rows, jnp.zeros((row_count, heads_here, head_size), F32))[1]
    grad_projected = jnp.concatenate(
        [rotate_back(grad_queries)[0], rotate_back(pair_rows[..., :head_size])[0], pair_rows[..., head_size:]],
        -1,
    ).astype(BF16)
    grad_flat = grad_projected.reshape(row_count, heads_here * 3 * head_size)

    bias_parts = jnp.concatenate([jnp.sum(grad_flat, 0, dtype=F32), jnp.sum(grad_pre, 0, dtype=F32)])
    bias_sums = links.sum_rows(bias_parts)
    attend_bias_grad = bias_sums[: grad_flat.shape[1]].reshape(attend_bias.shape)
    expand_bias_grad = bias_sums[grad_flat.shape[1] :]

    grad_first = row_product(grad_flat, attend_all)
    grad_second = row_product(grad_pre, expand_all)
    grad_unit = (grad_first * gains[0] + grad_second * gains[2]).astype(BF16)
    local_unit_grad = lax.psum_scatter(grad_unit, "tp", scatter_dimension=0, tiled=True).astype(F32)
    vector_parts = jnp.stack(
        [
            jnp.sum(grad_first * unit, 0),
            jnp.sum(grad_first, 0),
            jnp.sum(grad_second * unit, 0),
            jnp.sum(grad_second, 0),
            jnp.sum(grad_part.astype(F32), 0),
        ]
    )
    norm_sums = sum_tp(links.sum_rows(links.to_whole(vector_parts, 1)))

    local_center = local_inputs - jnp.mean(local_inputs, -1, keepdims=True)
    local_scale = lax.rsqrt(jnp.mean(local_center * local_center, -1, keepdims=True) + EPS)
    local_unit = local_center * local_scale
    input_grad = links.to_whole(
        grad_part.astype(F32)
        + local_scale
        * (
            local_unit_grad
            - jnp.mean(local_unit_grad, -1, keepdims=True)
            - local_unit * jnp.mean(local_unit_grad * local_unit, -1, keepdims=True)
        ),
        1,
    )

    half = width // 2

    def weight_grad(left, right):
        far = column_product(left[:, half:], right).astype(BF16)
        near = column_product(left[:, :half], right)
        return links.scatter(near, far)

    contract_weight_grad = weight_grad(grad_rows, activated)
    expand_weight_grad = weight_grad(second_norm, grad_pre)
    output_weight_grad = weight_grad(grad_rows, attended)
    attend_weight_grad = weight_grad(first_norm, grad_flat).reshape(attend_weight.shape)
    return (
        stream_out,
        input_grad,
        norm_sums[0],
        norm_sums[1],
        norm_sums[2],
        norm_sums[3],
        attend_weight_grad,
        attend_bias_grad,
        output_weight_grad,
        expand_weight_grad,
        expand_bias_grad,
        contract_weight_grad,
        norm_sums[4],
    )


def solution(mesh):
    tokens = P(("fsdp", "ctx", "tp"), None)
    weight = P(("fsdp", "ctx"), "tp")
    heads = P(("fsdp", "ctx"), "tp", None)
    return jax.shard_map(
        shards,
        mesh=mesh,
        in_specs=(
            tokens,
            tokens,
            P("fsdp"),
            P("fsdp"),
            P(),
            P(),
            P(),
            P(),
            heads,
            P("tp", None),
            weight,
            weight,
            P("tp"),
            weight,
            P(),
        ),
        out_specs=(
            tokens,
            tokens,
            P(),
            P(),
            P(),
            P(),
            heads,
            P("tp", None),
            weight,
            weight,
            P("tp"),
            weight,
            P(),
        ),
        check_vma=False,
    )
```

```python
from functools import partial, reduce
import math

import jax
import jax.numpy as jnp
from jax import lax
from jax.experimental import pallas as pl
from jax.experimental.pallas import tpu as pltpu
from jax.sharding import PartitionSpec as P

ROT = 64
PROMPT = 2048
EPS = 1e-05
F32 = jnp.float32
BF16 = jnp.bfloat16
ROWS = 256
HEAD = 256
NN = (((1,), (0,)), ((), ()))
NT = (((1,), (1,)), ((), ()))
TN = (((0,), (0,)), ((), ()))


def mul(a, b, dims):
    return lax.dot_general(a, b, dims, preferred_element_type=F32)


def call(kernel, grid, in_specs, out_specs, out_shape, flops, moved, exps=0, scratch=(), mib=48, name=None):
    return pl.pallas_call(
        kernel,
        grid=grid,
        in_specs=in_specs,
        out_specs=out_specs,
        out_shape=out_shape,
        scratch_shapes=scratch,
        compiler_params=pltpu.CompilerParams(vmem_limit_bytes=mib * 2**20),
        cost_estimate=pl.CostEstimate(flops=flops, bytes_accessed=moved, transcendentals=exps),
        name=name,
    )


def shape(*dims, kind=BF16):
    return jax.ShapeDtypeStruct(dims, kind)


def wide(row):
    return jnp.broadcast_to(row[None], (8, row.shape[0]))


def after(value, *others):
    return lax.optimization_barrier((value, *others))[0]


def turn(v, table, sign):
    head = v[:, :128]
    other = pltpu.roll(head, 96, 1) * table[:, 128:256] + pltpu.roll(head, 32, 1) * table[:, 256:]
    return jnp.concatenate([head * table[:, :128] + sign * other, v[:, 128:]], 1)


def turn_table(where_at):
    half = ROT // 2
    frequency = jnp.exp(jnp.arange(half, dtype=F32) * (-2.0 * math.log(10000.0) / ROT))
    angles = where_at.astype(F32)[:, None] * frequency[None, :]
    c, s = jnp.cos(angles), jnp.sin(angles)
    rows = where_at.shape[0]
    one, none = jnp.ones((rows, 128 - ROT), F32), jnp.zeros((rows, 128 - half), F32)
    return jnp.concatenate([c, c, one, -s, none, none[:, :half], s, none[:, : 128 - ROT]], 1)


def reorder_kernel(places, x_ref, o_ref):
    size = x_ref.shape[1] // len(places)
    for i, place in enumerate(places):
        o_ref[:, i * size : (i + 1) * size] = x_ref[:, pl.ds(pl.multiple_of(place() * size, size), size)]


def reorder(x, places):
    rows, cols = x.shape
    block = pl.BlockSpec((rows, cols), lambda: (0, 0))
    return call(partial(reorder_kernel, places), (), [block], block, shape(rows, cols, kind=x.dtype), 0, 4 * rows * cols, name="reorder")(x)


def norm_kernel(x_ref, gain_ref, first_ref, second_ref, stat_ref):
    x = x_ref[...].astype(F32)
    mean = jnp.mean(x, -1, keepdims=True)
    center = x - mean
    scale = lax.rsqrt(jnp.mean(center * center, -1, keepdims=True) + EPS)
    unit = center * scale
    first_ref[...] = (unit * gain_ref[0:1] + gain_ref[1:2]).astype(BF16)
    second_ref[...] = (unit * gain_ref[2:3] + gain_ref[3:4]).astype(BF16)
    lane = lax.broadcasted_iota(jnp.int32, stat_ref.shape, 1)
    stat_ref[...] = jnp.where(lane == 0, mean, scale)


def norms(x, gains):
    rows, width = x.shape
    block = pl.BlockSpec((128, width), lambda i: (i, 0))
    return call(
        norm_kernel,
        (rows // 128,),
        [block, pl.BlockSpec((8, width), lambda i: (0, 0))],
        [block, block, pl.BlockSpec((128, 128), lambda i: (i, 0))],
        [shape(rows, width), shape(rows, width), shape(rows, 128, kind=F32)],
        10 * rows * width,
        6 * rows * width,
        name="norms",
    )(x, gains)


def project_kernel(n_ref, w_ref, b_ref, table_ref, q_ref, kv_ref):
    head = q_ref.shape[1]
    for i in range(n_ref.shape[0] // ROWS):
        at = pl.ds(i * ROWS, ROWS)
        out = mul(n_ref[at, :], w_ref[...], NN) + b_ref[:1]
        q_ref[at, :] = turn(out[:, :head], table_ref[at, :], 1.0).astype(BF16)
        kv_ref[at, :head] = turn(out[:, head : 2 * head], table_ref[at, :], 1.0).astype(BF16)
        kv_ref[at, head:] = out[:, 2 * head :].astype(BF16)


def project(n, w, bias, table, heads):
    rows, depth = n.shape
    width = w.shape[1] // heads
    head = width // 3
    return call(
        project_kernel,
        (heads,),
        [
            pl.BlockSpec((rows, depth), lambda h: (0, 0)),
            pl.BlockSpec((depth, width), lambda h: (0, h)),
            pl.BlockSpec((8, width), lambda h: (0, h)),
            pl.BlockSpec((rows, 384), lambda h: (0, 0)),
        ],
        [pl.BlockSpec((rows, head), lambda h: (0, h)), pl.BlockSpec((rows, 2 * head), lambda h: (0, h))],
        [shape(rows, heads * head), shape(rows, heads * 2 * head)],
        2 * rows * depth * w.shape[1],
        2 * (rows * depth + w.size + rows * w.shape[1]),
        name="project",
    )(n, w, wide(bias), table)


def expand_kernel(n_ref, w_ref, b_ref, h_ref, d_ref):
    for i in range(n_ref.shape[0] // ROWS):
        at = pl.ds(i * ROWS, ROWS)
        pre = mul(n_ref[at, :], w_ref[...], NN) + b_ref[:1]
        below = 0.5 + 0.5 * lax.erf(pre * math.sqrt(0.5))
        h_ref[at, :] = (pre * below).astype(BF16)
        d_ref[at, :] = (below + pre * jnp.exp(-0.5 * pre * pre) * (1.0 / math.sqrt(2 * math.pi))).astype(BF16)


def expand(n, w, bias, tile=512):
    rows, depth = n.shape
    cols = w.shape[1]
    out = pl.BlockSpec((rows, tile), lambda j: (0, j))
    return call(
        expand_kernel,
        (cols // tile,),
        [
            pl.BlockSpec((rows, depth), lambda j: (0, 0)),
            pl.BlockSpec((depth, tile), lambda j: (0, j)),
            pl.BlockSpec((8, tile), lambda j: (0, j)),
        ],
        [out, out],
        [shape(rows, cols), shape(rows, cols)],
        2 * rows * depth * cols,
        2 * (rows * depth + w.size + 2 * rows * cols),
        2 * rows * cols,
        name="expand",
    )(n, w, wide(bias))


def attend_kernel(prompt, q_ref, ko, vo, kt, vt, bias_ref, segc_ref, segr_ref, o_ref, stat_ref):
    block = pl.program_id(1)
    tq = q_ref.shape[0]
    first_cont = prompt // tq
    cont = ko.shape[0] - prompt
    q = q_ref[...] * BF16(1.0 / math.sqrt(q_ref.shape[1]))
    rows = lax.broadcasted_iota(jnp.int32, (tq, 1), 0)

    def finish(scores, values):
        top = reduce(jnp.maximum, [jnp.max(s, -1, keepdims=True) for s in scores])
        exps = [jnp.exp(s - top) for s in scores]
        total = sum(jnp.sum(e, -1, keepdims=True) for e in exps)
        out = sum(mul(e.astype(BF16), v, NN) for e, v in zip(exps, values))
        o_ref[...] = (out / total).astype(BF16)
        stat_ref[0] = jnp.transpose(jnp.broadcast_to(top + jnp.log(total), (tq, 128)))[:8]

    @pl.when(block < first_cont)
    def _():
        cols = lax.broadcasted_iota(jnp.int32, (1, prompt), 1)
        own = jnp.where(cols <= rows + block * tq, mul(q, ko[:prompt], NT), -1e30)
        far = mul(q, kt[...], NT) + bias_ref[:1]
        finish([own, far], [vo[:prompt], vt[...]])

    @pl.when(block >= first_cont)
    def _():
        cols = lax.broadcasted_iota(jnp.int32, (1, cont), 1)
        own = mul(q, ko[:prompt], NT)
        read = (cols <= rows + (block - first_cont) * tq) & (segc_ref[:, :1] == segr_ref[:1])
        follow = jnp.where(read, mul(q, ko[prompt:], NT), -1e30)
        far = mul(q, kt[...], NT)
        finish([own, follow, far], [vo[:prompt], vo[prompt:], vt[...]])


def attend(q, kv, kv_far, bias, seg, prompt):
    rows, width = q.shape
    head = HEAD
    heads = width // head
    far = kv_far.shape[0]
    cont = rows - prompt
    tq = ROWS
    first = prompt // tq
    return call(
        partial(attend_kernel, prompt),
        (heads, rows // tq),
        [
            pl.BlockSpec((tq, head), lambda h, b: (b, h)),
            pl.BlockSpec((rows, head), lambda h, b: (0, 2 * h)),
            pl.BlockSpec((rows, head), lambda h, b: (0, 2 * h + 1)),
            pl.BlockSpec((far, head), lambda h, b: (0, 2 * h)),
            pl.BlockSpec((far, head), lambda h, b: (0, 2 * h + 1)),
            pl.BlockSpec((8, far), lambda h, b: (0, 0)),
            pl.BlockSpec((tq, 128), lambda h, b: (jnp.maximum(b - first, 0), 0)),
            pl.BlockSpec((8, cont), lambda h, b: (0, 0)),
        ],
        [pl.BlockSpec((tq, head), lambda h, b: (b, h)), pl.BlockSpec((1, 8, tq), lambda h, b: (h, 0, b))],
        [shape(rows, width), shape(heads, 8, rows, kind=F32)],
        4 * rows * (rows + far) * width,
        2 * (2 * q.size + kv.size + kv_far.size),
        rows * (rows + far) * heads,
        name="attend",
    )(q, kv, kv, kv_far, kv_far, wide(bias), jnp.broadcast_to(seg[prompt:, None], (cont, 128)), wide(seg[prompt:]))


def attend_back_kernel(
    prompt, q_ref, do_ref, o_ref, stat_ref, ko, vo, kt, vt, bias_ref, segc_ref, segr_ref, table_ref,
    dq_ref, own_ref, near_ref, far_ref, acc_k, acc_v,
):
    block = pl.program_id(1)
    tq, head = q_ref.shape
    first_cont = prompt // tq
    scale = 1.0 / math.sqrt(head)
    q = q_ref[...] * BF16(scale)
    do = do_ref[...]
    inner = jnp.sum(do.astype(F32) * o_ref[...].astype(F32), -1, keepdims=True)
    inner = jnp.transpose(jnp.broadcast_to(inner, (tq, 128)))[:1]
    stat = stat_ref[0, :1]
    cols = lax.broadcasted_iota(jnp.int32, (1, tq), 1)

    @pl.when(block == 0)
    def _():
        acc_k[...] = jnp.zeros_like(acc_k)
        acc_v[...] = jnp.zeros_like(acc_v)

    def part(keys, values, at, seen):
        probs = jnp.exp(seen(mul(keys, q, NT)) - stat)
        grads = (probs * (mul(values, do, NT) - inner)).astype(BF16)
        acc_v[at, :] += mul(probs.astype(BF16), do, NN)
        acc_k[at, :] += mul(grads, q, NN)
        return mul(grads, keys, TN)

    def far_parts(total, seen):
        for i in range(kt.shape[0] // prompt):
            at = pl.ds(i * prompt, prompt)
            total += part(kt[at, :], vt[at, :], pl.ds(ko.shape[0] + i * prompt, prompt), partial(seen, at))
        dq_ref[...] = turn(total * scale, table_ref[...], -1.0).astype(BF16)

    @pl.when(block < first_cont)
    def _():
        rows = lax.broadcasted_iota(jnp.int32, (prompt, 1), 0)
        total = part(
            ko[:prompt], vo[:prompt], pl.ds(0, prompt), lambda s: jnp.where(rows <= cols + block * tq, s, -1e30)
        )
        far_parts(total, lambda at, s: s + bias_ref[at, :1])

    @pl.when(block >= first_cont)
    def _():
        cont = ko.shape[0] - prompt
        rows = lax.broadcasted_iota(jnp.int32, (cont, 1), 0)
        total = part(ko[:prompt], vo[:prompt], pl.ds(0, prompt), lambda s: s)
        read = (rows <= cols + (block - first_cont) * tq) & (segc_ref[:, :1] == segr_ref[:1])
        total += part(ko[prompt:], vo[prompt:], pl.ds(prompt, cont), lambda s: jnp.where(read, s, -1e30))
        far_parts(total, lambda at, s: s)

    @pl.when(block == pl.num_programs(1) - 1)
    def _():
        start = 0
        for ref in (own_ref, near_ref, far_ref):
            at = pl.ds(start, ref.shape[0])
            ref[:, :head] = acc_k[at, :].astype(ref.dtype)
            ref[:, head:] = acc_v[at, :].astype(ref.dtype)
            start += ref.shape[0]


def attend_back(q, do, o, stat, kv, kv_far, bias, seg, prompt, table):
    rows, width = q.shape
    head = HEAD
    heads = width // head
    far = kv_far.shape[0]
    cont = rows - prompt
    tq = ROWS
    first = prompt // tq
    row = pl.BlockSpec((tq, head), lambda h, b: (b, h))

    def column(n, odd):
        return pl.BlockSpec((n, head), lambda h, b: (0, 2 * h + odd))

    def pair(n):
        return pl.BlockSpec((n, 2 * head), lambda h, b: (0, h))

    return call(
        partial(attend_back_kernel, prompt),
        (heads, rows // tq),
        [
            row,
            row,
            row,
            pl.BlockSpec((1, 8, tq), lambda h, b: (h, 0, b)),
            column(rows, 0),
            column(rows, 1),
            column(far, 0),
            column(far, 1),
            pl.BlockSpec((far, 128), lambda h, b: (0, 0)),
            pl.BlockSpec((cont, 128), lambda h, b: (0, 0)),
            pl.BlockSpec((8, tq), lambda h, b: (0, jnp.maximum(b - first, 0))),
            pl.BlockSpec((tq, 384), lambda h, b: (b, 0)),
        ],
        [row, pair(rows), pair(prompt), pair(far - prompt)],
        [
            shape(rows, width),
            shape(rows, 2 * width, kind=F32),
            shape(prompt, 2 * width),
            shape(far - prompt, 2 * width),
        ],
        10 * rows * (rows + far) * width,
        2 * (4 * q.size + 4 * kv.size + 2 * kv_far.size),
        rows * (rows + far) * heads,
        [pltpu.VMEM((rows + far, head), F32), pltpu.VMEM((rows + far, head), F32)],
        name="attend_back",
    )(
        q,
        do,
        o,
        stat,
        kv,
        kv,
        kv_far,
        kv_far,
        jnp.broadcast_to(bias[:, None], (far, 128)),
        jnp.broadcast_to(seg[prompt:, None], (cont, 128)),
        wide(seg[prompt:]),
        table,
    )


def mixed_kernel(a_ref, h_ref, wa_ref, wh_ref, o_ref):
    for i in range(a_ref.shape[0] // ROWS):
        at = pl.ds(i * ROWS, ROWS)
        o_ref[at, :] = (mul(a_ref[at, :], wa_ref[...], NT) + mul(h_ref[at, :], wh_ref[...], NT)).astype(BF16)


def mixed_sum(attended, activated, w_out, w_contract, tile=512):
    rows = attended.shape[0]
    deep, deeper = attended.shape[1], activated.shape[1]
    width = w_out.shape[0]
    return call(
        mixed_kernel,
        (width // tile,),
        [
            pl.BlockSpec((rows, deep), lambda j: (0, 0)),
            pl.BlockSpec((rows, deeper), lambda j: (0, 0)),
            pl.BlockSpec((tile, deep), lambda j: (j, 0)),
            pl.BlockSpec((tile, deeper), lambda j: (j, 0)),
        ],
        pl.BlockSpec((rows, tile), lambda j: (0, j)),
        shape(rows, width),
        2 * rows * width * (deep + deeper),
        2 * (rows + width) * (deep + deeper) + 2 * rows * width,
        name="mixed_sum",
    )(attended, activated, w_out, w_contract)


def grads_kernel(g_ref, wo_ref, wc_ref, d_ref, do_ref, gp_ref, sum_ref):
    @pl.when(pl.program_id(0) == 0)
    def _():
        for i in range(g_ref.shape[0] // ROWS):
            at = pl.ds(i * ROWS, ROWS)
            do_ref[at, :] = mul(g_ref[at, :], wo_ref[...], NN).astype(BF16)

    total = 0.0
    for i in range(g_ref.shape[0] // ROWS):
        at = pl.ds(i * ROWS, ROWS)
        grad = (mul(g_ref[at, :], wc_ref[...], NN) * d_ref[at, :].astype(F32)).astype(BF16)
        gp_ref[at, :] = grad
        total += jnp.sum(grad.astype(F32), 0, keepdims=True)
    sum_ref[...] = jnp.broadcast_to(total, sum_ref.shape)


def branch_grads(g, w_out, w_contract, slope, tile=512):
    rows, depth = g.shape
    deep, cols = w_out.shape[1], w_contract.shape[1]
    tall = pl.BlockSpec((rows, tile), lambda j: (0, j))
    return call(
        grads_kernel,
        (cols // tile,),
        [
            pl.BlockSpec((rows, depth), lambda j: (0, 0)),
            pl.BlockSpec((depth, deep), lambda j: (0, 0)),
            pl.BlockSpec((depth, tile), lambda j: (0, j)),
            tall,
        ],
        [pl.BlockSpec((rows, deep), lambda j: (0, 0)), tall, pl.BlockSpec((8, tile), lambda j: (0, j))],
        [shape(rows, deep), shape(rows, cols), shape(8, cols, kind=F32)],
        2 * rows * depth * (deep + cols),
        2 * (rows * depth + depth * (deep + cols) + 2 * rows * cols),
        name="branch_grads",
    )(g, w_out, w_contract, slope)


def pack_kernel(prompt_blocks, q_ref, own_ref, near_ref, far_ref, table_ref, o_ref, sum_ref):
    block = pl.program_id(1)
    head = q_ref.shape[1]
    theirs = near_ref[...].astype(F32) + far_ref[...].astype(F32)
    both = own_ref[...] + jnp.where(block < prompt_blocks, theirs, 0.0)
    out = [q_ref[...], turn(both[:, :head], table_ref[...], -1.0).astype(BF16), both[:, head:].astype(BF16)]

    @pl.when(block == 0)
    def _():
        sum_ref[...] = jnp.zeros_like(sum_ref)

    for i, part in enumerate(out):
        o_ref[:, i * head : (i + 1) * head] = part
        sum_ref[:, i * head : (i + 1) * head] += jnp.sum(part.astype(F32), 0, keepdims=True)


def pack(dq, own, near, far, table, prompt):
    rows, width = dq.shape
    head = HEAD
    heads = width // head
    tq = ROWS
    blocks = prompt // tq
    theirs = pl.BlockSpec((tq, 2 * head), lambda h, b: (jnp.minimum(b, blocks - 1), h))
    return call(
        partial(pack_kernel, blocks),
        (heads, rows // tq),
        [
            pl.BlockSpec((tq, head), lambda h, b: (b, h)),
            pl.BlockSpec((tq, 2 * head), lambda h, b: (b, h)),
            theirs,
            theirs,
            pl.BlockSpec((tq, 384), lambda h, b: (b, 0)),
        ],
        [pl.BlockSpec((tq, 3 * head), lambda h, b: (b, h)), pl.BlockSpec((8, 3 * head), lambda h, b: (0, h))],
        [shape(rows, 3 * width), shape(8, 3 * width, kind=F32)],
        10 * rows * width,
        16 * rows * width,
        name="pack",
    )(dq, own, near, far, table)


def unit_grad_kernel(gp_ref, gh_ref, wa_ref, we_ref, x_ref, stat_ref, gain_ref, e_ref, sum_ref):
    sums = [0.0] * 4
    for i in range(gp_ref.shape[0] // ROWS):
        at = pl.ds(i * ROWS, ROWS)
        first = mul(gp_ref[at, :], wa_ref[...], NT)
        second = mul(gh_ref[at, :], we_ref[...], NT)
        e_ref[at, :] = (first * gain_ref[0:1] + second * gain_ref[2:3]).astype(BF16)
        unit = (x_ref[at, :].astype(F32) - stat_ref[at, 0:1]) * stat_ref[at, 1:2]
        for j, v in enumerate((first * unit, first, second * unit, second)):
            sums[j] += jnp.sum(v, 0, keepdims=True)
    for j in range(4):
        sum_ref[j : j + 1] = sums[j]
    sum_ref[4:] = jnp.zeros_like(sum_ref[4:])


def unit_grads(gp, gh, w_attend, w_expand, x, stat, gains, tile=512):
    rows, width = x.shape
    deep, deeper = gp.shape[1], gh.shape[1]
    col = pl.BlockSpec((rows, tile), lambda j: (0, j))
    row = pl.BlockSpec((8, tile), lambda j: (0, j))
    return call(
        unit_grad_kernel,
        (width // tile,),
        [
            pl.BlockSpec((rows, deep), lambda j: (0, 0)),
            pl.BlockSpec((rows, deeper), lambda j: (0, 0)),
            pl.BlockSpec((tile, deep), lambda j: (j, 0)),
            pl.BlockSpec((tile, deeper), lambda j: (j, 0)),
            col,
            pl.BlockSpec((rows, 128), lambda j: (0, 0)),
            row,
        ],
        [col, row],
        [shape(rows, width), shape(8, width, kind=F32)],
        2 * rows * width * (deep + deeper),
        2 * (rows + width) * (deep + deeper) + 4 * rows * width,
        name="unit_grads",
    )(gp, gh, w_attend, w_expand, x, stat, gains)


def far_kernel(a_ref, b_ref, o_ref):
    for i in range(o_ref.shape[0] // ROWS):
        o_ref[pl.ds(i * ROWS, ROWS), :] = mul(a_ref[:, pl.ds(i * ROWS, ROWS)], b_ref[...], TN).astype(BF16)


def far_product(a, b, tile=512):
    tokens, width = a.shape
    half = width // 2
    cols = b.shape[1]
    return call(
        far_kernel,
        (cols // tile,),
        [pl.BlockSpec((tokens, half), lambda j: (0, 1)), pl.BlockSpec((tokens, tile), lambda j: (0, j))],
        pl.BlockSpec((half, tile), lambda j: (0, j)),
        shape(half, cols),
        2 * tokens * half * cols,
        2 * (tokens * half + tokens * cols + half * cols),
        name="far_product",
    )(a, b)


def near_kernel(a_ref, b_ref, r_ref, *outs):
    size = a_ref.shape[1] // len(outs)
    for i, out in enumerate(outs):
        at = pl.ds(i * size, size)
        out[...] = (mul(a_ref[:, at], b_ref[...], TN) + r_ref[at, :].astype(F32)).astype(out.dtype)


def near_product(a, b, received, tile=512):
    tokens, width = a.shape
    half = width // 2
    cols = b.shape[1]
    size = half // 4
    out = pl.BlockSpec((size, tile), lambda j: (0, j))
    return call(
        near_kernel,
        (cols // tile,),
        [
            pl.BlockSpec((tokens, half), lambda j: (0, 0)),
            pl.BlockSpec((tokens, tile), lambda j: (0, j)),
            pl.BlockSpec((half, tile), lambda j: (0, j)),
        ],
        [out] * 4,
        [shape(size, cols, kind=F32)] + [shape(size, cols)] * 3,
        2 * tokens * half * cols,
        2 * (tokens * half + tokens * cols + 2 * half * cols),
        name="near_product",
    )(a, b, received)


class SquareLinks:
    order = ((0, 0, 0), (1, 0, 0), (0, 1, 0), (1, 1, 0), (0, 0, 1), (1, 0, 1), (0, 1, 1), (1, 1, 1))

    def x_hop(self, v):
        return lax.ppermute(v, "fsdp", [(0, 1), (1, 0)])

    def y_hop(self, v):
        return lax.ppermute(v, "ctx", [(0, 2), (2, 0), (1, 3), (3, 1)])

    def core_hop(self, v):
        return lax.ppermute(v, "ctx", [(0, 1), (1, 0), (2, 3), (3, 2)])

    def place(self, bits):
        f, c = lax.axis_index("fsdp"), lax.axis_index("ctx")
        a, b, d = bits
        return ((f ^ a) * 2 + ((c // 2) ^ b)) * 2 + ((c % 2) ^ d)

    def spot(self, p):
        f, c = lax.axis_index("fsdp"), lax.axis_index("ctx")
        a, b, d = f ^ (p // 4), (c // 2) ^ (p // 2 % 2), (c % 2) ^ (p % 2)
        return d * 4 + b * 2 + a

    def to_relative(self, v):
        return reorder(v, [partial(self.place, bits) for bits in self.order])

    def to_whole(self, v):
        return reorder(v, [partial(self.spot, p) for p in range(8)])

    def gather(self, block):
        rows = block.shape[0]
        half = rows // 2
        from_x, from_y = self.x_hop(block), self.y_hop(block)
        corner = (self.x_hop(from_y[:half]), self.y_hop(from_x[half:]))
        near = jnp.concatenate([block, from_x, from_y, *corner], 0)
        return jnp.concatenate([near, self.core_hop(near)], 0)

    def scatter_far(self, left, right):
        return self.core_hop(far_product(left, right))

    def scatter_near(self, left, right, far):
        return near_product(left, right, far)

    def scatter_end(self, own, to_x, to_y, corner):
        half = corner.shape[0] // 2
        via_x, via_y = self.x_hop(corner[:half]), self.y_hop(corner[half:])
        to_y = jnp.concatenate([to_y[:half] + via_x, to_y[half:]], 0)
        to_x = jnp.concatenate([to_x[:half], to_x[half:] + via_y], 0)
        return own + self.x_hop(to_x).astype(F32) + self.y_hop(to_y).astype(F32)

    def others(self, v):
        c = lax.axis_index("ctx")
        return jnp.stack([v[c ^ bits] for bits in (2, 1, 3)])

    def gather_others(self, block):
        from_y = self.y_hop(block)
        return jnp.concatenate([from_y, self.core_hop(jnp.concatenate([block, from_y], 0))], 0)

    def scatter_others(self, near, far):
        theirs = self.core_hop(far)
        rows = near.shape[0]
        return theirs, lambda token: self.y_hop(after(theirs[rows:], token) + near)

    def sum_rows(self, v):
        v = v + self.core_hop(v)
        v = v + self.x_hop(v)
        return v + self.y_hop(v)


class AnyLinks:
    def to_relative(self, v):
        return v

    def to_whole(self, v):
        return v

    def gather(self, block):
        return lax.all_gather(block, ("fsdp", "ctx"), axis=0, tiled=True)

    def scatter_far(self, left, right):
        return None

    def scatter_near(self, left, right, far):
        return (jnp.einsum("tc,tk->ck", left, right, preferred_element_type=F32).astype(BF16),)

    def scatter_end(self, whole):
        return lax.psum_scatter(whole, ("fsdp", "ctx"), scatter_dimension=0, tiled=True).astype(F32)

    def others(self, v):
        return jnp.roll(v, -lax.axis_index("ctx"), 0)[1:]

    def gather_others(self, block):
        rows = block.shape[0]
        whole = lax.all_gather(block, "ctx", axis=0, tiled=True)
        return jnp.roll(whole, -rows * lax.axis_index("ctx"), 0)[rows:]

    def scatter_others(self, near, far):
        rows = near.shape[0]
        whole = jnp.concatenate([jnp.zeros_like(near), near, far], 0)
        whole = jnp.roll(whole, rows * lax.axis_index("ctx"), 0)
        theirs = lax.psum_scatter(whole, "ctx", scatter_dimension=0, tiled=True)
        return theirs, lambda token: jnp.zeros_like(theirs)

    def sum_rows(self, v):
        return lax.psum(v, ("fsdp", "ctx"))


def sum_tp(v):
    size = lax.axis_size("tp")
    if size & (size - 1):
        return lax.psum(v, "tp")
    step = 1
    while step < size:
        v = v + lax.ppermute(v, "tp", [(i, i ^ step) for i in range(size)])
        step *= 2
    return v


def end_kernel(x_ref, g_ref, e_ref, o_ref):
    x = x_ref[...].astype(F32)
    center = x - jnp.mean(x, -1, keepdims=True)
    scale = lax.rsqrt(jnp.mean(center * center, -1, keepdims=True) + EPS)
    unit = center * scale
    e = e_ref[...].astype(F32)
    rest = e - jnp.mean(e, -1, keepdims=True) - unit * jnp.mean(e * unit, -1, keepdims=True)
    o_ref[...] = g_ref[...].astype(F32) + scale * rest


def input_grads(x, g, e):
    rows, width = x.shape
    block = pl.BlockSpec((64, width), lambda i: (i, 0))
    return call(
        end_kernel, (rows // 64,), [block] * 3, block, shape(rows, width, kind=F32), 15 * x.size, 10 * x.size, name="input_grads"
    )(x, g, e)


def shards(
    stream_in,
    stream_grad,
    segments,
    positions,
    first_gain,
    first_shift,
    second_gain,
    second_shift,
    attend_weight,
    attend_bias,
    output_weight,
    expand_weight,
    expand_bias,
    contract_weight,
    output_bias,
):
    square = lax.axis_size("fsdp") == 2 and lax.axis_size("ctx") == 4
    links = SquareLinks() if square else AnyLinks()
    local_rows = attend_weight.shape[0]
    heads = attend_bias.shape[0]
    holders = lax.axis_size("ctx")
    holder = lax.axis_index("ctx")
    prompt = PROMPT // holders

    in_part = links.to_relative(stream_in)
    rows_in = lax.all_gather(in_part, "tp", axis=0, tiled=True)
    grad_part = links.to_relative(stream_grad)
    grad_late, rows_in = lax.optimization_barrier((grad_part, rows_in))
    rows_grad = lax.all_gather(grad_late, "tp", axis=0, tiled=True)
    row_count = rows_in.shape[0]

    attend_all = links.gather(attend_weight.reshape(local_rows, -1))
    expand_all = links.gather(expand_weight)
    contract_all = links.gather(contract_weight)
    output_all = links.gather(output_weight)

    gains = jnp.concatenate([jnp.stack([first_gain, first_shift, second_gain, second_shift]), jnp.zeros((4, first_gain.shape[0]), F32)])
    gains = links.to_relative(gains)
    row_pos = lax.dynamic_slice_in_dim(positions, holder * row_count, row_count)
    row_seg = lax.dynamic_slice_in_dim(segments, holder * row_count, row_count)
    starts = positions.reshape(holders, row_count)[:, 0]
    bias = jnp.where(links.others(starts) < row_pos[0], 0.0, -1e30).astype(F32)
    bias = jnp.repeat(bias, prompt)
    table = turn_table(row_pos)

    first_norm, second_norm, stat = norms(rows_in, gains)
    queries, pairs = project(first_norm, attend_all, attend_bias.reshape(-1), table, heads)
    pairs_far = links.gather_others(pairs[:prompt])
    activated, slope = expand(after(second_norm, pairs), expand_all, expand_bias)
    attended, row_sums = attend(after(queries, activated), pairs, pairs_far, bias, row_seg, prompt)
    mixed = mixed_sum(attended, activated, output_all, contract_all)
    branches = lax.psum_scatter(mixed, "tp", scatter_dimension=0, tiled=True)

    rows_grad = after(rows_grad, mixed)
    grad_attended, grad_pre, expand_sums = branch_grads(rows_grad, output_all, contract_all, slope)
    grad_queries, pair_own, pair_near, pair_far = attend_back(
        queries, grad_attended, attended, row_sums, pairs, pairs_far, bias, row_seg, prompt, table
    )
    core_part, y_part = links.scatter_others(pair_near, pair_far)
    far_c = links.scatter_far(rows_grad, after(activated, pair_own))
    y_part = y_part(pair_own)
    near_c = links.scatter_near(rows_grad, activated, far_c)
    far_e = links.scatter_far(second_norm, after(grad_pre, near_c[0]))
    grad_flat, attend_sums = pack(grad_queries, after(pair_own, near_c[0]), y_part, core_part, table, prompt)
    grad_unit, vector_parts = unit_grads(grad_flat, grad_pre, attend_all, expand_all, rows_in, stat, gains)
    unit_part = lax.psum_scatter(grad_unit, "tp", scatter_dimension=0, tiled=True)

    near_e = links.scatter_near(after(second_norm, grad_unit), grad_pre, far_e)
    far_a = links.scatter_far(first_norm, after(grad_flat, near_e[0]))
    far_o = links.scatter_far(rows_grad, after(attended, near_e[0]))
    near_a = links.scatter_near(first_norm, grad_flat, far_a)
    near_o = links.scatter_near(rows_grad, after(attended, near_a[0]), far_o)
    contract_weight_grad = links.scatter_end(*near_c)
    expand_weight_grad = links.scatter_end(*near_e)
    attend_weight_grad = links.scatter_end(*near_a).reshape(attend_weight.shape)
    output_weight_grad = links.scatter_end(*near_o)

    bias_sums = links.sum_rows(jnp.concatenate([attend_sums[0], expand_sums[0]]))
    attend_bias_grad = bias_sums[: grad_flat.shape[1]].reshape(attend_bias.shape)
    expand_bias_grad = bias_sums[grad_flat.shape[1] :]
    row_sum = jnp.sum(grad_part.astype(F32), 0)
    vectors = jnp.concatenate([vector_parts[:4], row_sum[None], jnp.zeros((3, row_sum.shape[0]), F32)])
    norm_sums = sum_tp(links.sum_rows(links.to_whole(vectors)))

    stream_out = links.to_whole((in_part.astype(F32) + branches.astype(F32))) + output_bias
    stream_out = stream_out.astype(BF16)
    input_grad = links.to_whole(input_grads(in_part, grad_part, unit_part))
    return (
        stream_out,
        input_grad,
        norm_sums[0],
        norm_sums[1],
        norm_sums[2],
        norm_sums[3],
        attend_weight_grad,
        attend_bias_grad,
        output_weight_grad,
        expand_weight_grad,
        expand_bias_grad,
        contract_weight_grad,
        norm_sums[4],
    )


def solution(mesh):
    tokens = P(("fsdp", "ctx", "tp"), None)
    weight = P(("fsdp", "ctx"), "tp")
    heads = P(("fsdp", "ctx"), "tp", None)
    return jax.shard_map(
        shards,
        mesh=mesh,
        in_specs=(
            tokens,
            tokens,
            P("fsdp"),
            P("fsdp"),
            P(),
            P(),
            P(),
            P(),
            heads,
            P("tp", None),
            weight,
            weight,
            P("tp"),
            weight,
            P(),
        ),
        out_specs=(
            tokens,
            tokens,
            P(),
            P(),
            P(),
            P(),
            heads,
            P("tp", None),
            weight,
            weight,
            P("tp"),
            weight,
            P(),
        ),
        check_vma=False,
    )
```

```python
from functools import partial, reduce
import math

import jax
import jax.numpy as jnp
from jax import lax
from jax.experimental import pallas as pl
from jax.experimental.pallas import tpu as pltpu
from jax.sharding import PartitionSpec as P

ROT = 64
PROMPT = 2048
EPS = 1e-05
F32 = jnp.float32
BF16 = jnp.bfloat16
ROWS = 256
HEAD = 256
NN = (((1,), (0,)), ((), ()))
NT = (((1,), (1,)), ((), ()))
TN = (((0,), (0,)), ((), ()))


def mul(a, b, dims):
    return lax.dot_general(a, b, dims, preferred_element_type=F32)


def call(kernel, grid, in_specs, out_specs, out_shape, flops, moved, exps=0, scratch=(), mib=48, name=None):
    return pl.pallas_call(
        kernel,
        grid=grid,
        in_specs=in_specs,
        out_specs=out_specs,
        out_shape=out_shape,
        scratch_shapes=scratch,
        compiler_params=pltpu.CompilerParams(vmem_limit_bytes=mib * 2**20),
        cost_estimate=pl.CostEstimate(flops=flops, bytes_accessed=moved, transcendentals=exps),
        name=name,
    )


def shape(*dims, kind=BF16):
    return jax.ShapeDtypeStruct(dims, kind)


def wide(row):
    return jnp.broadcast_to(row[None], (8, row.shape[0]))


def after(value, *others):
    return lax.optimization_barrier((value, *others))[0]


def turn(v, table, sign):
    head = v[:, :128]
    other = pltpu.roll(head, 96, 1) * table[:, 128:256] + pltpu.roll(head, 32, 1) * table[:, 256:]
    return jnp.concatenate([head * table[:, :128] + sign * other, v[:, 128:]], 1)


def turn_table(where_at):
    half = ROT // 2
    frequency = jnp.exp(jnp.arange(half, dtype=F32) * (-2.0 * math.log(10000.0) / ROT))
    angles = where_at.astype(F32)[:, None] * frequency[None, :]
    c, s = jnp.cos(angles), jnp.sin(angles)
    rows = where_at.shape[0]
    one, none = jnp.ones((rows, 128 - ROT), F32), jnp.zeros((rows, 128 - half), F32)
    return jnp.concatenate([c, c, one, -s, none, none[:, :half], s, none[:, : 128 - ROT]], 1)


def reorder_kernel(places, x_ref, o_ref):
    size = x_ref.shape[1] // len(places)
    for i, place in enumerate(places):
        o_ref[:, i * size : (i + 1) * size] = x_ref[:, pl.ds(pl.multiple_of(place() * size, size), size)]


def reorder(x, places):
    rows, cols = x.shape
    block = pl.BlockSpec((rows, cols), lambda: (0, 0))
    return call(partial(reorder_kernel, places), (), [block], block, shape(rows, cols, kind=x.dtype), 0, 4 * rows * cols, name="reorder")(x)


def norm_kernel(places, x_ref, gain_ref, first_ref, second_ref, x_out, stat_ref):
    x = x_ref[...].astype(F32)
    mean = jnp.mean(x, -1, keepdims=True)
    center = x - mean
    scale = lax.rsqrt(jnp.mean(center * center, -1, keepdims=True) + EPS)
    size = x_ref.shape[1] // len(places)
    for i, place in enumerate(places):
        at, to = pl.ds(pl.multiple_of(place() * size, size), size), pl.ds(i * size, size)
        part = x_ref[:, at]
        x_out[:, to] = part
        unit = (part.astype(F32) - mean) * scale
        first_ref[:, to] = (unit * gain_ref[0:1, at] + gain_ref[1:2, at]).astype(BF16)
        second_ref[:, to] = (unit * gain_ref[2:3, at] + gain_ref[3:4, at]).astype(BF16)
    lane = lax.broadcasted_iota(jnp.int32, stat_ref.shape, 1)
    stat_ref[...] = jnp.where(lane == 0, mean, scale)


def norms(x, gains, places):
    rows, width = x.shape
    block = pl.BlockSpec((128, width), lambda i: (i, 0))
    return call(
        partial(norm_kernel, places),
        (rows // 128,),
        [block, pl.BlockSpec((8, width), lambda i: (0, 0))],
        [block, block, block, pl.BlockSpec((128, 128), lambda i: (i, 0))],
        [shape(rows, width)] * 3 + [shape(rows, 128, kind=F32)],
        10 * rows * width,
        8 * rows * width,
        name="norms",
    )(x, gains)


def project_kernel(n_ref, w_ref, b_ref, table_ref, q_ref, kv_ref):
    head = q_ref.shape[1]
    for i in range(n_ref.shape[0] // ROWS):
        at = pl.ds(i * ROWS, ROWS)
        out = mul(n_ref[at, :], w_ref[...], NN) + b_ref[:1]
        q_ref[at, :] = turn(out[:, :head], table_ref[at, :], 1.0).astype(BF16)
        kv_ref[at, :head] = turn(out[:, head : 2 * head], table_ref[at, :], 1.0).astype(BF16)
        kv_ref[at, head:] = out[:, 2 * head :].astype(BF16)


def project(n, w, bias, table, heads):
    rows, depth = n.shape
    width = w.shape[1] // heads
    head = width // 3
    return call(
        project_kernel,
        (heads,),
        [
            pl.BlockSpec((rows, depth), lambda h: (0, 0)),
            pl.BlockSpec((depth, width), lambda h: (0, h)),
            pl.BlockSpec((8, width), lambda h: (0, h)),
            pl.BlockSpec((rows, 384), lambda h: (0, 0)),
        ],
        [pl.BlockSpec((rows, head), lambda h: (0, h)), pl.BlockSpec((rows, 2 * head), lambda h: (0, h))],
        [shape(rows, heads * head), shape(rows, heads * 2 * head)],
        2 * rows * depth * w.shape[1],
        2 * (rows * depth + w.size + rows * w.shape[1]),
        name="project",
    )(n, w, wide(bias), table)


def expand_kernel(n_ref, w_ref, b_ref, h_ref, d_ref):
    for i in range(n_ref.shape[0] // ROWS):
        at = pl.ds(i * ROWS, ROWS)
        pre = mul(n_ref[at, :], w_ref[...], NN) + b_ref[:1]
        below = 0.5 + 0.5 * lax.erf(pre * math.sqrt(0.5))
        h_ref[at, :] = (pre * below).astype(BF16)
        d_ref[at, :] = (below + pre * jnp.exp(-0.5 * pre * pre) * (1.0 / math.sqrt(2 * math.pi))).astype(BF16)


def expand(n, w, bias, tile=512):
    rows, depth = n.shape
    cols = w.shape[1]
    out = pl.BlockSpec((rows, tile), lambda j: (0, j))
    return call(
        expand_kernel,
        (cols // tile,),
        [
            pl.BlockSpec((rows, depth), lambda j: (0, 0)),
            pl.BlockSpec((depth, tile), lambda j: (0, j)),
            pl.BlockSpec((8, tile), lambda j: (0, j)),
        ],
        [out, out],
        [shape(rows, cols), shape(rows, cols)],
        2 * rows * depth * cols,
        2 * (rows * depth + w.size + 2 * rows * cols),
        2 * rows * cols,
        name="expand",
    )(n, w, wide(bias))


def attend_kernel(prompt, q_ref, ko, vo, kt, vt, bias_ref, segc_ref, segr_ref, o_ref, stat_ref):
    block = pl.program_id(1)
    tq = q_ref.shape[0]
    first_cont = prompt // tq
    cont = ko.shape[0] - prompt
    q = q_ref[...] * BF16(1.0 / math.sqrt(q_ref.shape[1]))
    rows = lax.broadcasted_iota(jnp.int32, (tq, 1), 0)

    def finish(scores, values):
        top = reduce(jnp.maximum, [jnp.max(s, -1, keepdims=True) for s in scores])
        exps = [jnp.exp(s - top) for s in scores]
        total = sum(jnp.sum(e, -1, keepdims=True) for e in exps)
        out = sum(mul(e.astype(BF16), v, NN) for e, v in zip(exps, values))
        o_ref[...] = (out / total).astype(BF16)
        stat_ref[0] = jnp.transpose(jnp.broadcast_to(top + jnp.log(total), (tq, 128)))[:8]

    @pl.when(block < first_cont)
    def _():
        cols = lax.broadcasted_iota(jnp.int32, (1, prompt), 1)
        own = jnp.where(cols <= rows + block * tq, mul(q, ko[:prompt], NT), -1e30)
        far = mul(q, kt[...], NT) + bias_ref[:1]
        finish([own, far], [vo[:prompt], vt[...]])

    @pl.when(block >= first_cont)
    def _():
        cols = lax.broadcasted_iota(jnp.int32, (1, cont), 1)
        own = mul(q, ko[:prompt], NT)
        read = (cols <= rows + (block - first_cont) * tq) & (segc_ref[:, :1] == segr_ref[:1])
        follow = jnp.where(read, mul(q, ko[prompt:], NT), -1e30)
        far = mul(q, kt[...], NT)
        finish([own, follow, far], [vo[:prompt], vo[prompt:], vt[...]])


def attend(q, kv, kv_far, bias, seg, prompt):
    rows, width = q.shape
    head = HEAD
    heads = width // head
    far = kv_far.shape[0]
    cont = rows - prompt
    tq = ROWS
    first = prompt // tq
    return call(
        partial(attend_kernel, prompt),
        (heads, rows // tq),
        [
            pl.BlockSpec((tq, head), lambda h, b: (b, h)),
            pl.BlockSpec((rows, head), lambda h, b: (0, 2 * h)),
            pl.BlockSpec((rows, head), lambda h, b: (0, 2 * h + 1)),
            pl.BlockSpec((far, head), lambda h, b: (0, 2 * h)),
            pl.BlockSpec((far, head), lambda h, b: (0, 2 * h + 1)),
            pl.BlockSpec((8, far), lambda h, b: (0, 0)),
            pl.BlockSpec((tq, 128), lambda h, b: (jnp.maximum(b - first, 0), 0)),
            pl.BlockSpec((8, cont), lambda h, b: (0, 0)),
        ],
        [pl.BlockSpec((tq, head), lambda h, b: (b, h)), pl.BlockSpec((1, 8, tq), lambda h, b: (h, 0, b))],
        [shape(rows, width), shape(heads, 8, rows, kind=F32)],
        4 * rows * (rows + far) * width,
        2 * (2 * q.size + kv.size + kv_far.size),
        rows * (rows + far) * heads,
        name="attend",
    )(q, kv, kv, kv_far, kv_far, wide(bias), jnp.broadcast_to(seg[prompt:, None], (cont, 128)), wide(seg[prompt:]))


def attend_back_kernel(
    prompt, q_ref, do_ref, o_ref, stat_ref, ko, vo, kt, vt, bias_ref, segc_ref, segr_ref, table_ref,
    dq_ref, own_ref, near_ref, far_ref, acc_k, acc_v,
):
    block = pl.program_id(1)
    tq, head = q_ref.shape
    first_cont = prompt // tq
    scale = 1.0 / math.sqrt(head)
    q = q_ref[...] * BF16(scale)
    do = do_ref[...]
    inner = jnp.sum(do.astype(F32) * o_ref[...].astype(F32), -1, keepdims=True)
    inner = jnp.transpose(jnp.broadcast_to(inner, (tq, 128)))[:1]
    stat = stat_ref[0, :1]
    cols = lax.broadcasted_iota(jnp.int32, (1, tq), 1)

    @pl.when(block == 0)
    def _():
        acc_k[...] = jnp.zeros_like(acc_k)
        acc_v[...] = jnp.zeros_like(acc_v)

    def part(keys, values, at, seen):
        probs = jnp.exp(seen(mul(keys, q, NT)) - stat)
        grads = (probs * (mul(values, do, NT) - inner)).astype(BF16)
        acc_v[at, :] += mul(probs.astype(BF16), do, NN)
        acc_k[at, :] += mul(grads, q, NN)
        return mul(grads, keys, TN)

    def far_parts(total, seen):
        for i in range(kt.shape[0] // prompt):
            at = pl.ds(i * prompt, prompt)
            total += part(kt[at, :], vt[at, :], pl.ds(ko.shape[0] + i * prompt, prompt), partial(seen, at))
        dq_ref[...] = turn(total * scale, table_ref[...], -1.0).astype(BF16)

    @pl.when(block < first_cont)
    def _():
        rows = lax.broadcasted_iota(jnp.int32, (prompt, 1), 0)
        total = part(
            ko[:prompt], vo[:prompt], pl.ds(0, prompt), lambda s: jnp.where(rows <= cols + block * tq, s, -1e30)
        )
        far_parts(total, lambda at, s: s + bias_ref[at, :1])

    @pl.when(block >= first_cont)
    def _():
        cont = ko.shape[0] - prompt
        rows = lax.broadcasted_iota(jnp.int32, (cont, 1), 0)
        total = part(ko[:prompt], vo[:prompt], pl.ds(0, prompt), lambda s: s)
        read = (rows <= cols + (block - first_cont) * tq) & (segc_ref[:, :1] == segr_ref[:1])
        total += part(ko[prompt:], vo[prompt:], pl.ds(prompt, cont), lambda s: jnp.where(read, s, -1e30))
        far_parts(total, lambda at, s: s)

    @pl.when(block == pl.num_programs(1) - 1)
    def _():
        start = 0
        for ref in (own_ref, near_ref, far_ref):
            at = pl.ds(start, ref.shape[0])
            ref[:, :head] = acc_k[at, :].astype(ref.dtype)
            ref[:, head:] = acc_v[at, :].astype(ref.dtype)
            start += ref.shape[0]


def attend_back(q, do, o, stat, kv, kv_far, bias, seg, prompt, table):
    rows, width = q.shape
    head = HEAD
    heads = width // head
    far = kv_far.shape[0]
    cont = rows - prompt
    tq = ROWS
    first = prompt // tq
    row = pl.BlockSpec((tq, head), lambda h, b: (b, h))

    def column(n, odd):
        return pl.BlockSpec((n, head), lambda h, b: (0, 2 * h + odd))

    def pair(n):
        return pl.BlockSpec((n, 2 * head), lambda h, b: (0, h))

    return call(
        partial(attend_back_kernel, prompt),
        (heads, rows // tq),
        [
            row,
            row,
            row,
            pl.BlockSpec((1, 8, tq), lambda h, b: (h, 0, b)),
            column(rows, 0),
            column(rows, 1),
            column(far, 0),
            column(far, 1),
            pl.BlockSpec((far, 128), lambda h, b: (0, 0)),
            pl.BlockSpec((cont, 128), lambda h, b: (0, 0)),
            pl.BlockSpec((8, tq), lambda h, b: (0, jnp.maximum(b - first, 0))),
            pl.BlockSpec((tq, 384), lambda h, b: (b, 0)),
        ],
        [row, pair(rows), pair(prompt), pair(far - prompt)],
        [
            shape(rows, width),
            shape(rows, 2 * width, kind=F32),
            shape(prompt, 2 * width),
            shape(far - prompt, 2 * width),
        ],
        10 * rows * (rows + far) * width,
        2 * (4 * q.size + 4 * kv.size + 2 * kv_far.size),
        rows * (rows + far) * heads,
        [pltpu.VMEM((rows + far, head), F32), pltpu.VMEM((rows + far, head), F32)],
        name="attend_back",
    )(
        q,
        do,
        o,
        stat,
        kv,
        kv,
        kv_far,
        kv_far,
        jnp.broadcast_to(bias[:, None], (far, 128)),
        jnp.broadcast_to(seg[prompt:, None], (cont, 128)),
        wide(seg[prompt:]),
        table,
    )


def mixed_kernel(a_ref, h_ref, wa_ref, wh_ref, o_ref):
    for i in range(a_ref.shape[0] // ROWS):
        at = pl.ds(i * ROWS, ROWS)
        o_ref[at, :] = (mul(a_ref[at, :], wa_ref[...], NT) + mul(h_ref[at, :], wh_ref[...], NT)).astype(BF16)


def mixed_sum(attended, activated, w_out, w_contract, tile=512):
    rows = attended.shape[0]
    deep, deeper = attended.shape[1], activated.shape[1]
    width = w_out.shape[0]
    return call(
        mixed_kernel,
        (width // tile,),
        [
            pl.BlockSpec((rows, deep), lambda j: (0, 0)),
            pl.BlockSpec((rows, deeper), lambda j: (0, 0)),
            pl.BlockSpec((tile, deep), lambda j: (j, 0)),
            pl.BlockSpec((tile, deeper), lambda j: (j, 0)),
        ],
        pl.BlockSpec((rows, tile), lambda j: (0, j)),
        shape(rows, width),
        2 * rows * width * (deep + deeper),
        2 * (rows + width) * (deep + deeper) + 2 * rows * width,
        name="mixed_sum",
    )(attended, activated, w_out, w_contract)


def attended_grad_kernel(g_ref, w_ref, o_ref):
    for i in range(g_ref.shape[0] // ROWS):
        at = pl.ds(i * ROWS, ROWS)
        o_ref[at, :] = mul(g_ref[at, :], w_ref[...], NN).astype(BF16)


def attended_grads(g, w, tile=256):
    rows, depth = g.shape
    cols = w.shape[1]
    return call(
        attended_grad_kernel,
        (cols // tile,),
        [pl.BlockSpec((rows, depth), lambda j: (0, 0)), pl.BlockSpec((depth, tile), lambda j: (0, j))],
        pl.BlockSpec((rows, tile), lambda j: (0, j)),
        shape(rows, cols),
        2 * rows * depth * cols,
        2 * (rows * depth + w.size + rows * cols),
        name="attended_grads",
    )(g, w)


def hidden_grad_kernel(g_ref, w_ref, d_ref, gp_ref, sum_ref):
    total = 0.0
    for i in range(g_ref.shape[0] // ROWS):
        at = pl.ds(i * ROWS, ROWS)
        grad = (mul(g_ref[at, :], w_ref[...], NN) * d_ref[at, :].astype(F32)).astype(BF16)
        gp_ref[at, :] = grad
        total += jnp.sum(grad.astype(F32), 0, keepdims=True)
    sum_ref[...] = jnp.broadcast_to(total, sum_ref.shape)


def hidden_grads(g, w, slope, tile=512):
    rows, depth = g.shape
    cols = w.shape[1]
    tall = pl.BlockSpec((rows, tile), lambda j: (0, j))
    return call(
        hidden_grad_kernel,
        (cols // tile,),
        [pl.BlockSpec((rows, depth), lambda j: (0, 0)), pl.BlockSpec((depth, tile), lambda j: (0, j)), tall],
        [tall, pl.BlockSpec((8, tile), lambda j: (0, j))],
        [shape(rows, cols), shape(8, cols, kind=F32)],
        2 * rows * depth * cols,
        2 * (rows * depth + w.size + 2 * rows * cols),
        name="hidden_grads",
    )(g, w, slope)


def pack_kernel(prompt_blocks, q_ref, own_ref, near_ref, far_ref, table_ref, o_ref, sum_ref):
    block = pl.program_id(1)
    head = q_ref.shape[1]
    theirs = near_ref[...].astype(F32) + far_ref[...].astype(F32)
    both = own_ref[...] + jnp.where(block < prompt_blocks, theirs, 0.0)
    out = [q_ref[...], turn(both[:, :head], table_ref[...], -1.0).astype(BF16), both[:, head:].astype(BF16)]

    @pl.when(block == 0)
    def _():
        sum_ref[...] = jnp.zeros_like(sum_ref)

    for i, part in enumerate(out):
        o_ref[:, i * head : (i + 1) * head] = part
        sum_ref[:, i * head : (i + 1) * head] += jnp.sum(part.astype(F32), 0, keepdims=True)


def pack(dq, own, near, far, table, prompt):
    rows, width = dq.shape
    head = HEAD
    heads = width // head
    tq = ROWS
    blocks = prompt // tq
    theirs = pl.BlockSpec((tq, 2 * head), lambda h, b: (jnp.minimum(b, blocks - 1), h))
    return call(
        partial(pack_kernel, blocks),
        (heads, rows // tq),
        [
            pl.BlockSpec((tq, head), lambda h, b: (b, h)),
            pl.BlockSpec((tq, 2 * head), lambda h, b: (b, h)),
            theirs,
            theirs,
            pl.BlockSpec((tq, 384), lambda h, b: (b, 0)),
        ],
        [pl.BlockSpec((tq, 3 * head), lambda h, b: (b, h)), pl.BlockSpec((8, 3 * head), lambda h, b: (0, h))],
        [shape(rows, 3 * width), shape(8, 3 * width, kind=F32)],
        10 * rows * width,
        16 * rows * width,
        name="pack",
    )(dq, own, near, far, table)


def unit_grad_kernel(gp_ref, gh_ref, wa_ref, we_ref, x_ref, stat_ref, gain_ref, e_ref, sum_ref):
    sums = [0.0] * 4
    for i in range(gp_ref.shape[0] // ROWS):
        at = pl.ds(i * ROWS, ROWS)
        first = mul(gp_ref[at, :], wa_ref[...], NT)
        second = mul(gh_ref[at, :], we_ref[...], NT)
        e_ref[at, :] = (first * gain_ref[0:1] + second * gain_ref[2:3]).astype(BF16)
        unit = (x_ref[at, :].astype(F32) - stat_ref[at, 0:1]) * stat_ref[at, 1:2]
        for j, v in enumerate((first * unit, first, second * unit, second)):
            sums[j] += jnp.sum(v, 0, keepdims=True)
    for j in range(4):
        sum_ref[j : j + 1] = sums[j]
    sum_ref[4:] = jnp.zeros_like(sum_ref[4:])


def unit_grads(gp, gh, w_attend, w_expand, x, stat, gains, tile=512):
    rows, width = x.shape
    deep, deeper = gp.shape[1], gh.shape[1]
    col = pl.BlockSpec((rows, tile), lambda j: (0, j))
    row = pl.BlockSpec((8, tile), lambda j: (0, j))
    return call(
        unit_grad_kernel,
        (width // tile,),
        [
            pl.BlockSpec((rows, deep), lambda j: (0, 0)),
            pl.BlockSpec((rows, deeper), lambda j: (0, 0)),
            pl.BlockSpec((tile, deep), lambda j: (j, 0)),
            pl.BlockSpec((tile, deeper), lambda j: (j, 0)),
            col,
            pl.BlockSpec((rows, 128), lambda j: (0, 0)),
            row,
        ],
        [col, row],
        [shape(rows, width), shape(8, width, kind=F32)],
        2 * rows * width * (deep + deeper),
        2 * (rows + width) * (deep + deeper) + 4 * rows * width,
        name="unit_grads",
    )(gp, gh, w_attend, w_expand, x, stat, gains)


def far_kernel(a_ref, b_ref, o_ref):
    for i in range(o_ref.shape[0] // ROWS):
        o_ref[pl.ds(i * ROWS, ROWS), :] = mul(a_ref[:, pl.ds(i * ROWS, ROWS)], b_ref[...], TN).astype(BF16)


def far_product(a, b, tile=512):
    tokens, width = a.shape
    half = width // 2
    cols = b.shape[1]
    return call(
        far_kernel,
        (cols // tile,),
        [pl.BlockSpec((tokens, half), lambda j: (0, 1)), pl.BlockSpec((tokens, tile), lambda j: (0, j))],
        pl.BlockSpec((half, tile), lambda j: (0, j)),
        shape(half, cols),
        2 * tokens * half * cols,
        2 * (tokens * half + tokens * cols + half * cols),
        name="far_product",
    )(a, b)


def near_kernel(a_ref, b_ref, r_ref, *outs):
    size = a_ref.shape[1] // len(outs)
    for i, out in enumerate(outs):
        at = pl.ds(i * size, size)
        out[...] = (mul(a_ref[:, at], b_ref[...], TN) + r_ref[at, :].astype(F32)).astype(out.dtype)


def near_product(a, b, received, tile=512):
    tokens, width = a.shape
    half = width // 2
    cols = b.shape[1]
    size = half // 4
    out = pl.BlockSpec((size, tile), lambda j: (0, j))
    return call(
        near_kernel,
        (cols // tile,),
        [
            pl.BlockSpec((tokens, half), lambda j: (0, 0)),
            pl.BlockSpec((tokens, tile), lambda j: (0, j)),
            pl.BlockSpec((half, tile), lambda j: (0, j)),
        ],
        [out] * 4,
        [shape(size, cols, kind=F32)] + [shape(size, cols)] * 3,
        2 * tokens * half * cols,
        2 * (tokens * half + tokens * cols + 2 * half * cols),
        name="near_product",
    )(a, b, received)


class Hops:
    def __init__(self, send, recv):
        self.send, self.recv, self.count = send, recv, 0
        f, c, t = (lax.axis_index(a) for a in ("fsdp", "ctx", "tp"))
        ring = lax.axis_size("tp")
        self.to = {
            "x": {"fsdp": 1 - f},
            "y": {"ctx": (c + 2) % 4},
            "core": {"ctx": c + 1 - 2 * (c % 2)},
            "up": {"tp": (t + 1) % ring},
        }
        self.back = {"tp": (t + ring - 1) % ring}

    def greet(self):
        barrier = pltpu.get_barrier_semaphore()
        near = [*self.to.values(), self.back]
        for device in near:
            pl.semaphore_signal(barrier, inc=1, device_id=device, device_id_type=pl.DeviceIdType.MESH)
        pl.semaphore_wait(barrier, len(near))

    def copy(self, way, src, dst):
        made = pltpu.make_async_remote_copy(
            src, dst, self.send.at[self.count], self.recv.at[self.count],
            device_id=self.to[way], device_id_type=pl.DeviceIdType.MESH,
        )
        self.count += 1
        made.start()
        return made


def collect_kernel(n, x_ref, *refs):
    parts, rows_ref, wholes = refs[:n], refs[n], refs[n + 1 : 2 * n + 1]
    send, recv, local = refs[2 * n + 1 :]
    hops = Hops(send, recv)
    t, ring = lax.axis_index("tp"), lax.axis_size("tp")
    rows = x_ref.shape[0]
    chunk = rows // 2
    own = [pltpu.make_async_copy(p, w.at[pl.ds(0, p.shape[0])], local.at[1 + i]) for i, (p, w) in enumerate(zip(parts, wholes))]
    own.append(pltpu.make_async_copy(x_ref, rows_ref.at[pl.ds(t * rows, rows)], local.at[0]))
    for copy in own:
        copy.start()
    hops.greet()
    sent = []

    def ring_hop(step, part):
        at = pl.ds(((t + ring - step) % ring) * rows + part * chunk, chunk)
        src = x_ref.at[pl.ds(part * chunk, chunk)] if step == 0 else rows_ref.at[at]
        return hops.copy("up", src, rows_ref.at[at])

    def first(i):
        size = parts[i].shape[0]
        return [hops.copy(way, parts[i], wholes[i].at[pl.ds(slot * size, size)]) for way, slot in (("x", 1), ("y", 2))]

    def across(i, slots):
        size = parts[i].shape[0]
        for slot in slots:
            src = parts[i] if slot == 0 else wholes[i].at[pl.ds(slot * size, size)]
            sent.append(hops.copy("core", src, wholes[i].at[pl.ds((4 + slot) * size, size)]))

    def corner(i):
        size = parts[i].shape[0]
        half = size // 2
        top, low = pl.ds(3 * size, half), pl.ds(3 * size + half, half)
        return [
            hops.copy("x", wholes[i].at[pl.ds(2 * size, half)], wholes[i].at[top]),
            hops.copy("y", wholes[i].at[pl.ds(size + half, half)], wholes[i].at[low]),
        ]

    def arrive(copies):
        for copy in copies:
            copy.wait_recv()
        sent.extend(("sent", copy) for copy in copies)

    firsts, corners, rings = {}, {}, {}
    firsts[0] = first(0)
    rings[0, 0], rings[0, 1] = ring_hop(0, 0), ring_hop(0, 1)
    if n > 1:
        firsts[1] = first(1)
    for i in range(n):
        across(i, [0])
    plan = [("r", 0, 0), ("f", 0), ("r", 0, 1), ("r", 1, 0), ("f", 1), ("r", 1, 1), ("c", 0), ("f", 2), ("r", 2, 0), ("c", 1), ("r", 2, 1), ("c", 2)]
    for kind, *which in plan:
        if kind == "r":
            step, part = which
            arrive([rings[step, part]])
            if step < ring - 2:
                rings[step + 1, part] = ring_hop(step + 1, part)
            continue
        i = which[0]
        if kind == "f":
            arrive(firsts[i])
            corners[i] = corner(i)
            if i + 2 < n:
                firsts[i + 2] = first(i + 2)
            across(i, [1, 2])
        else:
            arrive(corners[i])
            across(i, [3])
    for copy in sent:
        if isinstance(copy, tuple):
            copy[1].wait_send()
        else:
            copy.wait()
    for copy in own:
        copy.wait()


def collect(x, parts):
    ring = lax.axis_size("tp")
    n = len(parts)
    copies = 2 * (ring - 1) + 8 * n
    ref = pl.BlockSpec(memory_space=pl.ANY)
    return pl.pallas_call(
        partial(collect_kernel, n),
        in_specs=[ref] * (n + 1),
        out_specs=[ref] * (n + 1),
        out_shape=[shape(ring * x.shape[0], x.shape[1])] + [shape(8 * p.shape[0], p.shape[1]) for p in parts],
        scratch_shapes=[
            pltpu.SemaphoreType.DMA((copies,)),
            pltpu.SemaphoreType.DMA((copies,)),
            pltpu.SemaphoreType.DMA((n + 1,)),
        ],
        compiler_params=pltpu.CompilerParams(collective_id=0, has_side_effects=True),
        cost_estimate=pl.CostEstimate(flops=0, bytes_accessed=200 * 2**20, transcendentals=0),
        name="collect",
    )(x, *parts)


class SquareLinks:
    order = ((0, 0, 0), (1, 0, 0), (0, 1, 0), (1, 1, 0), (0, 0, 1), (1, 0, 1), (0, 1, 1), (1, 1, 1))

    def x_hop(self, v):
        return lax.ppermute(v, "fsdp", [(0, 1), (1, 0)])

    def y_hop(self, v):
        return lax.ppermute(v, "ctx", [(0, 2), (2, 0), (1, 3), (3, 1)])

    def core_hop(self, v):
        return lax.ppermute(v, "ctx", [(0, 1), (1, 0), (2, 3), (3, 2)])

    def place(self, bits):
        f, c = lax.axis_index("fsdp"), lax.axis_index("ctx")
        a, b, d = bits
        return ((f ^ a) * 2 + ((c // 2) ^ b)) * 2 + ((c % 2) ^ d)

    def spot(self, p):
        f, c = lax.axis_index("fsdp"), lax.axis_index("ctx")
        a, b, d = f ^ (p // 4), (c // 2) ^ (p // 2 % 2), (c % 2) ^ (p % 2)
        return d * 4 + b * 2 + a

    def places(self):
        return [partial(self.place, bits) for bits in self.order]

    def spots(self):
        return [partial(self.spot, p) for p in range(8)]

    def to_relative(self, v):
        return reorder(v, self.places())

    def to_whole(self, v):
        return reorder(v, self.spots())

    def collect(self, x, parts):
        return collect(x, parts)

    def gather(self, block):
        rows = block.shape[0]
        half = rows // 2
        from_x, from_y = self.x_hop(block), self.y_hop(block)
        corner = (self.x_hop(from_y[:half]), self.y_hop(from_x[half:]))
        near = jnp.concatenate([block, from_x, from_y, *corner], 0)
        return jnp.concatenate([near, self.core_hop(near)], 0)

    def scatter_far(self, left, right):
        return self.core_hop(far_product(left, right))

    def scatter_near(self, left, right, far):
        return near_product(left, right, far)

    def scatter_end(self, own, to_x, to_y, corner):
        half = corner.shape[0] // 2
        via_x, via_y = self.x_hop(corner[:half]), self.y_hop(corner[half:])
        to_y = jnp.concatenate([to_y[:half] + via_x, to_y[half:]], 0)
        to_x = jnp.concatenate([to_x[:half], to_x[half:] + via_y], 0)
        return own + self.x_hop(to_x).astype(F32) + self.y_hop(to_y).astype(F32)

    def others(self, v):
        c = lax.axis_index("ctx")
        return jnp.stack([v[c ^ bits] for bits in (2, 1, 3)])

    def gather_others(self, block):
        from_y = self.y_hop(block)
        return jnp.concatenate([from_y, self.core_hop(jnp.concatenate([block, from_y], 0))], 0)

    def scatter_others(self, near, far):
        theirs = self.core_hop(far)
        rows = near.shape[0]
        return theirs, lambda token: self.y_hop(after(theirs, token)[rows:] + near)

    def sum_rows(self, v):
        v = v + self.core_hop(v)
        v = v + self.x_hop(v)
        return v + self.y_hop(v)


class AnyLinks:
    def places(self):
        return [lambda: 0]

    def spots(self):
        return [lambda: 0]

    def collect(self, x, parts):
        return [lax.all_gather(x, "tp", axis=0, tiled=True)] + [self.gather(part) for part in parts]

    def to_relative(self, v):
        return v

    def to_whole(self, v):
        return v

    def gather(self, block):
        return lax.all_gather(block, ("fsdp", "ctx"), axis=0, tiled=True)

    def scatter_far(self, left, right):
        return None

    def scatter_near(self, left, right, far):
        return (jnp.einsum("tc,tk->ck", left, right, preferred_element_type=F32).astype(BF16),)

    def scatter_end(self, whole):
        return lax.psum_scatter(whole, ("fsdp", "ctx"), scatter_dimension=0, tiled=True).astype(F32)

    def others(self, v):
        return jnp.roll(v, -lax.axis_index("ctx"), 0)[1:]

    def gather_others(self, block):
        rows = block.shape[0]
        whole = lax.all_gather(block, "ctx", axis=0, tiled=True)
        return jnp.roll(whole, -rows * lax.axis_index("ctx"), 0)[rows:]

    def scatter_others(self, near, far):
        rows = near.shape[0]
        whole = jnp.concatenate([jnp.zeros_like(near), near, far], 0)
        whole = jnp.roll(whole, rows * lax.axis_index("ctx"), 0)
        theirs = lax.psum_scatter(whole, "ctx", scatter_dimension=0, tiled=True)
        return theirs, lambda token: jnp.zeros_like(theirs)

    def sum_rows(self, v):
        return lax.psum(v, ("fsdp", "ctx"))


def sum_tp(v):
    size = lax.axis_size("tp")
    if size & (size - 1):
        return lax.psum(v, "tp")
    step = 1
    while step < size:
        v = v + lax.ppermute(v, "tp", [(i, i ^ step) for i in range(size)])
        step *= 2
    return v


def output_kernel(spots, x_ref, m_ref, b_ref, o_ref):
    size = x_ref.shape[1] // len(spots)
    for i, spot in enumerate(spots):
        at, to = pl.ds(pl.multiple_of(spot() * size, size), size), pl.ds(i * size, size)
        o_ref[:, to] = (x_ref[:, to].astype(F32) + m_ref[:, at].astype(F32) + b_ref[:1, to]).astype(BF16)


def output_rows(x, mixed, bias, spots):
    rows, width = x.shape
    block = pl.BlockSpec((64, width), lambda i: (i, 0))
    return call(
        partial(output_kernel, spots),
        (rows // 64,),
        [block, block, pl.BlockSpec((8, width), lambda i: (0, 0))],
        block,
        shape(rows, width),
        2 * x.size,
        6 * x.size,
        name="output_rows",
    )(x, mixed, wide(bias))


def end_kernel(spots, x_ref, g_ref, e_ref, o_ref, e_whole):
    size = x_ref.shape[1] // len(spots)
    for i, spot in enumerate(spots):
        e_whole[:, i * size : (i + 1) * size] = e_ref[:, pl.ds(pl.multiple_of(spot() * size, size), size)].astype(F32)
    x = x_ref[...].astype(F32)
    center = x - jnp.mean(x, -1, keepdims=True)
    scale = lax.rsqrt(jnp.mean(center * center, -1, keepdims=True) + EPS)
    unit = center * scale
    e = e_whole[...]
    rest = e - jnp.mean(e, -1, keepdims=True) - unit * jnp.mean(e * unit, -1, keepdims=True)
    o_ref[...] = g_ref[...].astype(F32) + scale * rest


def input_grads(x, g, e, spots):
    rows, width = x.shape
    block = pl.BlockSpec((64, width), lambda i: (i, 0))
    return call(
        partial(end_kernel, spots),
        (rows // 64,),
        [block] * 3,
        block,
        shape(rows, width, kind=F32),
        15 * x.size,
        10 * x.size,
        scratch=[pltpu.VMEM((64, width), F32)],
        name="input_grads",
    )(x, g, e)


def shards(
    stream_in,
    stream_grad,
    segments,
    positions,
    first_gain,
    first_shift,
    second_gain,
    second_shift,
    attend_weight,
    attend_bias,
    output_weight,
    expand_weight,
    expand_bias,
    contract_weight,
    output_bias,
):
    square = (lax.axis_size("fsdp"), lax.axis_size("ctx"), lax.axis_size("tp")) == (2, 4, 4)
    links = SquareLinks() if square else AnyLinks()
    local_rows = attend_weight.shape[0]
    heads = attend_bias.shape[0]
    holders = lax.axis_size("ctx")
    holder = lax.axis_index("ctx")
    prompt = PROMPT // holders

    rows_in, attend_all, expand_all, output_all = links.collect(
        stream_in, [attend_weight.reshape(local_rows, -1), expand_weight, output_weight]
    )
    row_count = rows_in.shape[0]
    rows_grad = lax.all_gather(links.to_relative(after(stream_grad, rows_in)), "tp", axis=0, tiled=True)
    contract_all = links.gather(after(contract_weight, rows_in))

    gains = jnp.concatenate([jnp.stack([first_gain, first_shift, second_gain, second_shift]), jnp.zeros((4, first_gain.shape[0]), F32)])
    own_gains = links.to_relative(gains)
    row_pos = lax.dynamic_slice_in_dim(positions, holder * row_count, row_count)
    row_seg = lax.dynamic_slice_in_dim(segments, holder * row_count, row_count)
    starts = positions.reshape(holders, row_count)[:, 0]
    bias = jnp.where(links.others(starts) < row_pos[0], 0.0, -1e30).astype(F32)
    bias = jnp.repeat(bias, prompt)
    table = turn_table(row_pos)

    first_norm, second_norm, rows_in, stat = norms(rows_in, gains, links.places())
    queries, pairs = project(first_norm, attend_all, attend_bias.reshape(-1), table, heads)
    pairs_far = links.gather_others(pairs[:prompt])
    activated, slope = expand(after(second_norm, pairs), expand_all, expand_bias)
    attended, row_sums = attend(after(queries, activated), pairs, pairs_far, bias, row_seg, prompt)
    mixed = mixed_sum(attended, activated, output_all, contract_all)
    branches = lax.psum_scatter(mixed, "tp", scatter_dimension=0, tiled=True)

    rows_grad = after(rows_grad, mixed)
    grad_attended = attended_grads(rows_grad, output_all)
    grad_queries, pair_own, pair_near, pair_far = attend_back(
        queries, grad_attended, attended, row_sums, pairs, pairs_far, bias, row_seg, prompt, table
    )
    core_part, y_part = links.scatter_others(pair_near, pair_far)
    far_c = links.scatter_far(rows_grad, after(activated, pair_own))
    y_part = y_part(pair_own if far_c is None else far_c)
    grad_pre, expand_sums = hidden_grads(after(rows_grad, y_part), contract_all, slope)
    near_c = links.scatter_near(rows_grad, after(activated, grad_pre), far_c)
    grad_flat, attend_sums = pack(grad_queries, after(pair_own, near_c[0]), y_part, core_part, table, prompt)
    grad_unit, vector_parts = unit_grads(grad_flat, grad_pre, attend_all, expand_all, rows_in, stat, own_gains)
    unit_part = lax.psum_scatter(grad_unit, "tp", scatter_dimension=0, tiled=True)

    far_e = links.scatter_far(second_norm, after(grad_pre, grad_unit))
    near_e = links.scatter_near(second_norm, grad_pre, far_e)
    far_a = links.scatter_far(first_norm, after(grad_flat, near_e[0]))
    far_o = links.scatter_far(rows_grad, after(attended, near_e[0]))
    near_a = links.scatter_near(first_norm, grad_flat, far_a)
    near_o = links.scatter_near(rows_grad, after(attended, near_a[0]), far_o)
    contract_weight_grad = links.scatter_end(*near_c)
    expand_weight_grad = links.scatter_end(*near_e)
    attend_weight_grad = links.scatter_end(*near_a).reshape(attend_weight.shape)
    output_weight_grad = links.scatter_end(*near_o)

    bias_sums = links.sum_rows(jnp.concatenate([attend_sums[0], expand_sums[0]]))
    attend_bias_grad = bias_sums[: grad_flat.shape[1]].reshape(attend_bias.shape)
    expand_bias_grad = bias_sums[grad_flat.shape[1] :]
    row_sum = jnp.sum(stream_grad.astype(F32), 0)
    vectors = jnp.concatenate([links.to_whole(vector_parts)[:4], row_sum[None]])
    norm_sums = sum_tp(links.sum_rows(vectors))

    stream_out = output_rows(stream_in, branches, output_bias, links.spots())
    input_grad = input_grads(stream_in, stream_grad, unit_part, links.spots())
    return (
        stream_out,
        input_grad,
        norm_sums[0],
        norm_sums[1],
        norm_sums[2],
        norm_sums[3],
        attend_weight_grad,
        attend_bias_grad,
        output_weight_grad,
        expand_weight_grad,
        expand_bias_grad,
        contract_weight_grad,
        norm_sums[4],
    )


def solution(mesh):
    tokens = P(("fsdp", "ctx", "tp"), None)
    weight = P(("fsdp", "ctx"), "tp")
    heads = P(("fsdp", "ctx"), "tp", None)
    return jax.shard_map(
        shards,
        mesh=mesh,
        in_specs=(
            tokens,
            tokens,
            P("fsdp"),
            P("fsdp"),
            P(),
            P(),
            P(),
            P(),
            heads,
            P("tp", None),
            weight,
            weight,
            P("tp"),
            weight,
            P(),
        ),
        out_specs=(
            tokens,
            tokens,
            P(),
            P(),
            P(),
            P(),
            heads,
            P("tp", None),
            weight,
            weight,
            P("tp"),
            weight,
            P(),
        ),
        check_vma=False,
    )
```

```python
from functools import partial, reduce
import math

import jax
import jax.numpy as jnp
from jax import lax
from jax.experimental import pallas as pl
from jax.experimental.pallas import tpu as pltpu
from jax.sharding import PartitionSpec as P

ROT = 64
PROMPT = 2048
EPS = 1e-05
F32 = jnp.float32
BF16 = jnp.bfloat16
ROWS = 256
HEAD = 256
NN = (((1,), (0,)), ((), ()))
NT = (((1,), (1,)), ((), ()))
TN = (((0,), (0,)), ((), ()))


def mul(a, b, dims):
    return lax.dot_general(a, b, dims, preferred_element_type=F32)


def call(kernel, grid, in_specs, out_specs, out_shape, flops, moved, exps=0, scratch=(), mib=48, name=None):
    return pl.pallas_call(
        kernel,
        grid=grid,
        in_specs=in_specs,
        out_specs=out_specs,
        out_shape=out_shape,
        scratch_shapes=scratch,
        compiler_params=pltpu.CompilerParams(vmem_limit_bytes=mib * 2**20),
        cost_estimate=pl.CostEstimate(flops=flops, bytes_accessed=moved, transcendentals=exps),
        name=name,
    )


def shape(*dims, kind=BF16):
    return jax.ShapeDtypeStruct(dims, kind)


def wide(row):
    return jnp.broadcast_to(row[None], (8, row.shape[0]))


def after(value, *others):
    return lax.optimization_barrier((value, *others))[0]


def turn(v, table, sign):
    head = v[:, :128]
    other = pltpu.roll(head, 96, 1) * table[:, 128:256] + pltpu.roll(head, 32, 1) * table[:, 256:]
    return jnp.concatenate([head * table[:, :128] + sign * other, v[:, 128:]], 1)


def turn_table(where_at):
    half = ROT // 2
    frequency = jnp.exp(jnp.arange(half, dtype=F32) * (-2.0 * math.log(10000.0) / ROT))
    angles = where_at.astype(F32)[:, None] * frequency[None, :]
    c, s = jnp.cos(angles), jnp.sin(angles)
    rows = where_at.shape[0]
    one, none = jnp.ones((rows, 128 - ROT), F32), jnp.zeros((rows, 128 - half), F32)
    return jnp.concatenate([c, c, one, -s, none, none[:, :half], s, none[:, : 128 - ROT]], 1)


def reorder_kernel(places, x_ref, o_ref):
    size = x_ref.shape[1] // len(places)
    for i, place in enumerate(places):
        o_ref[:, i * size : (i + 1) * size] = x_ref[:, pl.ds(pl.multiple_of(place() * size, size), size)]


def reorder(x, places):
    rows, cols = x.shape
    block = pl.BlockSpec((rows, cols), lambda: (0, 0))
    return call(partial(reorder_kernel, places), (), [block], block, shape(rows, cols, kind=x.dtype), 0, 4 * rows * cols, name="reorder")(x)


def norm_kernel(places, x_ref, gain_ref, first_ref, second_ref, x_out, stat_ref):
    x = x_ref[...].astype(F32)
    mean = jnp.mean(x, -1, keepdims=True)
    center = x - mean
    scale = lax.rsqrt(jnp.mean(center * center, -1, keepdims=True) + EPS)
    size = x_ref.shape[1] // len(places)
    for i, place in enumerate(places):
        at, to = pl.ds(pl.multiple_of(place() * size, size), size), pl.ds(i * size, size)
        part = x_ref[:, at]
        x_out[:, to] = part
        unit = (part.astype(F32) - mean) * scale
        first_ref[:, to] = (unit * gain_ref[0:1, at] + gain_ref[1:2, at]).astype(BF16)
        second_ref[:, to] = (unit * gain_ref[2:3, at] + gain_ref[3:4, at]).astype(BF16)
    lane = lax.broadcasted_iota(jnp.int32, stat_ref.shape, 1)
    stat_ref[...] = jnp.where(lane == 0, mean, scale)


def norms(x, gains, places):
    rows, width = x.shape
    block = pl.BlockSpec((128, width), lambda i: (i, 0))
    return call(
        partial(norm_kernel, places),
        (rows // 128,),
        [block, pl.BlockSpec((8, width), lambda i: (0, 0))],
        [block, block, block, pl.BlockSpec((128, 128), lambda i: (i, 0))],
        [shape(rows, width)] * 3 + [shape(rows, 128, kind=F32)],
        10 * rows * width,
        8 * rows * width,
        name="norms",
    )(x, gains)


def project_kernel(n_ref, w_ref, b_ref, table_ref, q_ref, kv_ref):
    head = q_ref.shape[1]
    for i in range(n_ref.shape[0] // ROWS):
        at = pl.ds(i * ROWS, ROWS)
        out = mul(n_ref[at, :], w_ref[...], NN) + b_ref[:1]
        q_ref[at, :] = turn(out[:, :head], table_ref[at, :], 1.0).astype(BF16)
        kv_ref[at, :head] = turn(out[:, head : 2 * head], table_ref[at, :], 1.0).astype(BF16)
        kv_ref[at, head:] = out[:, 2 * head :].astype(BF16)


def project(n, w, bias, table, heads):
    rows, depth = n.shape
    width = w.shape[1] // heads
    head = width // 3
    return call(
        project_kernel,
        (heads,),
        [
            pl.BlockSpec((rows, depth), lambda h: (0, 0)),
            pl.BlockSpec((depth, width), lambda h: (0, h)),
            pl.BlockSpec((8, width), lambda h: (0, h)),
            pl.BlockSpec((rows, 384), lambda h: (0, 0)),
        ],
        [pl.BlockSpec((rows, head), lambda h: (0, h)), pl.BlockSpec((rows, 2 * head), lambda h: (0, h))],
        [shape(rows, heads * head), shape(rows, heads * 2 * head)],
        2 * rows * depth * w.shape[1],
        2 * (rows * depth + w.size + rows * w.shape[1]),
        name="project",
    )(n, w, wide(bias), table)


def expand_kernel(n_ref, w_ref, b_ref, h_ref, d_ref):
    for i in range(n_ref.shape[0] // ROWS):
        at = pl.ds(i * ROWS, ROWS)
        pre = mul(n_ref[at, :], w_ref[...], NN) + b_ref[:1]
        below = 0.5 + 0.5 * lax.erf(pre * math.sqrt(0.5))
        h_ref[at, :] = (pre * below).astype(BF16)
        d_ref[at, :] = (below + pre * jnp.exp(-0.5 * pre * pre) * (1.0 / math.sqrt(2 * math.pi))).astype(BF16)


def expand(n, w, bias, tile=512):
    rows, depth = n.shape
    cols = w.shape[1]
    out = pl.BlockSpec((rows, tile), lambda j: (0, j))
    return call(
        expand_kernel,
        (cols // tile,),
        [
            pl.BlockSpec((rows, depth), lambda j: (0, 0)),
            pl.BlockSpec((depth, tile), lambda j: (0, j)),
            pl.BlockSpec((8, tile), lambda j: (0, j)),
        ],
        [out, out],
        [shape(rows, cols), shape(rows, cols)],
        2 * rows * depth * cols,
        2 * (rows * depth + w.size + 2 * rows * cols),
        2 * rows * cols,
        name="expand",
    )(n, w, wide(bias))


def attend_kernel(prompt, q_ref, ko, vo, kt, vt, bias_ref, segc_ref, segr_ref, o_ref, stat_ref):
    block = pl.program_id(1)
    tq = q_ref.shape[0]
    first_cont = prompt // tq
    cont = ko.shape[0] - prompt
    q = q_ref[...] * BF16(1.0 / math.sqrt(q_ref.shape[1]))
    rows = lax.broadcasted_iota(jnp.int32, (tq, 1), 0)

    def finish(scores, values):
        top = reduce(jnp.maximum, [jnp.max(s, -1, keepdims=True) for s in scores])
        exps = [jnp.exp(s - top) for s in scores]
        total = sum(jnp.sum(e, -1, keepdims=True) for e in exps)
        out = sum(mul(e.astype(BF16), v, NN) for e, v in zip(exps, values))
        o_ref[...] = (out / total).astype(BF16)
        stat_ref[0] = jnp.transpose(jnp.broadcast_to(top + jnp.log(total), (tq, 128)))[:8]

    @pl.when(block < first_cont)
    def _():
        cols = lax.broadcasted_iota(jnp.int32, (1, prompt), 1)
        own = jnp.where(cols <= rows + block * tq, mul(q, ko[:prompt], NT), -1e30)
        far = mul(q, kt[...], NT) + bias_ref[:1]
        finish([own, far], [vo[:prompt], vt[...]])

    @pl.when(block >= first_cont)
    def _():
        cols = lax.broadcasted_iota(jnp.int32, (1, cont), 1)
        own = mul(q, ko[:prompt], NT)
        read = (cols <= rows + (block - first_cont) * tq) & (segc_ref[:, :1] == segr_ref[:1])
        follow = jnp.where(read, mul(q, ko[prompt:], NT), -1e30)
        far = mul(q, kt[...], NT)
        finish([own, follow, far], [vo[:prompt], vo[prompt:], vt[...]])


def attend(q, kv, kv_far, bias, seg, prompt):
    rows, width = q.shape
    head = HEAD
    heads = width // head
    far = kv_far.shape[0]
    cont = rows - prompt
    tq = ROWS
    first = prompt // tq
    return call(
        partial(attend_kernel, prompt),
        (heads, rows // tq),
        [
            pl.BlockSpec((tq, head), lambda h, b: (b, h)),
            pl.BlockSpec((rows, head), lambda h, b: (0, 2 * h)),
            pl.BlockSpec((rows, head), lambda h, b: (0, 2 * h + 1)),
            pl.BlockSpec((far, head), lambda h, b: (0, 2 * h)),
            pl.BlockSpec((far, head), lambda h, b: (0, 2 * h + 1)),
            pl.BlockSpec((8, far), lambda h, b: (0, 0)),
            pl.BlockSpec((tq, 128), lambda h, b: (jnp.maximum(b - first, 0), 0)),
            pl.BlockSpec((8, cont), lambda h, b: (0, 0)),
        ],
        [pl.BlockSpec((tq, head), lambda h, b: (b, h)), pl.BlockSpec((1, 8, tq), lambda h, b: (h, 0, b))],
        [shape(rows, width), shape(heads, 8, rows, kind=F32)],
        4 * rows * (rows + far) * width,
        2 * (2 * q.size + kv.size + kv_far.size),
        rows * (rows + far) * heads,
        name="attend",
    )(q, kv, kv, kv_far, kv_far, wide(bias), jnp.broadcast_to(seg[prompt:, None], (cont, 128)), wide(seg[prompt:]))


def attend_back_kernel(
    prompt, q_ref, do_ref, o_ref, stat_ref, ko, vo, kt, vt, bias_ref, segc_ref, segr_ref, table_ref,
    dq_ref, own_ref, near_ref, far_ref, acc_k, acc_v,
):
    block = pl.program_id(1)
    tq, head = q_ref.shape
    first_cont = prompt // tq
    scale = 1.0 / math.sqrt(head)
    q = q_ref[...] * BF16(scale)
    do = do_ref[...]
    inner = jnp.sum(do.astype(F32) * o_ref[...].astype(F32), -1, keepdims=True)
    inner = jnp.transpose(jnp.broadcast_to(inner, (tq, 128)))[:1]
    stat = stat_ref[0, :1]
    cols = lax.broadcasted_iota(jnp.int32, (1, tq), 1)

    @pl.when(block == 0)
    def _():
        acc_k[...] = jnp.zeros_like(acc_k)
        acc_v[...] = jnp.zeros_like(acc_v)

    def part(keys, values, at, seen):
        probs = jnp.exp(seen(mul(keys, q, NT)) - stat)
        grads = (probs * (mul(values, do, NT) - inner)).astype(BF16)
        acc_v[at, :] += mul(probs.astype(BF16), do, NN)
        acc_k[at, :] += mul(grads, q, NN)
        return mul(grads, keys, TN)

    def far_parts(total, seen):
        for i in range(kt.shape[0] // prompt):
            at = pl.ds(i * prompt, prompt)
            total += part(kt[at, :], vt[at, :], pl.ds(ko.shape[0] + i * prompt, prompt), partial(seen, at))
        dq_ref[...] = turn(total * scale, table_ref[...], -1.0).astype(BF16)

    @pl.when(block < first_cont)
    def _():
        rows = lax.broadcasted_iota(jnp.int32, (prompt, 1), 0)
        total = part(
            ko[:prompt], vo[:prompt], pl.ds(0, prompt), lambda s: jnp.where(rows <= cols + block * tq, s, -1e30)
        )
        far_parts(total, lambda at, s: s + bias_ref[at, :1])

    @pl.when(block >= first_cont)
    def _():
        cont = ko.shape[0] - prompt
        rows = lax.broadcasted_iota(jnp.int32, (cont, 1), 0)
        total = part(ko[:prompt], vo[:prompt], pl.ds(0, prompt), lambda s: s)
        read = (rows <= cols + (block - first_cont) * tq) & (segc_ref[:, :1] == segr_ref[:1])
        total += part(ko[prompt:], vo[prompt:], pl.ds(prompt, cont), lambda s: jnp.where(read, s, -1e30))
        far_parts(total, lambda at, s: s)

    @pl.when(block == pl.num_programs(1) - 1)
    def _():
        start = 0
        for ref in (own_ref, near_ref, far_ref):
            at = pl.ds(start, ref.shape[0])
            ref[:, :head] = acc_k[at, :].astype(ref.dtype)
            ref[:, head:] = acc_v[at, :].astype(ref.dtype)
            start += ref.shape[0]


def attend_back(q, do, o, stat, kv, kv_far, bias, seg, prompt, table):
    rows, width = q.shape
    head = HEAD
    heads = width // head
    far = kv_far.shape[0]
    cont = rows - prompt
    tq = ROWS
    first = prompt // tq
    row = pl.BlockSpec((tq, head), lambda h, b: (b, h))

    def column(n, odd):
        return pl.BlockSpec((n, head), lambda h, b: (0, 2 * h + odd))

    def pair(n):
        return pl.BlockSpec((n, 2 * head), lambda h, b: (0, h))

    return call(
        partial(attend_back_kernel, prompt),
        (heads, rows // tq),
        [
            row,
            row,
            row,
            pl.BlockSpec((1, 8, tq), lambda h, b: (h, 0, b)),
            column(rows, 0),
            column(rows, 1),
            column(far, 0),
            column(far, 1),
            pl.BlockSpec((far, 128), lambda h, b: (0, 0)),
            pl.BlockSpec((cont, 128), lambda h, b: (0, 0)),
            pl.BlockSpec((8, tq), lambda h, b: (0, jnp.maximum(b - first, 0))),
            pl.BlockSpec((tq, 384), lambda h, b: (b, 0)),
        ],
        [row, pair(rows), pair(prompt), pair(far - prompt)],
        [
            shape(rows, width),
            shape(rows, 2 * width, kind=F32),
            shape(prompt, 2 * width),
            shape(far - prompt, 2 * width),
        ],
        10 * rows * (rows + far) * width,
        2 * (4 * q.size + 4 * kv.size + 2 * kv_far.size),
        rows * (rows + far) * heads,
        [pltpu.VMEM((rows + far, head), F32), pltpu.VMEM((rows + far, head), F32)],
        name="attend_back",
    )(
        q,
        do,
        o,
        stat,
        kv,
        kv,
        kv_far,
        kv_far,
        jnp.broadcast_to(bias[:, None], (far, 128)),
        jnp.broadcast_to(seg[prompt:, None], (cont, 128)),
        wide(seg[prompt:]),
        table,
    )


def mixed_kernel(a_ref, h_ref, wa_ref, wh_ref, o_ref):
    for i in range(a_ref.shape[0] // ROWS):
        at = pl.ds(i * ROWS, ROWS)
        o_ref[at, :] = (mul(a_ref[at, :], wa_ref[...], NT) + mul(h_ref[at, :], wh_ref[...], NT)).astype(BF16)


def mixed_sum(attended, activated, w_out, w_contract, tile=512):
    rows = attended.shape[0]
    deep, deeper = attended.shape[1], activated.shape[1]
    width = w_out.shape[0]
    return call(
        mixed_kernel,
        (width // tile,),
        [
            pl.BlockSpec((rows, deep), lambda j: (0, 0)),
            pl.BlockSpec((rows, deeper), lambda j: (0, 0)),
            pl.BlockSpec((tile, deep), lambda j: (j, 0)),
            pl.BlockSpec((tile, deeper), lambda j: (j, 0)),
        ],
        pl.BlockSpec((rows, tile), lambda j: (0, j)),
        shape(rows, width),
        2 * rows * width * (deep + deeper),
        2 * (rows + width) * (deep + deeper) + 2 * rows * width,
        name="mixed_sum",
    )(attended, activated, w_out, w_contract)


def attended_grad_kernel(g_ref, w_ref, o_ref):
    for i in range(g_ref.shape[0] // ROWS):
        at = pl.ds(i * ROWS, ROWS)
        o_ref[at, :] = mul(g_ref[at, :], w_ref[...], NN).astype(BF16)


def attended_grads(g, w, tile=256):
    rows, depth = g.shape
    cols = w.shape[1]
    return call(
        attended_grad_kernel,
        (cols // tile,),
        [pl.BlockSpec((rows, depth), lambda j: (0, 0)), pl.BlockSpec((depth, tile), lambda j: (0, j))],
        pl.BlockSpec((rows, tile), lambda j: (0, j)),
        shape(rows, cols),
        2 * rows * depth * cols,
        2 * (rows * depth + w.size + rows * cols),
        name="attended_grads",
    )(g, w)


def hidden_grad_kernel(g_ref, w_ref, d_ref, gp_ref, sum_ref):
    total = 0.0
    for i in range(g_ref.shape[0] // ROWS):
        at = pl.ds(i * ROWS, ROWS)
        grad = (mul(g_ref[at, :], w_ref[...], NN) * d_ref[at, :].astype(F32)).astype(BF16)
        gp_ref[at, :] = grad
        total += jnp.sum(grad.astype(F32), 0, keepdims=True)
    sum_ref[...] = jnp.broadcast_to(total, sum_ref.shape)


def hidden_grads(g, w, slope, tile=512):
    rows, depth = g.shape
    cols = w.shape[1]
    tall = pl.BlockSpec((rows, tile), lambda j: (0, j))
    return call(
        hidden_grad_kernel,
        (cols // tile,),
        [pl.BlockSpec((rows, depth), lambda j: (0, 0)), pl.BlockSpec((depth, tile), lambda j: (0, j)), tall],
        [tall, pl.BlockSpec((8, tile), lambda j: (0, j))],
        [shape(rows, cols), shape(8, cols, kind=F32)],
        2 * rows * depth * cols,
        2 * (rows * depth + w.size + 2 * rows * cols),
        name="hidden_grads",
    )(g, w, slope)


def pack_kernel(prompt_blocks, q_ref, own_ref, near_ref, far_ref, table_ref, o_ref, sum_ref):
    block = pl.program_id(1)
    head = q_ref.shape[1]
    theirs = near_ref[...].astype(F32) + far_ref[...].astype(F32)
    both = own_ref[...] + jnp.where(block < prompt_blocks, theirs, 0.0)
    out = [q_ref[...], turn(both[:, :head], table_ref[...], -1.0).astype(BF16), both[:, head:].astype(BF16)]

    @pl.when(block == 0)
    def _():
        sum_ref[...] = jnp.zeros_like(sum_ref)

    for i, part in enumerate(out):
        o_ref[:, i * head : (i + 1) * head] = part
        sum_ref[:, i * head : (i + 1) * head] += jnp.sum(part.astype(F32), 0, keepdims=True)


def pack(dq, own, near, far, table, prompt):
    rows, width = dq.shape
    head = HEAD
    heads = width // head
    tq = ROWS
    blocks = prompt // tq
    theirs = pl.BlockSpec((tq, 2 * head), lambda h, b: (jnp.minimum(b, blocks - 1), h))
    return call(
        partial(pack_kernel, blocks),
        (heads, rows // tq),
        [
            pl.BlockSpec((tq, head), lambda h, b: (b, h)),
            pl.BlockSpec((tq, 2 * head), lambda h, b: (b, h)),
            theirs,
            theirs,
            pl.BlockSpec((tq, 384), lambda h, b: (b, 0)),
        ],
        [pl.BlockSpec((tq, 3 * head), lambda h, b: (b, h)), pl.BlockSpec((8, 3 * head), lambda h, b: (0, h))],
        [shape(rows, 3 * width), shape(8, 3 * width, kind=F32)],
        10 * rows * width,
        16 * rows * width,
        name="pack",
    )(dq, own, near, far, table)


def unit_grad_kernel(gp_ref, gh_ref, wa_ref, we_ref, x_ref, stat_ref, gain_ref, e_ref, sum_ref):
    sums = [0.0] * 4
    for i in range(gp_ref.shape[0] // ROWS):
        at = pl.ds(i * ROWS, ROWS)
        first = mul(gp_ref[at, :], wa_ref[...], NT)
        second = mul(gh_ref[at, :], we_ref[...], NT)
        e_ref[at, :] = (first * gain_ref[0:1] + second * gain_ref[2:3]).astype(BF16)
        unit = (x_ref[at, :].astype(F32) - stat_ref[at, 0:1]) * stat_ref[at, 1:2]
        for j, v in enumerate((first * unit, first, second * unit, second)):
            sums[j] += jnp.sum(v, 0, keepdims=True)
    for j in range(4):
        sum_ref[j : j + 1] = sums[j]
    sum_ref[4:] = jnp.zeros_like(sum_ref[4:])


def unit_grads(gp, gh, w_attend, w_expand, x, stat, gains, tile=512):
    rows, width = x.shape
    deep, deeper = gp.shape[1], gh.shape[1]
    col = pl.BlockSpec((rows, tile), lambda j: (0, j))
    row = pl.BlockSpec((8, tile), lambda j: (0, j))
    return call(
        unit_grad_kernel,
        (width // tile,),
        [
            pl.BlockSpec((rows, deep), lambda j: (0, 0)),
            pl.BlockSpec((rows, deeper), lambda j: (0, 0)),
            pl.BlockSpec((tile, deep), lambda j: (j, 0)),
            pl.BlockSpec((tile, deeper), lambda j: (j, 0)),
            col,
            pl.BlockSpec((rows, 128), lambda j: (0, 0)),
            row,
        ],
        [col, row],
        [shape(rows, width), shape(8, width, kind=F32)],
        2 * rows * width * (deep + deeper),
        2 * (rows + width) * (deep + deeper) + 4 * rows * width,
        name="unit_grads",
    )(gp, gh, w_attend, w_expand, x, stat, gains)


def far_kernel(a_ref, b_ref, o_ref):
    for i in range(o_ref.shape[0] // ROWS):
        o_ref[pl.ds(i * ROWS, ROWS), :] = mul(a_ref[:, pl.ds(i * ROWS, ROWS)], b_ref[...], TN).astype(BF16)


def far_product(a, b, tile=512):
    tokens, width = a.shape
    half = width // 2
    cols = b.shape[1]
    return call(
        far_kernel,
        (cols // tile,),
        [pl.BlockSpec((tokens, half), lambda j: (0, 1)), pl.BlockSpec((tokens, tile), lambda j: (0, j))],
        pl.BlockSpec((half, tile), lambda j: (0, j)),
        shape(half, cols),
        2 * tokens * half * cols,
        2 * (tokens * half + tokens * cols + half * cols),
        name="far_product",
    )(a, b)


def near_kernel(a_ref, b_ref, r_ref, *outs):
    size = a_ref.shape[1] // len(outs)
    for i, out in enumerate(outs):
        at = pl.ds(i * size, size)
        out[...] = (mul(a_ref[:, at], b_ref[...], TN) + r_ref[at, :].astype(F32)).astype(out.dtype)


def near_product(a, b, received, tile=512):
    tokens, width = a.shape
    half = width // 2
    cols = b.shape[1]
    size = half // 4
    out = pl.BlockSpec((size, tile), lambda j: (0, j))
    return call(
        near_kernel,
        (cols // tile,),
        [
            pl.BlockSpec((tokens, half), lambda j: (0, 0)),
            pl.BlockSpec((tokens, tile), lambda j: (0, j)),
            pl.BlockSpec((half, tile), lambda j: (0, j)),
        ],
        [out] * 4,
        [shape(size, cols, kind=F32)] + [shape(size, cols)] * 3,
        2 * tokens * half * cols,
        2 * (tokens * half + tokens * cols + 2 * half * cols),
        name="near_product",
    )(a, b, received)


class Hops:
    def __init__(self, send, recv):
        self.send, self.recv, self.made = send, recv, []
        f, c, t = (lax.axis_index(a) for a in ("fsdp", "ctx", "tp"))
        ring = lax.axis_size("tp")
        self.to = {
            "x": {"fsdp": 1 - f},
            "y": {"ctx": (c + 2) % 4},
            "core": {"ctx": c + 1 - 2 * (c % 2)},
            "up": {"tp": (t + 1) % ring},
        }
        self.back = {"tp": (t + ring - 1) % ring}

    def greet(self):
        barrier = pltpu.get_barrier_semaphore()
        near = [*self.to.values(), self.back]
        for device in near:
            pl.semaphore_signal(barrier, inc=1, device_id=device, device_id_type=pl.DeviceIdType.MESH)
        pl.semaphore_wait(barrier, len(near))

    def copy(self, way, src, dst):
        i = len(self.made)
        self.made.append(
            pltpu.make_async_remote_copy(
                src,
                dst,
                self.send.at[i],
                self.recv.at[i],
                device_id=self.to[way],
                device_id_type=pl.DeviceIdType.MESH,
            )
        )
        return self.made[-1]

    def end(self):
        for copy in self.made:
            copy.wait_send()


class Block:
    def __init__(self, hops, part, whole, halves=1):
        size = part.shape[0]
        half, piece = size // 2, size // halves

        def at(slot, start=0, rows=size):
            return whole.at[pl.ds(slot * size + start, rows)]

        self.first = [
            [
                hops.copy(way, part.at[pl.ds(i * piece, piece)], at(slot, i * piece, piece))
                for way, slot in (("x", 1), ("y", 2))
            ]
            for i in range(halves)
        ]
        self.corner = [
            hops.copy("x", at(2, 0, half), at(3, 0, half)),
            hops.copy("y", at(1, half, half), at(3, half, half)),
        ]
        self.core = [hops.copy("core", part if slot == 0 else at(slot), at(4 + slot)) for slot in range(4)]


def start(copies):
    for copy in copies:
        copy.start()


def arrive(copies):
    for copy in copies:
        copy.wait_recv()


def table_kernel(pos_ref, freq_ref, o_ref):
    angle = pos_ref[...] * freq_ref[:1]
    c, s = jnp.cos(angle), jnp.sin(angle)
    lane = lax.broadcasted_iota(jnp.int32, angle.shape, 1)
    half = ROT // 2
    o_ref[:, :128] = jnp.where(lane < ROT, c, 1.0)
    o_ref[:, 128:256] = jnp.where(lane < half, -s, 0.0)
    o_ref[:, 256:] = jnp.where((lane >= half) & (lane < ROT), s, 0.0)


def norm_block_kernel(x_ref, gain_ref, first_ref, second_ref, stat_ref):
    x = x_ref[...].astype(F32)
    mean = jnp.mean(x, -1, keepdims=True)
    center = x - mean
    scale = lax.rsqrt(jnp.mean(center * center, -1, keepdims=True) + EPS)
    unit = center * scale
    first_ref[...] = (unit * gain_ref[0:1] + gain_ref[1:2]).astype(BF16)
    second_ref[...] = (unit * gain_ref[2:3] + gain_ref[3:4]).astype(BF16)
    lane = lax.broadcasted_iota(jnp.int32, stat_ref.shape, 1)
    stat_ref[...] = jnp.where(lane == 0, mean, scale)


def project_block_kernel(n_ref, w_ref, b_ref, table_ref, q_ref, kv_ref):
    head = q_ref.shape[1]
    out = mul(n_ref[...], w_ref[...], NN) + b_ref[:1]
    q_ref[...] = turn(out[:, :head], table_ref[...], 1.0).astype(BF16)
    kv_ref[:, :head] = turn(out[:, head : 2 * head], table_ref[...], 1.0).astype(BF16)
    kv_ref[:, head:] = out[:, 2 * head :].astype(BF16)


def expand_block_kernel(n_ref, w_ref, b_ref, h_ref, d_ref):
    pre = mul(n_ref[...], w_ref[...], NN) + b_ref[:1]
    below = 0.5 + 0.5 * lax.erf(pre * math.sqrt(0.5))
    h_ref[...] = (pre * below).astype(BF16)
    d_ref[...] = (below + pre * jnp.exp(-0.5 * pre * pre) * (1.0 / math.sqrt(2 * math.pi))).astype(BF16)


def forward_kernel(places, prompt, *refs):
    (
        x_ref, g_ref, wa, we, wo, wc, gain_ref, bias_a, bias_e, far_bias, segc, segr, pos_ref, freq_ref,
        rows_in, rows_grad, gains, attend_all, expand_all, output_all, contract_all,
        first, second, stat, table, queries, pairs, pairs_far, activated, slope, attended, row_sums, mixed,
        send, recv, local, held_x, held_g, held_gains, *held,
    ) = refs
    hops = Hops(send, recv)
    t, ring = lax.axis_index("tp"), lax.axis_size("tp")
    rows, width = x_ref.shape
    total = rows * ring
    block = width // len(places)
    chunk = rows // 2

    here = pl.ds(t * rows, rows)
    moves = [(x_ref, held_x, rows_in.at[here]), (gain_ref, held_gains, gains), (g_ref, held_g, rows_grad.at[here])]
    loads, stores, count = [], [], 0
    for src, mid, dst in moves:
        loads.append([])
        for i, place in enumerate(places):
            at = pl.ds(pl.multiple_of(place() * block, block), block)
            loads[-1].append(pltpu.make_async_copy(src.at[:, at], mid.at[:, pl.ds(i * block, block)], local.at[count]))
            count += 1
        stores.append(pltpu.make_async_copy(mid, dst, local.at[count]))
        count += 1
    for src, mid, whole in zip((wa, we, wo, wc), held, (attend_all, expand_all, output_all, contract_all)):
        loads.append([pltpu.make_async_copy(src, mid, local.at[count])])
        stores.append(pltpu.make_async_copy(mid, whole.at[pl.ds(0, src.shape[0])], local.at[count + 1]))
        count += 2

    def rings(ref, held_rows):
        made = {}
        for step in range(ring - 1):
            for half in range(2):
                at = ref.at[pl.ds(((t + ring - step) % ring) * rows + half * chunk, chunk)]
                src = held_rows.at[pl.ds(half * chunk, chunk)] if step == 0 else at
                made[step, half] = hops.copy("up", src, at)
        return made

    ring_x, ring_g = rings(rows_in, held_x), rings(rows_grad, held_g)
    a, e, o = (Block(hops, part, whole) for part, whole in ((wa, attend_all), (we, expand_all), (wo, output_all)))
    c = Block(hops, wc, contract_all, 2)
    own_pairs = pairs.at[pl.ds(0, prompt)]
    far = [pairs_far.at[pl.ds(i * prompt, prompt)] for i in range(3)]
    pair_y, pair_core = hops.copy("y", own_pairs, far[0]), hops.copy("core", own_pairs, far[1])
    pair_corner = hops.copy("core", far[0], far[2])

    def forward(copies, step, half):
        arrive([copies[step, half]])
        if step < ring - 2:
            start([copies[step + 1, half]])

    head = HEAD
    heads = queries.shape[1] // head

    def span(step):
        return pl.ds(((t + ring - step) % ring) * rows, rows)

    def norm(step):
        tile = 128
        row = pl.BlockSpec((tile, width), lambda i: (i, 0))
        pltpu.emit_pipeline(
            norm_block_kernel,
            grid=(rows // tile,),
            in_specs=[row, pl.BlockSpec((8, width), lambda i: (0, 0))],
            out_specs=[row, row, pl.BlockSpec((tile, 128), lambda i: (i, 0))],
        )(rows_in.at[span(step)], gains, first.at[span(step)], second.at[span(step)], stat.at[span(step)])

    def project(step):
        pltpu.emit_pipeline(
            project_block_kernel,
            grid=(heads,),
            in_specs=[
                pl.BlockSpec((rows, width), lambda h: (0, 0)),
                pl.BlockSpec((width, 3 * head), lambda h: (0, h)),
                pl.BlockSpec((8, 3 * head), lambda h: (0, h)),
                pl.BlockSpec((rows, 384), lambda h: (0, 0)),
            ],
            out_specs=[pl.BlockSpec((rows, head), lambda h: (0, h)), pl.BlockSpec((rows, 2 * head), lambda h: (0, h))],
        )(first.at[span(step)], attend_all, bias_a, table.at[span(step)], queries.at[span(step)], pairs.at[span(step)])

    def expand(step):
        tile = 512
        out = pl.BlockSpec((rows, tile), lambda j: (0, j))
        pltpu.emit_pipeline(
            expand_block_kernel,
            grid=(expand_all.shape[1] // tile,),
            in_specs=[
                pl.BlockSpec((rows, width), lambda j: (0, 0)),
                pl.BlockSpec((width, tile), lambda j: (0, j)),
                pl.BlockSpec((8, tile), lambda j: (0, j)),
            ],
            out_specs=[out, out],
        )(second.at[span(step)], expand_all, bias_e, activated.at[span(step)], slope.at[span(step)])

    for load in loads:
        start(load)
    hops.greet()
    start(a.first[0])
    start([a.core[0]])
    for i, (load, store) in enumerate(zip(loads, stores)):
        for copy in load:
            copy.wait()
        store.start()
        if i == 0:
            start([ring_x[0, 0], ring_x[0, 1], e.core[0]])
    for store in stores:
        store.wait()
    pltpu.emit_pipeline(
        table_kernel,
        grid=(total // rows,),
        in_specs=[pl.BlockSpec((rows, 128), lambda i: (i, 0)), pl.BlockSpec((8, 128), lambda i: (0, 0))],
        out_specs=[pl.BlockSpec((rows, 384), lambda i: (i, 0))],
    )(pos_ref, freq_ref, table)
    norm(0)
    forward(ring_x, 0, 0)
    start(e.first[0])
    arrive(a.first[0])
    start(a.corner + a.core[1:3])
    forward(ring_x, 0, 1)
    norm(1)
    forward(ring_x, 1, 0)
    arrive(a.corner)
    start([a.core[3]])
    arrive(e.first[0])
    start(e.corner + e.core[1:3] + o.first[0] + [o.core[0]] + c.first[0] + [c.core[0]])
    forward(ring_x, 1, 1)
    start([ring_g[0, 0], ring_g[0, 1]])
    norm(2)
    arrive(a.core)
    project(0)
    forward(ring_x, 2, 0)
    arrive(e.corner)
    start([e.core[3]])
    project(1)
    project(2)
    arrive(o.first[0])
    start(o.core[1:3])
    forward(ring_x, 2, 1)
    norm(3)
    project(3)
    start([pair_y, pair_core] + o.corner)
    arrive(e.core)
    expand(0)
    forward(ring_g, 0, 0)
    arrive(c.first[0])
    start(c.first[1])
    expand(1)
    arrive(o.corner)
    start([o.core[3]])
    expand(2)
    forward(ring_g, 0, 1)
    expand(3)
    arrive([pair_y])
    start([pair_corner])
    arrive(c.first[1])
    start(c.corner + c.core[1:3])
    arrive([pair_core, pair_corner])

    def attend_step(*args):
        step = pl.program_id(0) * pl.num_programs(1) + pl.program_id(1)
        pl.when(step == 2)(lambda: forward(ring_g, 1, 0))
        pl.when(step == 7)(lambda: forward(ring_g, 1, 1))
        attend_kernel(prompt, *args)

    tq = ROWS
    cont = total - prompt
    n_far = far_bias.shape[1]
    first_cont = prompt // tq
    pltpu.emit_pipeline(
        attend_step,
        grid=(heads, total // tq),
        in_specs=[
            pl.BlockSpec((tq, head), lambda h, b: (b, h)),
            pl.BlockSpec((total, head), lambda h, b: (0, 2 * h)),
            pl.BlockSpec((total, head), lambda h, b: (0, 2 * h + 1)),
            pl.BlockSpec((n_far, head), lambda h, b: (0, 2 * h)),
            pl.BlockSpec((n_far, head), lambda h, b: (0, 2 * h + 1)),
            pl.BlockSpec((8, n_far), lambda h, b: (0, 0)),
            pl.BlockSpec((tq, 128), lambda h, b: (jnp.maximum(b - first_cont, 0), 0)),
            pl.BlockSpec((8, cont), lambda h, b: (0, 0)),
        ],
        out_specs=[pl.BlockSpec((tq, head), lambda h, b: (b, h)), pl.BlockSpec((1, 8, tq), lambda h, b: (h, 0, b))],
    )(queries, pairs, pairs, pairs_far, pairs_far, far_bias, segc, segr, attended, row_sums)

    forward(ring_g, 2, 0)
    arrive(c.corner)
    start([c.core[3]])
    arrive(o.core + c.core)
    tile = 512
    pltpu.emit_pipeline(
        mixed_kernel,
        grid=(width // tile,),
        in_specs=[
            pl.BlockSpec((total, attended.shape[1]), lambda j: (0, 0)),
            pl.BlockSpec((total, activated.shape[1]), lambda j: (0, 0)),
            pl.BlockSpec((tile, attended.shape[1]), lambda j: (j, 0)),
            pl.BlockSpec((tile, activated.shape[1]), lambda j: (j, 0)),
        ],
        out_specs=[pl.BlockSpec((total, tile), lambda j: (0, j))],
    )(attended, activated, output_all, contract_all, mixed)
    forward(ring_g, 2, 1)
    hops.end()


def forward_pass(places, prompt, heads, x, g, weights, gains, bias_a, bias_e, far_bias, seg, where_at):
    ring = lax.axis_size("tp")
    rows, width = x.shape
    total = ring * rows
    wa, we, wo, wc = weights
    head = HEAD
    hidden = we.shape[1]
    cont = total - prompt
    far = far_bias.shape[0]
    half = ROT // 2
    lanes = jnp.arange(128) % half
    freq = jnp.exp(lanes.astype(F32) * (-2.0 * math.log(10000.0) / ROT))
    inputs = [
        x, g, wa, we, wo, wc, gains, wide(bias_a), wide(bias_e), wide(far_bias),
        jnp.broadcast_to(seg[prompt:, None], (cont, 128)), wide(seg[prompt:]),
        jnp.broadcast_to(where_at.astype(F32)[:, None], (total, 128)), wide(freq),
    ]
    outs = [
        shape(total, width), shape(total, width), shape(*gains.shape, kind=F32),
        *(shape(8 * w.shape[0], w.shape[1]) for w in (wa, we, wo, wc)),
        shape(total, width), shape(total, width), shape(total, 128, kind=F32), shape(total, 384, kind=F32),
        shape(total, heads * head), shape(total, 2 * heads * head), shape(3 * prompt, 2 * heads * head),
        shape(total, hidden), shape(total, hidden), shape(total, heads * head), shape(heads, 8, total, kind=F32),
        shape(total, width),
    ]
    copies = 4 * (ring - 1) + 34 + 3
    ref = pl.BlockSpec(memory_space=pl.ANY)
    return pl.pallas_call(
        partial(forward_kernel, places, prompt),
        in_specs=[ref] * len(inputs),
        out_specs=[ref] * len(outs),
        out_shape=outs,
        scratch_shapes=[
            pltpu.SemaphoreType.DMA((copies,)),
            pltpu.SemaphoreType.DMA((copies,)),
            pltpu.SemaphoreType.DMA((3 * len(places) + 11,)),
            pltpu.VMEM(x.shape, BF16),
            pltpu.VMEM(g.shape, BF16),
            pltpu.VMEM(gains.shape, F32),
            *(pltpu.VMEM(w.shape, BF16) for w in weights),
        ],
        compiler_params=pltpu.CompilerParams(collective_id=0, has_side_effects=True, vmem_limit_bytes=56 * 2**20),
        cost_estimate=pl.CostEstimate(flops=40 * 10**9, bytes_accessed=200 * 2**20, transcendentals=10**7),
        name="forward_pass",
    )(*inputs)


class SquareLinks:
    order = ((0, 0, 0), (1, 0, 0), (0, 1, 0), (1, 1, 0), (0, 0, 1), (1, 0, 1), (0, 1, 1), (1, 1, 1))

    def x_hop(self, v):
        return lax.ppermute(v, "fsdp", [(0, 1), (1, 0)])

    def y_hop(self, v):
        return lax.ppermute(v, "ctx", [(0, 2), (2, 0), (1, 3), (3, 1)])

    def core_hop(self, v):
        return lax.ppermute(v, "ctx", [(0, 1), (1, 0), (2, 3), (3, 2)])

    def place(self, bits):
        f, c = lax.axis_index("fsdp"), lax.axis_index("ctx")
        a, b, d = bits
        return ((f ^ a) * 2 + ((c // 2) ^ b)) * 2 + ((c % 2) ^ d)

    def spot(self, p):
        f, c = lax.axis_index("fsdp"), lax.axis_index("ctx")
        a, b, d = f ^ (p // 4), (c // 2) ^ (p // 2 % 2), (c % 2) ^ (p % 2)
        return d * 4 + b * 2 + a

    def places(self):
        return [partial(self.place, bits) for bits in self.order]

    def spots(self):
        return [partial(self.spot, p) for p in range(8)]

    def to_relative(self, v):
        return reorder(v, self.places())

    def to_whole(self, v):
        return reorder(v, self.spots())


    def scatter_far(self, left, right):
        return self.core_hop(far_product(left, right))

    def scatter_near(self, left, right, far):
        return near_product(left, right, far)

    def scatter_end(self, own, to_x, to_y, corner):
        half = corner.shape[0] // 2
        via_x, via_y = self.x_hop(corner[:half]), self.y_hop(corner[half:])
        to_y = jnp.concatenate([to_y[:half] + via_x, to_y[half:]], 0)
        to_x = jnp.concatenate([to_x[:half], to_x[half:] + via_y], 0)
        return own + self.x_hop(to_x).astype(F32) + self.y_hop(to_y).astype(F32)

    def others(self, v):
        c = lax.axis_index("ctx")
        return jnp.stack([v[c ^ bits] for bits in (2, 1, 3)])

    def scatter_others(self, near, far):
        theirs = self.core_hop(far)
        rows = near.shape[0]
        return theirs, lambda token: self.y_hop(after(theirs, token)[rows:] + near)

    def sum_rows(self, v):
        v = v + self.core_hop(v)
        v = v + self.x_hop(v)
        return v + self.y_hop(v)


class AnyLinks:
    def places(self):
        return [lambda: 0]

    def spots(self):
        return [lambda: 0]

    def to_whole(self, v):
        return v

    def gather(self, block):
        return lax.all_gather(block, ("fsdp", "ctx"), axis=0, tiled=True)

    def scatter_far(self, left, right):
        return None

    def scatter_near(self, left, right, far):
        return (jnp.einsum("tc,tk->ck", left, right, preferred_element_type=F32).astype(BF16),)

    def scatter_end(self, whole):
        return lax.psum_scatter(whole, ("fsdp", "ctx"), scatter_dimension=0, tiled=True).astype(F32)

    def others(self, v):
        return jnp.roll(v, -lax.axis_index("ctx"), 0)[1:]

    def gather_others(self, block):
        rows = block.shape[0]
        whole = lax.all_gather(block, "ctx", axis=0, tiled=True)
        return jnp.roll(whole, -rows * lax.axis_index("ctx"), 0)[rows:]

    def scatter_others(self, near, far):
        rows = near.shape[0]
        whole = jnp.concatenate([jnp.zeros_like(near), near, far], 0)
        whole = jnp.roll(whole, rows * lax.axis_index("ctx"), 0)
        theirs = lax.psum_scatter(whole, "ctx", scatter_dimension=0, tiled=True)
        return theirs, lambda token: jnp.zeros_like(theirs)

    def sum_rows(self, v):
        return lax.psum(v, ("fsdp", "ctx"))


def sum_tp(v):
    size = lax.axis_size("tp")
    if size & (size - 1):
        return lax.psum(v, "tp")
    step = 1
    while step < size:
        v = v + lax.ppermute(v, "tp", [(i, i ^ step) for i in range(size)])
        step *= 2
    return v


def output_kernel(spots, x_ref, m_ref, b_ref, o_ref):
    size = x_ref.shape[1] // len(spots)
    for i, spot in enumerate(spots):
        at, to = pl.ds(pl.multiple_of(spot() * size, size), size), pl.ds(i * size, size)
        o_ref[:, to] = (x_ref[:, to].astype(F32) + m_ref[:, at].astype(F32) + b_ref[:1, to]).astype(BF16)


def output_rows(x, mixed, bias, spots):
    rows, width = x.shape
    block = pl.BlockSpec((64, width), lambda i: (i, 0))
    return call(
        partial(output_kernel, spots),
        (rows // 64,),
        [block, block, pl.BlockSpec((8, width), lambda i: (0, 0))],
        block,
        shape(rows, width),
        2 * x.size,
        6 * x.size,
        name="output_rows",
    )(x, mixed, wide(bias))


def end_kernel(spots, x_ref, g_ref, e_ref, o_ref, e_whole):
    size = x_ref.shape[1] // len(spots)
    for i, spot in enumerate(spots):
        e_whole[:, i * size : (i + 1) * size] = e_ref[:, pl.ds(pl.multiple_of(spot() * size, size), size)].astype(F32)
    x = x_ref[...].astype(F32)
    center = x - jnp.mean(x, -1, keepdims=True)
    scale = lax.rsqrt(jnp.mean(center * center, -1, keepdims=True) + EPS)
    unit = center * scale
    e = e_whole[...]
    rest = e - jnp.mean(e, -1, keepdims=True) - unit * jnp.mean(e * unit, -1, keepdims=True)
    o_ref[...] = g_ref[...].astype(F32) + scale * rest


def input_grads(x, g, e, spots):
    rows, width = x.shape
    block = pl.BlockSpec((64, width), lambda i: (i, 0))
    return call(
        partial(end_kernel, spots),
        (rows // 64,),
        [block] * 3,
        block,
        shape(rows, width, kind=F32),
        15 * x.size,
        10 * x.size,
        scratch=[pltpu.VMEM((64, width), F32)],
        name="input_grads",
    )(x, g, e)


def shards(
    stream_in,
    stream_grad,
    segments,
    positions,
    first_gain,
    first_shift,
    second_gain,
    second_shift,
    attend_weight,
    attend_bias,
    output_weight,
    expand_weight,
    expand_bias,
    contract_weight,
    output_bias,
):
    square = (lax.axis_size("fsdp"), lax.axis_size("ctx"), lax.axis_size("tp")) == (2, 4, 4)
    links = SquareLinks() if square else AnyLinks()
    local_rows = attend_weight.shape[0]
    heads = attend_bias.shape[0]
    holders = lax.axis_size("ctx")
    holder = lax.axis_index("ctx")
    prompt = PROMPT // holders

    row_count = stream_in.shape[0] * lax.axis_size("tp")
    gains = jnp.concatenate([jnp.stack([first_gain, first_shift, second_gain, second_shift]), jnp.zeros((4, first_gain.shape[0]), F32)])
    row_pos = lax.dynamic_slice_in_dim(positions, holder * row_count, row_count)
    row_seg = lax.dynamic_slice_in_dim(segments, holder * row_count, row_count)
    starts = positions.reshape(holders, row_count)[:, 0]
    bias = jnp.where(links.others(starts) < row_pos[0], 0.0, -1e30).astype(F32)
    bias = jnp.repeat(bias, prompt)
    weights = (attend_weight.reshape(local_rows, -1), expand_weight, output_weight, contract_weight)

    if square:
        (
            rows_in, rows_grad, own_gains, attend_all, expand_all, output_all, contract_all, first_norm, second_norm,
            stat, table, queries, pairs, pairs_far, activated, slope, attended, row_sums, mixed,
        ) = forward_pass(
            links.places(), prompt, heads, stream_in, stream_grad, weights, gains, attend_bias.reshape(-1), expand_bias,
            bias, row_seg, row_pos,
        )
    else:
        own_gains = gains
        rows_in, rows_grad = (lax.all_gather(v, "tp", axis=0, tiled=True) for v in (stream_in, stream_grad))
        attend_all, expand_all, output_all, contract_all = (links.gather(v) for v in weights)
        table = turn_table(row_pos)
        first_norm, second_norm, rows_in, stat = norms(rows_in, gains, links.places())
        queries, pairs = project(first_norm, attend_all, attend_bias.reshape(-1), table, heads)
        pairs_far = links.gather_others(pairs[:prompt])
        activated, slope = expand(second_norm, expand_all, expand_bias)
        attended, row_sums = attend(queries, pairs, pairs_far, bias, row_seg, prompt)
        mixed = mixed_sum(attended, activated, output_all, contract_all)
    branches = lax.psum_scatter(mixed, "tp", scatter_dimension=0, tiled=True)

    grad_attended = attended_grads(rows_grad, output_all)
    grad_queries, pair_own, pair_near, pair_far = attend_back(
        queries, grad_attended, attended, row_sums, pairs, pairs_far, bias, row_seg, prompt, table
    )
    core_part, y_part = links.scatter_others(pair_near, pair_far)
    far_c = links.scatter_far(rows_grad, after(activated, pair_own))
    y_part = y_part(pair_own if far_c is None else far_c)
    grad_pre, expand_sums = hidden_grads(after(rows_grad, y_part), contract_all, slope)
    near_c = links.scatter_near(rows_grad, after(activated, grad_pre), far_c)
    grad_flat, attend_sums = pack(grad_queries, after(pair_own, near_c[0]), y_part, core_part, table, prompt)
    grad_unit, vector_parts = unit_grads(grad_flat, grad_pre, attend_all, expand_all, rows_in, stat, own_gains)
    unit_part = lax.psum_scatter(grad_unit, "tp", scatter_dimension=0, tiled=True)

    far_e = links.scatter_far(second_norm, after(grad_pre, grad_unit))
    near_e = links.scatter_near(second_norm, grad_pre, far_e)
    far_a = links.scatter_far(first_norm, after(grad_flat, near_e[0]))
    far_o = links.scatter_far(rows_grad, after(attended, near_e[0]))
    near_a = links.scatter_near(first_norm, grad_flat, far_a)
    near_o = links.scatter_near(rows_grad, after(attended, near_a[0]), far_o)
    contract_weight_grad = links.scatter_end(*near_c)
    expand_weight_grad = links.scatter_end(*near_e)
    attend_weight_grad = links.scatter_end(*near_a).reshape(attend_weight.shape)
    output_weight_grad = links.scatter_end(*near_o)

    bias_sums = links.sum_rows(jnp.concatenate([attend_sums[0], expand_sums[0]]))
    attend_bias_grad = bias_sums[: grad_flat.shape[1]].reshape(attend_bias.shape)
    expand_bias_grad = bias_sums[grad_flat.shape[1] :]
    row_sum = jnp.sum(stream_grad.astype(F32), 0)
    vectors = jnp.concatenate([links.to_whole(vector_parts)[:4], row_sum[None]])
    norm_sums = sum_tp(links.sum_rows(vectors))

    stream_out = output_rows(stream_in, branches, output_bias, links.spots())
    input_grad = input_grads(stream_in, stream_grad, unit_part, links.spots())
    return (
        stream_out,
        input_grad,
        norm_sums[0],
        norm_sums[1],
        norm_sums[2],
        norm_sums[3],
        attend_weight_grad,
        attend_bias_grad,
        output_weight_grad,
        expand_weight_grad,
        expand_bias_grad,
        contract_weight_grad,
        norm_sums[4],
    )


def solution(mesh):
    tokens = P(("fsdp", "ctx", "tp"), None)
    weight = P(("fsdp", "ctx"), "tp")
    heads = P(("fsdp", "ctx"), "tp", None)
    return jax.shard_map(
        shards,
        mesh=mesh,
        in_specs=(
            tokens,
            tokens,
            P("fsdp"),
            P("fsdp"),
            P(),
            P(),
            P(),
            P(),
            heads,
            P("tp", None),
            weight,
            weight,
            P("tp"),
            weight,
            P(),
        ),
        out_specs=(
            tokens,
            tokens,
            P(),
            P(),
            P(),
            P(),
            heads,
            P("tp", None),
            weight,
            weight,
            P("tp"),
            weight,
            P(),
        ),
        check_vma=False,
    )
```

```python
from functools import partial, reduce
import math
from types import SimpleNamespace

import jax
import jax.numpy as jnp
import numpy as np
from jax import lax
from jax.experimental import pallas as pl
from jax.experimental.pallas import tpu as pltpu
from jax.sharding import PartitionSpec as P

ROT = 64
PROMPT = 2048
EPS = 1e-05
F32 = jnp.float32
BF16 = jnp.bfloat16
ROWS = 256
HEAD = 256
NN = (((1,), (0,)), ((), ()))
NT = (((1,), (1,)), ((), ()))
TN = (((0,), (0,)), ((), ()))


def mul(a, b, dims):
    return lax.dot_general(a, b, dims, preferred_element_type=F32)


def call(kernel, grid, in_specs, out_specs, out_shape, flops, moved, exps=0, scratch=(), mib=48, name=None):
    return pl.pallas_call(
        kernel,
        grid=grid,
        in_specs=in_specs,
        out_specs=out_specs,
        out_shape=out_shape,
        scratch_shapes=scratch,
        compiler_params=pltpu.CompilerParams(vmem_limit_bytes=mib * 2**20),
        cost_estimate=pl.CostEstimate(flops=flops, bytes_accessed=moved, transcendentals=exps),
        name=name,
    )


def shape(*dims, kind=BF16):
    return jax.ShapeDtypeStruct(dims, kind)


def wide(row):
    return jnp.broadcast_to(row[None], (8, row.shape[0]))


def turn(v, table, sign):
    head = v[:, :128]
    other = pltpu.roll(head, 96, 1) * table[:, 128:256] + pltpu.roll(head, 32, 1) * table[:, 256:]
    return jnp.concatenate([head * table[:, :128] + sign * other, v[:, 128:]], 1)


def turn_table(where_at):
    half = ROT // 2
    frequency = jnp.exp(jnp.arange(half, dtype=F32) * (-2.0 * math.log(10000.0) / ROT))
    angles = where_at.astype(F32)[:, None] * frequency[None, :]
    c, s = jnp.cos(angles), jnp.sin(angles)
    rows = where_at.shape[0]
    one, none = jnp.ones((rows, 128 - ROT), F32), jnp.zeros((rows, 128 - half), F32)
    return jnp.concatenate([c, c, one, -s, none, none[:, :half], s, none[:, : 128 - ROT]], 1)


def norm_kernel(places, x_ref, gain_ref, first_ref, second_ref, x_out, stat_ref):
    x = x_ref[...].astype(F32)
    mean = jnp.mean(x, -1, keepdims=True)
    center = x - mean
    scale = lax.rsqrt(jnp.mean(center * center, -1, keepdims=True) + EPS)
    size = x_ref.shape[1] // len(places)
    for i, place in enumerate(places):
        at, to = pl.ds(pl.multiple_of(place() * size, size), size), pl.ds(i * size, size)
        part = x_ref[:, at]
        x_out[:, to] = part
        unit = (part.astype(F32) - mean) * scale
        first_ref[:, to] = (unit * gain_ref[0:1, at] + gain_ref[1:2, at]).astype(BF16)
        second_ref[:, to] = (unit * gain_ref[2:3, at] + gain_ref[3:4, at]).astype(BF16)
    lane = lax.broadcasted_iota(jnp.int32, stat_ref.shape, 1)
    stat_ref[...] = jnp.where(lane == 0, mean, scale)


def norms(x, gains, places):
    rows, width = x.shape
    block = pl.BlockSpec((128, width), lambda i: (i, 0))
    return call(
        partial(norm_kernel, places),
        (rows // 128,),
        [block, pl.BlockSpec((8, width), lambda i: (0, 0))],
        [block, block, block, pl.BlockSpec((128, 128), lambda i: (i, 0))],
        [shape(rows, width)] * 3 + [shape(rows, 128, kind=F32)],
        10 * rows * width,
        8 * rows * width,
        name="norms",
    )(x, gains)


def project_kernel(n_ref, w_ref, b_ref, table_ref, q_ref, kv_ref):
    head = q_ref.shape[1]
    for i in range(n_ref.shape[0] // ROWS):
        at = pl.ds(i * ROWS, ROWS)
        out = mul(n_ref[at, :], w_ref[...], NN) + b_ref[:1]
        q_ref[at, :] = turn(out[:, :head], table_ref[at, :], 1.0).astype(BF16)
        kv_ref[at, :head] = turn(out[:, head : 2 * head], table_ref[at, :], 1.0).astype(BF16)
        kv_ref[at, head:] = out[:, 2 * head :].astype(BF16)


def project(n, w, bias, table, heads):
    rows, depth = n.shape
    width = w.shape[1] // heads
    head = width // 3
    return call(
        project_kernel,
        (heads,),
        [
            pl.BlockSpec((rows, depth), lambda h: (0, 0)),
            pl.BlockSpec((depth, width), lambda h: (0, h)),
            pl.BlockSpec((8, width), lambda h: (0, h)),
            pl.BlockSpec((rows, 384), lambda h: (0, 0)),
        ],
        [pl.BlockSpec((rows, head), lambda h: (0, h)), pl.BlockSpec((rows, 2 * head), lambda h: (0, h))],
        [shape(rows, heads * head), shape(rows, heads * 2 * head)],
        2 * rows * depth * w.shape[1],
        2 * (rows * depth + w.size + rows * w.shape[1]),
        name="project",
    )(n, w, wide(bias), table)


def expand_kernel(n_ref, w_ref, b_ref, h_ref, d_ref):
    for i in range(n_ref.shape[0] // ROWS):
        at = pl.ds(i * ROWS, ROWS)
        pre = mul(n_ref[at, :], w_ref[...], NN) + b_ref[:1]
        below = 0.5 + 0.5 * lax.erf(pre * math.sqrt(0.5))
        h_ref[at, :] = (pre * below).astype(BF16)
        d_ref[at, :] = (below + pre * jnp.exp(-0.5 * pre * pre) * (1.0 / math.sqrt(2 * math.pi))).astype(BF16)


def expand(n, w, bias, tile=512):
    rows, depth = n.shape
    cols = w.shape[1]
    out = pl.BlockSpec((rows, tile), lambda j: (0, j))
    return call(
        expand_kernel,
        (cols // tile,),
        [
            pl.BlockSpec((rows, depth), lambda j: (0, 0)),
            pl.BlockSpec((depth, tile), lambda j: (0, j)),
            pl.BlockSpec((8, tile), lambda j: (0, j)),
        ],
        [out, out],
        [shape(rows, cols), shape(rows, cols)],
        2 * rows * depth * cols,
        2 * (rows * depth + w.size + 2 * rows * cols),
        2 * rows * cols,
        name="expand",
    )(n, w, wide(bias))


def attend_block(prompt, block, allow, segc_ref, segr, q_ref, ko, vo, kt, vt, o_ref, stat_ref):
    tq = q_ref.shape[0]
    first_cont = prompt // tq
    cont = ko.shape[0] - prompt
    q = q_ref[...] * BF16(1.0 / math.sqrt(q_ref.shape[1]))
    rows = lax.broadcasted_iota(jnp.int32, (tq, 1), 0)

    def finish(scores, values):
        top = reduce(jnp.maximum, [jnp.max(s, -1, keepdims=True) for s in scores])
        exps = [jnp.exp(s - top) for s in scores]
        total = sum(jnp.sum(e, -1, keepdims=True) for e in exps)
        out = sum(mul(e.astype(BF16), v, NN) for e, v in zip(exps, values))
        o_ref[...] = (out / total).astype(BF16)
        stat_ref[0] = jnp.transpose(jnp.broadcast_to(top + jnp.log(total), (tq, 128)))[:8]

    @pl.when(block < first_cont)
    def _():
        cols = lax.broadcasted_iota(jnp.int32, (1, prompt), 1)
        own = jnp.where(cols <= rows + block * tq, mul(q, ko[:prompt], NT), -1e30)
        spans = [pl.ds(i * prompt, prompt) for i in range(len(allow))]
        far = [mul(q, kt[at, :], NT) + add for at, add in zip(spans, allow)]
        finish([own, *far], [vo[:prompt], *(vt[at, :] for at in spans)])

    @pl.when(block >= first_cont)
    def _():
        cols = lax.broadcasted_iota(jnp.int32, (1, cont), 1)
        own = mul(q, ko[:prompt], NT)
        at = jnp.maximum(block - first_cont, 0) * tq
        segc = segc_ref[pl.ds(pl.multiple_of(at, tq), tq), :1]
        follow = jnp.where((cols <= rows + at) & (segc == segr), mul(q, ko[prompt:], NT), -1e30)
        far = mul(q, kt[...], NT)
        finish([own, follow, far], [vo[:prompt], vo[prompt:], vt[...]])


def sequence_places(prompt, holder, places_ref, rows):
    own = places_ref[0:1, pl.ds(pl.multiple_of(holder * rows, 128), 128)][:, :1]

    def allow(other):
        start = places_ref[0:1, pl.ds(pl.multiple_of(other * rows, 128), 128)][:, :1]
        return jnp.where(start < own, 0.0, -1e30)

    return allow


def down(row):
    return jnp.transpose(jnp.broadcast_to(row, (128, row.shape[1])))


def attend_kernel(prompt, bias_ref, segc_ref, segr_ref, *refs):
    allow = [bias_ref[i : i + 1, :1] for i in range(refs[3].shape[0] // prompt)]
    attend_block(prompt, pl.program_id(1), allow, segc_ref, segr_ref[:1], *refs)


def attend(q, kv, kv_far, bias, seg, prompt):
    rows, width = q.shape
    head = HEAD
    heads = width // head
    far = kv_far.shape[0]
    cont = rows - prompt
    tq = ROWS
    return call(
        partial(attend_kernel, prompt),
        (heads, rows // tq),
        [
            pl.BlockSpec((8, 128), lambda h, b: (0, 0)),
            pl.BlockSpec((cont, 128), lambda h, b: (0, 0)),
            pl.BlockSpec((8, cont), lambda h, b: (0, 0)),
            pl.BlockSpec((tq, head), lambda h, b: (b, h)),
            pl.BlockSpec((rows, head), lambda h, b: (0, 2 * h)),
            pl.BlockSpec((rows, head), lambda h, b: (0, 2 * h + 1)),
            pl.BlockSpec((far, head), lambda h, b: (0, 2 * h)),
            pl.BlockSpec((far, head), lambda h, b: (0, 2 * h + 1)),
        ],
        [pl.BlockSpec((tq, head), lambda h, b: (b, h)), pl.BlockSpec((1, 8, tq), lambda h, b: (h, 0, b))],
        [shape(rows, width), shape(heads, 8, rows, kind=F32)],
        4 * rows * (rows + far) * width,
        2 * (2 * q.size + kv.size + kv_far.size),
        rows * (rows + far) * heads,
        name="attend",
    )(bias, jnp.broadcast_to(seg[prompt:, None], (cont, 128)), wide(seg[prompt:]), q, kv, kv, kv_far, kv_far)


def attend_back_block(
    prompt, block, last, allow, segc, segr, q_ref, do_ref, o_ref, stat_ref, ko, vo, kt, vt, table_ref,
    dq_ref, own_ref, near_ref, far_ref, acc_k, acc_v,
):
    tq, head = q_ref.shape
    first_cont = prompt // tq
    scale = 1.0 / math.sqrt(head)
    q = q_ref[...] * BF16(scale)
    do = do_ref[...]
    inner = jnp.sum(do.astype(F32) * o_ref[...].astype(F32), -1, keepdims=True)
    inner = jnp.transpose(jnp.broadcast_to(inner, (tq, 128)))[:1]
    stat = stat_ref[0, :1]
    cols = lax.broadcasted_iota(jnp.int32, (1, tq), 1)

    @pl.when(block == 0)
    def _():
        acc_k[...] = jnp.zeros_like(acc_k)
        acc_v[...] = jnp.zeros_like(acc_v)

    def part(keys, values, at, seen):
        probs = jnp.exp(seen(mul(keys, q, NT)) - stat)
        grads = (probs * (mul(values, do, NT) - inner)).astype(BF16)
        acc_v[at, :] += mul(probs.astype(BF16), do, NN)
        acc_k[at, :] += mul(grads, q, NN)
        return mul(grads, keys, TN)

    def far_parts(total, seen):
        for i in range(kt.shape[0] // prompt):
            at = pl.ds(i * prompt, prompt)
            total += part(kt[at, :], vt[at, :], pl.ds(ko.shape[0] + i * prompt, prompt), partial(seen, i))
        dq_ref[...] = turn(total * scale, table_ref[...], -1.0).astype(BF16)

    @pl.when(block < first_cont)
    def _():
        rows = lax.broadcasted_iota(jnp.int32, (prompt, 1), 0)
        total = part(
            ko[:prompt], vo[:prompt], pl.ds(0, prompt), lambda s: jnp.where(rows <= cols + block * tq, s, -1e30)
        )
        far_parts(total, lambda i, s: s + allow[i])

    @pl.when(block >= first_cont)
    def _():
        cont = ko.shape[0] - prompt
        rows = lax.broadcasted_iota(jnp.int32, (cont, 1), 0)
        total = part(ko[:prompt], vo[:prompt], pl.ds(0, prompt), lambda s: s)
        read = (rows <= cols + (block - first_cont) * tq) & (segc() == segr())
        total += part(ko[prompt:], vo[prompt:], pl.ds(prompt, cont), lambda s: jnp.where(read, s, -1e30))
        far_parts(total, lambda i, s: s)

    @pl.when(block == last)
    def _():
        start = 0
        for ref in (own_ref, near_ref, far_ref):
            at = pl.ds(start, ref.shape[0])
            ref[:, :head] = acc_k[at, :].astype(ref.dtype)
            ref[:, head:] = acc_v[at, :].astype(ref.dtype)
            start += ref.shape[0]


def attend_back_kernel(prompt, bias_ref, segc_ref, segr_ref, *refs):
    allow = [bias_ref[i : i + 1, :1] for i in range(refs[6].shape[0] // prompt)]
    last = pl.num_programs(1) - 1
    attend_back_block(prompt, pl.program_id(1), last, allow, lambda: segc_ref[:, :1], lambda: segr_ref[:1], *refs)


def attend_back(q, do, o, stat, kv, kv_far, bias, seg, prompt, table):
    rows, width = q.shape
    head = HEAD
    heads = width // head
    far = kv_far.shape[0]
    cont = rows - prompt
    tq = ROWS
    first = prompt // tq
    row = pl.BlockSpec((tq, head), lambda h, b: (b, h))

    def column(n, odd):
        return pl.BlockSpec((n, head), lambda h, b: (0, 2 * h + odd))

    def pair(n):
        return pl.BlockSpec((n, 2 * head), lambda h, b: (0, h))

    return call(
        partial(attend_back_kernel, prompt),
        (heads, rows // tq),
        [
            pl.BlockSpec((8, 128), lambda h, b: (0, 0)),
            pl.BlockSpec((cont, 128), lambda h, b: (0, 0)),
            pl.BlockSpec((8, tq), lambda h, b: (0, jnp.maximum(b - first, 0))),
            row,
            row,
            row,
            pl.BlockSpec((1, 8, tq), lambda h, b: (h, 0, b)),
            column(rows, 0),
            column(rows, 1),
            column(far, 0),
            column(far, 1),
            pl.BlockSpec((tq, 384), lambda h, b: (b, 0)),
        ],
        [row, pair(rows), pair(prompt), pair(far - prompt)],
        [
            shape(rows, width),
            shape(rows, 2 * width, kind=F32),
            shape(prompt, 2 * width),
            shape(far - prompt, 2 * width),
        ],
        10 * rows * (rows + far) * width,
        2 * (4 * q.size + 4 * kv.size + 2 * kv_far.size),
        rows * (rows + far) * heads,
        [pltpu.VMEM((rows + far, head), F32), pltpu.VMEM((rows + far, head), F32)],
        name="attend_back",
    )(
        bias, jnp.broadcast_to(seg[prompt:, None], (cont, 128)), wide(seg[prompt:]),
        q, do, o, stat, kv, kv, kv_far, kv_far, table,
    )


def mixed_kernel(a_ref, h_ref, wa_ref, wh_ref, o_ref):
    for i in range(a_ref.shape[0] // ROWS):
        at = pl.ds(i * ROWS, ROWS)
        o_ref[at, :] = (mul(a_ref[at, :], wa_ref[...], NT) + mul(h_ref[at, :], wh_ref[...], NT)).astype(BF16)


def mixed_sum(attended, activated, w_out, w_contract, tile=512):
    rows = attended.shape[0]
    deep, deeper = attended.shape[1], activated.shape[1]
    width = w_out.shape[0]
    return call(
        mixed_kernel,
        (width // tile,),
        [
            pl.BlockSpec((rows, deep), lambda j: (0, 0)),
            pl.BlockSpec((rows, deeper), lambda j: (0, 0)),
            pl.BlockSpec((tile, deep), lambda j: (j, 0)),
            pl.BlockSpec((tile, deeper), lambda j: (j, 0)),
        ],
        pl.BlockSpec((rows, tile), lambda j: (0, j)),
        shape(rows, width),
        2 * rows * width * (deep + deeper),
        2 * (rows + width) * (deep + deeper) + 2 * rows * width,
        name="mixed_sum",
    )(attended, activated, w_out, w_contract)


def attended_grad_kernel(g_ref, w_ref, o_ref):
    for i in range(g_ref.shape[0] // ROWS):
        at = pl.ds(i * ROWS, ROWS)
        o_ref[at, :] = mul(g_ref[at, :], w_ref[...], NN).astype(BF16)


def attended_grads(g, w, tile=256):
    rows, depth = g.shape
    cols = w.shape[1]
    return call(
        attended_grad_kernel,
        (cols // tile,),
        [pl.BlockSpec((rows, depth), lambda j: (0, 0)), pl.BlockSpec((depth, tile), lambda j: (0, j))],
        pl.BlockSpec((rows, tile), lambda j: (0, j)),
        shape(rows, cols),
        2 * rows * depth * cols,
        2 * (rows * depth + w.size + rows * cols),
        name="attended_grads",
    )(g, w)


def hidden_grad_kernel(g_ref, w_ref, d_ref, gp_ref, sum_ref):
    total = 0.0
    for i in range(g_ref.shape[0] // ROWS):
        at = pl.ds(i * ROWS, ROWS)
        grad = (mul(g_ref[at, :], w_ref[...], NN) * d_ref[at, :].astype(F32)).astype(BF16)
        gp_ref[at, :] = grad
        total += jnp.sum(grad.astype(F32), 0, keepdims=True)
    sum_ref[...] = jnp.broadcast_to(total, sum_ref.shape)


def hidden_grads(g, w, slope, tile=512):
    rows, depth = g.shape
    cols = w.shape[1]
    tall = pl.BlockSpec((rows, tile), lambda j: (0, j))
    return call(
        hidden_grad_kernel,
        (cols // tile,),
        [pl.BlockSpec((rows, depth), lambda j: (0, 0)), pl.BlockSpec((depth, tile), lambda j: (0, j)), tall],
        [tall, pl.BlockSpec((8, tile), lambda j: (0, j))],
        [shape(rows, cols), shape(8, cols, kind=F32)],
        2 * rows * depth * cols,
        2 * (rows * depth + w.size + 2 * rows * cols),
        name="hidden_grads",
    )(g, w, slope)


def pack_kernel(prompt_blocks, q_ref, own_ref, near_ref, far_ref, table_ref, o_ref, sum_ref):
    block = pl.program_id(1)
    head = q_ref.shape[1]
    theirs = near_ref[...].astype(F32) + far_ref[...].astype(F32)
    both = own_ref[...] + jnp.where(block < prompt_blocks, theirs, 0.0)
    out = [q_ref[...], turn(both[:, :head], table_ref[...], -1.0).astype(BF16), both[:, head:].astype(BF16)]

    @pl.when(block == 0)
    def _():
        sum_ref[...] = jnp.zeros_like(sum_ref)

    for i, part in enumerate(out):
        o_ref[:, i * head : (i + 1) * head] = part
        sum_ref[:, i * head : (i + 1) * head] += jnp.sum(part.astype(F32), 0, keepdims=True)


def pack(dq, own, near, far, table, prompt):
    rows, width = dq.shape
    head = HEAD
    heads = width // head
    tq = ROWS
    blocks = prompt // tq
    theirs = pl.BlockSpec((tq, 2 * head), lambda h, b: (jnp.minimum(b, blocks - 1), h))
    return call(
        partial(pack_kernel, blocks),
        (heads, rows // tq),
        [
            pl.BlockSpec((tq, head), lambda h, b: (b, h)),
            pl.BlockSpec((tq, 2 * head), lambda h, b: (b, h)),
            theirs,
            theirs,
            pl.BlockSpec((tq, 384), lambda h, b: (b, 0)),
        ],
        [pl.BlockSpec((tq, 3 * head), lambda h, b: (b, h)), pl.BlockSpec((8, 3 * head), lambda h, b: (0, h))],
        [shape(rows, 3 * width), shape(8, 3 * width, kind=F32)],
        10 * rows * width,
        16 * rows * width,
        name="pack",
    )(dq, own, near, far, table)


def unit_grad_kernel(gp_ref, gh_ref, wa_ref, we_ref, x_ref, stat_ref, gain_ref, e_ref, sum_ref):
    sums = [0.0] * 4
    for i in range(gp_ref.shape[0] // ROWS):
        at = pl.ds(i * ROWS, ROWS)
        first = mul(gp_ref[at, :], wa_ref[...], NT)
        second = mul(gh_ref[at, :], we_ref[...], NT)
        e_ref[at, :] = (first * gain_ref[0:1] + second * gain_ref[2:3]).astype(BF16)
        unit = (x_ref[at, :].astype(F32) - stat_ref[at, 0:1]) * stat_ref[at, 1:2]
        for j, v in enumerate((first * unit, first, second * unit, second)):
            sums[j] += jnp.sum(v, 0, keepdims=True)
    for j in range(4):
        sum_ref[j : j + 1] = sums[j]
    sum_ref[4:] = jnp.zeros_like(sum_ref[4:])


def unit_grads(gp, gh, w_attend, w_expand, x, stat, gains, tile=512):
    rows, width = x.shape
    deep, deeper = gp.shape[1], gh.shape[1]
    col = pl.BlockSpec((rows, tile), lambda j: (0, j))
    row = pl.BlockSpec((8, tile), lambda j: (0, j))
    return call(
        unit_grad_kernel,
        (width // tile,),
        [
            pl.BlockSpec((rows, deep), lambda j: (0, 0)),
            pl.BlockSpec((rows, deeper), lambda j: (0, 0)),
            pl.BlockSpec((tile, deep), lambda j: (j, 0)),
            pl.BlockSpec((tile, deeper), lambda j: (j, 0)),
            col,
            pl.BlockSpec((rows, 128), lambda j: (0, 0)),
            row,
        ],
        [col, row],
        [shape(rows, width), shape(8, width, kind=F32)],
        2 * rows * width * (deep + deeper),
        2 * (rows + width) * (deep + deeper) + 4 * rows * width,
        name="unit_grads",
    )(gp, gh, w_attend, w_expand, x, stat, gains)


def far_kernel(a_ref, b_ref, o_ref):
    for i in range(o_ref.shape[0] // ROWS):
        o_ref[pl.ds(i * ROWS, ROWS), :] = mul(a_ref[:, pl.ds(i * ROWS, ROWS)], b_ref[...], TN).astype(BF16)


def near_kernel(a_ref, b_ref, r_ref, *outs):
    size = a_ref.shape[1] // len(outs)
    for i, out in enumerate(outs):
        at = pl.ds(i * size, size)
        out[...] = (mul(a_ref[:, at], b_ref[...], TN) + r_ref[at, :].astype(F32)).astype(out.dtype)


class Hops:
    def __init__(self, send, recv, pairs=False):
        self.send, self.recv, self.made = send, recv, []
        f, c, t = (lax.axis_index(a) for a in ("fsdp", "ctx", "tp"))
        ring = lax.axis_size("tp")
        self.to = {
            "x": {"fsdp": 1 - f},
            "y": {"ctx": (c + 2) % 4},
            "core": {"ctx": c + 1 - 2 * (c % 2)},
            "up": {"tp": (t + 1) % ring},
        }
        self.back = {"tp": (t + ring - 1) % ring}
        if pairs:
            self.to["t1"] = {"tp": t + 1 - 2 * (t % 2)}
            self.to["t2"] = {"tp": t + 2 - 4 * (t // 2 % 2)}

    def greet(self):
        barrier = pltpu.get_barrier_semaphore()
        near = [*self.to.values(), self.back]
        for device in near:
            pl.semaphore_signal(barrier, inc=1, device_id=device, device_id_type=pl.DeviceIdType.MESH)
        pl.semaphore_wait(barrier, len(near))

    def copy(self, way, src, dst):
        i = len(self.made)
        self.made.append(
            pltpu.make_async_remote_copy(
                src,
                dst,
                self.send.at[i],
                self.recv.at[i],
                device_id=self.to[way],
                device_id_type=pl.DeviceIdType.MESH,
            )
        )
        return self.made[-1]

    def end(self):
        for copy in self.made:
            copy.wait_send()


class Block:
    def __init__(self, hops, part, whole, halves=1):
        size = part.shape[0]
        half, piece = size // 2, size // halves

        def at(slot, start=0, rows=size):
            return whole.at[pl.ds(slot * size + start, rows)]

        self.first = [
            [
                hops.copy(way, part.at[pl.ds(i * piece, piece)], at(slot, i * piece, piece))
                for way, slot in (("x", 1), ("y", 2))
            ]
            for i in range(halves)
        ]
        self.corner = [
            hops.copy("x", at(2, 0, half), at(3, 0, half)),
            hops.copy("y", at(1, half, half), at(3, half, half)),
        ]
        self.core = [hops.copy("core", part if slot == 0 else at(slot), at(4 + slot)) for slot in range(4)]


def start(copies):
    for copy in copies:
        copy.start()


def arrive(copies):
    for copy in copies:
        copy.wait_recv()


def table_kernel(pos_ref, freq_ref, o_ref):
    angle = down(pos_ref[...].astype(F32)) * freq_ref[:1]
    c, s = jnp.cos(angle), jnp.sin(angle)
    lane = lax.broadcasted_iota(jnp.int32, angle.shape, 1)
    half = ROT // 2
    o_ref[:, :128] = jnp.where(lane < ROT, c, 1.0)
    o_ref[:, 128:256] = jnp.where(lane < half, -s, 0.0)
    o_ref[:, 256:] = jnp.where((lane >= half) & (lane < ROT), s, 0.0)


def norm_block_kernel(x_ref, gain_ref, first_ref, second_ref, stat_ref):
    x = x_ref[...].astype(F32)
    mean = jnp.mean(x, -1, keepdims=True)
    center = x - mean
    scale = lax.rsqrt(jnp.mean(center * center, -1, keepdims=True) + EPS)
    unit = center * scale
    first_ref[...] = (unit * gain_ref[0:1] + gain_ref[1:2]).astype(BF16)
    second_ref[...] = (unit * gain_ref[2:3] + gain_ref[3:4]).astype(BF16)
    lane = lax.broadcasted_iota(jnp.int32, stat_ref.shape, 1)
    stat_ref[...] = jnp.where(lane == 0, mean, scale)


def project_block_kernel(n_ref, w_ref, b_ref, table_ref, q_ref, kv_ref):
    head = q_ref.shape[1]
    out = mul(n_ref[...], w_ref[...], NN) + b_ref[:1]
    q_ref[...] = turn(out[:, :head], table_ref[...], 1.0).astype(BF16)
    kv_ref[:, :head] = turn(out[:, head : 2 * head], table_ref[...], 1.0).astype(BF16)
    kv_ref[:, head:] = out[:, 2 * head :].astype(BF16)


def expand_block_kernel(n_ref, w_ref, b_ref, h_ref, d_ref):
    pre = mul(n_ref[...], w_ref[...], NN) + b_ref[:1]
    below = 0.5 + 0.5 * lax.erf(pre * math.sqrt(0.5))
    h_ref[...] = (pre * below).astype(BF16)
    d_ref[...] = (below + pre * jnp.exp(-0.5 * pre * pre) * (1.0 / math.sqrt(2 * math.pi))).astype(BF16)


def forward_kernel(places, prompt, *refs):
    (
        x_ref, g_ref, wa, we, wo, wc, gain_1, gain_2, gain_3, gain_4, bias_a, bias_e, seg_ref, pos_ref, freq_ref,
        rows_in, rows_grad, gains, attend_all, expand_all, output_all, contract_all,
        first, second, stat, table, queries, pairs, pairs_far, activated, slope, attended, row_sums, mixed, grad_sum,
        send, recv, local, held_x, held_g, held_gains, held_sum, held_seg, held_pos, segc, gain_rows, *held,
    ) = refs
    hops = Hops(send, recv)
    t, ring = lax.axis_index("tp"), lax.axis_size("tp")
    rows, width = x_ref.shape
    total = rows * ring
    block = width // len(places)
    chunk = rows // 2

    here = pl.ds(t * rows, rows)
    moves = [(x_ref, held_x, rows_in.at[here]), (g_ref, held_g, rows_grad.at[here])]
    loads, stores, count = [], [], 0
    for src, mid, dst in moves:
        loads.append([])
        for i, place in enumerate(places):
            at = pl.ds(pl.multiple_of(place() * block, block), block)
            loads[-1].append(pltpu.make_async_copy(src.at[:, at], mid.at[:, pl.ds(i * block, block)], local.at[count]))
            count += 1
        stores.append(pltpu.make_async_copy(mid, dst, local.at[count]))
        count += 1
    small = [pltpu.make_async_copy(seg_ref, held_seg, local.at[count]), pltpu.make_async_copy(pos_ref, held_pos, local.at[count + 1])]
    count += 2
    for i, src in enumerate((gain_1, gain_2, gain_3, gain_4)):
        small.append(pltpu.make_async_copy(src, gain_rows.at[i], local.at[count]))
        count += 1
    for src, mid, whole in zip((wa, we, wo, wc), held, (attend_all, expand_all, output_all, contract_all)):
        loads.append([pltpu.make_async_copy(src, mid, local.at[count])])
        stores.append(pltpu.make_async_copy(mid, whole.at[pl.ds(0, src.shape[0])], local.at[count + 1]))
        count += 2

    def rings(ref, held_rows):
        made = {}
        for step in range(ring - 1):
            for half in range(2):
                at = ref.at[pl.ds(((t + ring - step) % ring) * rows + half * chunk, chunk)]
                src = held_rows.at[pl.ds(half * chunk, chunk)] if step == 0 else at
                made[step, half] = hops.copy("up", src, at)
        return made

    ring_x, ring_g = rings(rows_in, held_x), rings(rows_grad, held_g)
    a, e, o = (Block(hops, part, whole) for part, whole in ((wa, attend_all), (we, expand_all), (wo, output_all)))
    c = Block(hops, wc, contract_all, 2)
    own_pairs = pairs.at[pl.ds(0, prompt)]
    far = [pairs_far.at[pl.ds(i * prompt, prompt)] for i in range(3)]
    pair_y, pair_core = hops.copy("y", own_pairs, far[0]), hops.copy("core", own_pairs, far[1])
    pair_corner = hops.copy("core", far[0], far[2])

    def forward(copies, step, half):
        arrive([copies[step, half]])
        if step < ring - 2:
            start([copies[step + 1, half]])

    head = HEAD
    heads = queries.shape[1] // head

    def span(step):
        return pl.ds(((t + ring - step) % ring) * rows, rows)

    def norm(step):
        tile = 128
        row = pl.BlockSpec((tile, width), lambda i: (i, 0))
        pltpu.emit_pipeline(
            norm_block_kernel,
            grid=(rows // tile,),
            in_specs=[row, pl.BlockSpec((8, width), lambda i: (0, 0))],
            out_specs=[row, row, pl.BlockSpec((tile, 128), lambda i: (i, 0))],
        )(rows_in.at[span(step)], gains, first.at[span(step)], second.at[span(step)], stat.at[span(step)])

    def project(step):
        pltpu.emit_pipeline(
            project_block_kernel,
            grid=(heads,),
            in_specs=[
                pl.BlockSpec((rows, width), lambda h: (0, 0)),
                pl.BlockSpec((width, 3 * head), lambda h: (0, h)),
                pl.BlockSpec((1, 3 * head), lambda h: (0, h)),
                pl.BlockSpec((rows, 384), lambda h: (0, 0)),
            ],
            out_specs=[pl.BlockSpec((rows, head), lambda h: (0, h)), pl.BlockSpec((rows, 2 * head), lambda h: (0, h))],
        )(first.at[span(step)], attend_all, bias_a, table.at[span(step)], queries.at[span(step)], pairs.at[span(step)])

    def expand(pumps):
        tile = 512
        out = pl.BlockSpec((total, tile), lambda j: (0, j))

        def body(n_ref, w_ref, b_ref, h_ref, d_ref):
            for when, pump in pumps.items():
                pl.when(pl.program_id(0) == when)(pump)
            for i in range(ring):
                at = pl.ds(i * rows, rows)
                expand_block_kernel(n_ref.at[at], w_ref, b_ref, h_ref.at[at], d_ref.at[at])

        pltpu.emit_pipeline(
            body,
            grid=(expand_all.shape[1] // tile,),
            in_specs=[
                pl.BlockSpec((total, width), lambda j: (0, 0)),
                pl.BlockSpec((width, tile), lambda j: (0, j)),
                pl.BlockSpec((1, tile), lambda j: (0, j)),
            ],
            out_specs=[out, out],
        )(second, expand_all, bias_e, activated, slope)

    for load in loads:
        start(load)
    start(small)
    hops.greet()
    start(a.first[0])
    start([a.core[0]])
    for i, (load, store) in enumerate(zip(loads, stores)):
        for copy in load:
            copy.wait()
        store.start()
        if i == 0:
            start([ring_x[0, 0], ring_x[0, 1], e.core[0]])
    for copy in small:
        copy.wait()
    held_gains[...] = jnp.zeros_like(held_gains)
    for i, place in enumerate(places):
        at = pl.ds(pl.multiple_of(place() * block, block), block)
        for k in range(4):
            held_gains[k : k + 1, i * block : (i + 1) * block] = gain_rows[k, :, at]
    gains_out = pltpu.make_async_copy(held_gains, gains, local.at[count + 1])
    gains_out.start()
    holder = lax.axis_index("ctx")
    after_prompt = pl.ds(pl.multiple_of(holder * total + prompt, 128), total - prompt)
    segc[...] = down(held_seg[0:1, after_prompt])
    allow_of = sequence_places(prompt, holder, held_pos, total)
    c_bits = holder // 2, holder % 2
    others = [((c_bits[0] + b) % 2) * 2 + (c_bits[1] + d) % 2 for b, d in ((1, 0), (0, 1), (1, 1))]
    held_sum[...] = jnp.broadcast_to(jnp.sum(held_g[...].astype(F32), 0, keepdims=True), held_sum.shape)
    sum_out = pltpu.make_async_copy(held_sum, grad_sum, local.at[count])
    sum_out.start()
    for store in stores + [sum_out, gains_out]:
        store.wait()
    pltpu.emit_pipeline(
        table_kernel,
        grid=(total // rows,),
        in_specs=[pl.BlockSpec((1, rows), lambda i: (0, holder * ring + i)), pl.BlockSpec((8, 128), lambda i: (0, 0))],
        out_specs=[pl.BlockSpec((rows, 384), lambda i: (i, 0))],
    )(pos_ref, freq_ref, table)
    norm(0)
    forward(ring_x, 0, 0)
    start(e.first[0])
    arrive(a.first[0])
    start(a.corner + a.core[1:3])
    forward(ring_x, 0, 1)
    norm(1)
    forward(ring_x, 1, 0)
    arrive(a.corner)
    start([a.core[3]])
    arrive(e.first[0])
    start(e.corner + e.core[1:3] + o.first[0] + [o.core[0]] + c.first[0] + [c.core[0]])
    forward(ring_x, 1, 1)
    start([ring_g[0, 0], ring_g[0, 1]])
    norm(2)
    arrive(a.core)
    project(0)
    forward(ring_x, 2, 0)
    arrive(e.corner)
    start([e.core[3]])
    project(1)
    project(2)
    arrive(o.first[0])
    start(o.core[1:3])
    forward(ring_x, 2, 1)
    norm(3)
    project(3)
    start([pair_y, pair_core] + o.corner)
    arrive(e.core)

    def second_halves():
        arrive(c.first[0])
        start(c.first[1])

    def corners():
        arrive(o.corner)
        start([o.core[3]])

    expand({0: lambda: forward(ring_g, 0, 0), 1: second_halves, 2: corners, 3: lambda: forward(ring_g, 0, 1)})
    arrive([pair_y])
    start([pair_corner])
    arrive(c.first[1])
    start(c.corner + c.core[1:3])
    arrive([pair_core, pair_corner])

    def attend_step(*args):
        step = pl.program_id(0) * pl.num_programs(1) + pl.program_id(1)
        pl.when(step == 2)(lambda: forward(ring_g, 1, 0))
        pl.when(step == 7)(lambda: forward(ring_g, 1, 1))
        attend_block(prompt, pl.program_id(1), [allow_of(i) for i in others], segc, held_seg[0:1, after_prompt], *args)

    tq = ROWS
    n_far = pairs_far.shape[0]
    pltpu.emit_pipeline(
        attend_step,
        grid=(heads, total // tq),
        in_specs=[
            pl.BlockSpec((tq, head), lambda h, b: (b, h)),
            pl.BlockSpec((total, head), lambda h, b: (0, 2 * h)),
            pl.BlockSpec((total, head), lambda h, b: (0, 2 * h + 1)),
            pl.BlockSpec((n_far, head), lambda h, b: (0, 2 * h)),
            pl.BlockSpec((n_far, head), lambda h, b: (0, 2 * h + 1)),
        ],
        out_specs=[pl.BlockSpec((tq, head), lambda h, b: (b, h)), pl.BlockSpec((1, 8, tq), lambda h, b: (h, 0, b))],
    )(queries, pairs, pairs, pairs_far, pairs_far, attended, row_sums)

    forward(ring_g, 2, 0)
    arrive(c.corner)
    start([c.core[3]])
    arrive(o.core + c.core)
    tile = 512
    pltpu.emit_pipeline(
        mixed_kernel,
        grid=(width // tile,),
        in_specs=[
            pl.BlockSpec((total, attended.shape[1]), lambda j: (0, 0)),
            pl.BlockSpec((total, activated.shape[1]), lambda j: (0, 0)),
            pl.BlockSpec((tile, attended.shape[1]), lambda j: (j, 0)),
            pl.BlockSpec((tile, activated.shape[1]), lambda j: (j, 0)),
        ],
        out_specs=[pl.BlockSpec((total, tile), lambda j: (0, j))],
    )(attended, activated, output_all, contract_all, mixed)
    forward(ring_g, 2, 1)
    hops.end()


def forward_pass(places, prompt, heads, x, g, weights, gains, bias_a, bias_e, segments, positions):
    ring = lax.axis_size("tp")
    rows, width = x.shape
    total = ring * rows
    wa, we, wo, wc = weights
    head = HEAD
    hidden = we.shape[1]
    freq = 10000.0 ** (-2.0 * (np.arange(128) % (ROT // 2)) / ROT)
    freq = jnp.asarray(np.tile(freq.astype(np.float32)[None], (8, 1)))
    inputs = [x, g, wa, we, wo, wc, *gains, bias_a, bias_e, segments, positions, freq]
    outs = [
        shape(total, width), shape(total, width), shape(8, width, kind=F32),
        *(shape(8 * w.shape[0], w.shape[1]) for w in (wa, we, wo, wc)),
        shape(total, width), shape(total, width), shape(total, 128, kind=F32), shape(total, 384, kind=F32),
        shape(total, heads * head), shape(total, 2 * heads * head), shape(3 * prompt, 2 * heads * head),
        shape(total, hidden), shape(total, hidden), shape(total, heads * head), shape(heads, 8, total, kind=F32),
        shape(total, width), shape(8, width, kind=F32),
    ]
    copies = 4 * (ring - 1) + 34 + 3
    ref = pl.BlockSpec(memory_space=pl.ANY)
    return pl.pallas_call(
        partial(forward_kernel, places, prompt),
        in_specs=[ref] * len(inputs),
        out_specs=[ref] * len(outs),
        out_shape=outs,
        scratch_shapes=[
            pltpu.SemaphoreType.DMA((copies,)),
            pltpu.SemaphoreType.DMA((copies,)),
            pltpu.SemaphoreType.DMA((2 * len(places) + 18,)),
            pltpu.VMEM(x.shape, BF16),
            pltpu.VMEM(g.shape, BF16),
            pltpu.VMEM((8, width), F32),
            pltpu.VMEM((8, width), F32),
            pltpu.VMEM(segments.shape, jnp.int32),
            pltpu.VMEM(positions.shape, jnp.int32),
            pltpu.VMEM((total - prompt, 128), jnp.int32),
            pltpu.VMEM((4, 1, width), F32),
            *(pltpu.VMEM(w.shape, BF16) for w in weights),
        ],
        compiler_params=pltpu.CompilerParams(collective_id=0, has_side_effects=True, vmem_limit_bytes=56 * 2**20),
        cost_estimate=pl.CostEstimate(flops=40 * 10**9, bytes_accessed=200 * 2**20, transcendentals=10**7),
        name="forward_pass",
    )(*inputs)


class RingSum:
    def __init__(self, hops, copies, source, landing, held, last):
        t, ring = lax.axis_index("tp"), lax.axis_size("tp")
        rows = last.shape[0]
        half = rows // 2
        self.sends, self.loads, self.adds = {}, {}, {}
        for h in range(2):
            part = pl.ds(h * half, half)
            for step in range(ring - 1):
                mine = source.at[pl.ds(((t + 2 * ring - 1 - step) % ring) * rows + h * half, half)]
                src = landing[step - 1].at[part] if step else mine
                if step:
                    if held:
                        self.loads[step, h] = copies(mine, held[step - 1].at[part])
                        mine = held[step - 1].at[part]
                    self.adds[step, h] = (src, mine)
                dst = landing[step].at[part] if step < ring - 2 else last.at[part]
                self.sends[step, h] = hops.copy("up", src, dst)

    def begin(self):
        start(self.sends[0, h] for h in range(2))
        start(self.loads.values())

    def pump(self, step, h):
        arrive([self.sends[step - 1, h]])
        if self.loads:
            self.loads[step, h].wait()
        here, own = self.adds[step, h]
        here[...] = (here[...].astype(F32) + own[...].astype(F32)).astype(BF16)
        start([self.sends[step, h]])

    def finish(self, h):
        arrive([self.sends[max(step for step, _ in self.sends), h]])


class Sums:
    def __init__(self, hops, r, i):
        to_x, to_y, corner = r.to_x[i], r.to_y[i], r.corner[i]
        half = corner.shape[0] // 2
        top, low = pl.ds(0, half), pl.ds(half, half)
        self.core = hops.copy("core", r.far[i], r.core[i])
        self.corner = [hops.copy("x", corner.at[top], r.via_x[i]), hops.copy("y", corner.at[low], r.via_y[i])]
        self.plain = [hops.copy("x", to_x.at[top], r.from_x[i].at[top]), hops.copy("y", to_y.at[low], r.from_y[i].at[low])]
        self.merged = [hops.copy("x", to_x.at[low], r.from_x[i].at[low]), hops.copy("y", to_y.at[top], r.from_y[i].at[top])]
        self.pairs = [
            (self.corner[1], to_x.at[low], r.via_y[i], self.merged[0]),
            (self.corner[0], to_y.at[top], r.via_x[i], self.merged[1]),
        ]

    def merge(self):
        for came, mine, theirs, send in self.pairs:
            arrive([came])
            mine[...] = (mine[...].astype(F32) + theirs[...].astype(F32)).astype(BF16)
            start([send])

    def finish(self):
        arrive(self.plain + self.merged)


def backward_kernel(names, places, prompt, *refs):
    r = SimpleNamespace()
    for name, ref in zip(names, refs):
        if name[-1].isdigit():
            getattr(r, name[:-1]).append(ref) if hasattr(r, name[:-1]) else setattr(r, name[:-1], [ref])
        else:
            setattr(r, name, ref)
    hops = Hops(r.send, r.recv, True)
    made = []

    def local_copy(src, dst):
        made.append(pltpu.make_async_copy(src, dst, r.local.at[len(made)]))
        return made[-1]

    t, ring = lax.axis_index("tp"), lax.axis_size("tp")
    total, width = r.rows_grad.shape
    rows = total // ring
    head = HEAD
    heads = r.queries.shape[1] // head
    tq = ROWS
    cont = total - prompt
    n_far = r.pairs_far.shape[0]
    first_cont = prompt // tq
    blocks = total // tq
    holder = lax.axis_index("ctx")
    c_bits = holder // 2, holder % 2
    others = [((c_bits[0] + b) % 2) * 2 + (c_bits[1] + d) % 2 for b, d in ((1, 0), (0, 1), (1, 1))]
    seq_start = holder * total + prompt

    sum_out = RingSum(hops, local_copy, r.mixed, r.land_out, r.held_out, r.out_recv)
    sum_unit = RingSum(hops, local_copy, r.unit, r.land_unit, None, r.unit_recv)
    pair_core = [hops.copy("core", r.pair_far.at[h], r.pair_core.at[h]) for h in range(heads)]
    pair_y = [hops.copy("y", r.pair_near.at[h], r.pair_recv.at[h]) for h in range(heads)]
    grads = {w: Sums(hops, r, i) for i, w in enumerate("aeoc")}
    vector_hops = [
        hops.copy(way, r.vals.at[i, pl.ds(0, n)], r.got.at[i, pl.ds(0, n)])
        for i, (way, n) in enumerate((("core", 16), ("x", 16), ("y", 16), ("t1", 8), ("t2", 8)))
    ]
    vectors_out = local_copy(r.vals.at[len(vector_hops)], r.vectors)
    sum_load = local_copy(r.grad_sum, r.held_sum)
    grad_load = local_copy(r.rows_grad, r.grad)
    small = [local_copy(r.segments, r.held_seg), local_copy(r.positions, r.held_pos)]
    half = width // 2
    tile = 512

    def pumped(pumps):
        for when, pump in pumps.items():
            pl.when(pl.program_id(0) == when)(pump)

    def back_to_rows():
        cols = 256

        def body(w_ref, o_ref):
            for i in range(total // ROWS):
                at = pl.ds(i * ROWS, ROWS)
                o_ref[at, :] = mul(r.grad[at, :], w_ref[...], NN).astype(BF16)

        pltpu.emit_pipeline(
            body,
            grid=(heads * head // cols,),
            in_specs=[pl.BlockSpec((width, cols), lambda j: (0, j))],
            out_specs=[pl.BlockSpec((total, cols), lambda j: (0, j))],
        )(r.output_all, r.grad_att)

    def attention(pumps):
        def body(*args):
            h, block = pl.program_id(0), pl.program_id(1)
            for (at_h, at_b), pump in pumps.items():
                pl.when((h == at_h) & (block == at_b))(pump)
            outs = (r.pair_own.at[h], r.pair_near.at[h], r.pair_far.at[h])
            at = pl.multiple_of(seq_start + jnp.maximum(block - first_cont, 0) * tq, 128)
            allow_of = sequence_places(prompt, holder, r.held_pos, total)
            attend_back_block(
                prompt, block, blocks - 1, [allow_of(i) for i in others], lambda: r.segc[:, :1],
                lambda: r.held_seg[0:1, pl.ds(at, tq)], *args, *outs, r.acc_k, r.acc_v,
            )
            for k in range(heads):
                pl.when((h == k) & (block == blocks - 1))(lambda: start([pair_core[k]]))

        row = pl.BlockSpec((tq, head), lambda h, b: (b, h))

        def column(n, odd):
            return pl.BlockSpec((n, head), lambda h, b: (0, 2 * h + odd))

        pltpu.emit_pipeline(
            body,
            grid=(heads, blocks),
            in_specs=[
                row,
                row,
                row,
                pl.BlockSpec((1, 8, tq), lambda h, b: (h, 0, b)),
                column(total, 0),
                column(total, 1),
                column(n_far, 0),
                column(n_far, 1),
                pl.BlockSpec((tq, 384), lambda h, b: (b, 0)),
            ],
            out_specs=[row],
        )(
            r.queries, r.grad_att, r.attended, r.row_sums, r.pairs, r.pairs, r.pairs_far, r.pairs_far, r.table, r.grad_q,
        )

    def pair_on(h):
        arrive([pair_core[h]])
        near, theirs = r.pair_near.at[h], r.pair_core.at[h, pl.ds(prompt, prompt)]
        near[...] = (near[...].astype(F32) + theirs[...].astype(F32)).astype(BF16)
        start([pair_y[h]])

    def hidden(pumps={}):
        def body(w_ref, d_ref, gp_ref):
            pumped(pumps)
            j = pl.program_id(0)
            sums = 0.0
            for i in range(total // ROWS):
                at = pl.ds(i * ROWS, ROWS)
                grad = (mul(r.grad[at, :], w_ref[...], NN) * d_ref[at, :].astype(F32)).astype(BF16)
                gp_ref[at, :] = grad
                sums += jnp.sum(grad.astype(F32), 0, keepdims=True)
            r.vals[0, 9:10, pl.ds(pl.multiple_of(j * tile, tile), tile)] = sums

        tall = pl.BlockSpec((total, tile), lambda j: (0, j))
        pltpu.emit_pipeline(
            body,
            grid=(r.grad_pre.shape[1] // tile,),
            in_specs=[pl.BlockSpec((width, tile), lambda j: (0, j)), tall],
            out_specs=[tall],
        )(r.contract_all, r.slope, r.grad_pre)

    def far_tile(left, right, out):
        for i in range(half // ROWS):
            out[pl.ds(i * ROWS, ROWS), :] = mul(left[:, pl.ds(i * ROWS, ROWS)], right[...], TN).astype(BF16)

    def near_tile(left, right, received, own, outs, j):
        size = half // 4
        cols = pl.ds(pl.multiple_of(j * tile, tile), tile)
        for i in range(4):
            at = pl.ds(i * size, size)
            out = mul(left[:, at], right[...], TN) + received[at, :].astype(F32)
            if i:
                outs[i - 1][:, cols] = out.astype(BF16)
            else:
                own[...] = out

    def stays(i):
        return (r.to_x[i], r.to_y[i], r.corner[i])

    def far_both(pumps={}):
        steps = r.activated.shape[1] // tile

        def body(h_ref, a_ref, c_out, o_out):
            pumped(pumps)
            j = pl.program_id(0)
            left = r.grad.at[:, pl.ds(half, half)]
            pl.when(j < steps)(lambda: far_tile(left, h_ref, c_out))
            pl.when(j == steps)(lambda: far_tile(left, a_ref, o_out))

        pltpu.emit_pipeline(
            body,
            grid=(steps + 1,),
            in_specs=[
                pl.BlockSpec((total, tile), lambda j: (0, jnp.minimum(j, steps - 1))),
                pl.BlockSpec((total, tile), lambda j: (0, 0)),
            ],
            out_specs=[
                pl.BlockSpec((half, tile), lambda j: (0, jnp.minimum(j, steps - 1))),
                pl.BlockSpec((half, tile), lambda j: (0, 0)),
            ],
        )(r.activated, r.attended, r.far[3], r.far[2])
        start([grads["c"].core, grads["o"].core])

    def near_both(pumps={}):
        steps = r.activated.shape[1] // tile
        arrive([grads["c"].core, grads["o"].core])

        def body(h_ref, a_ref, c_in, o_in, c_own, o_own):
            pumped(pumps)
            j = pl.program_id(0)
            left = r.grad.at[:, pl.ds(0, half)]
            pl.when(j < steps)(lambda: near_tile(left, h_ref, c_in, c_own, stays(3), jnp.minimum(j, steps - 1)))
            pl.when(j == steps)(lambda: near_tile(left, a_ref, o_in, o_own, stays(2), 0))

        def wide_tile(rows):
            return pl.BlockSpec((rows, tile), lambda j: (0, jnp.minimum(j, steps - 1)))

        def one_tile(rows):
            return pl.BlockSpec((rows, tile), lambda j: (0, 0))

        pltpu.emit_pipeline(
            body,
            grid=(steps + 1,),
            in_specs=[wide_tile(total), one_tile(total), wide_tile(half), one_tile(half)],
            out_specs=[wide_tile(half // 4), one_tile(half // 4)],
        )(r.activated, r.attended, r.core[3], r.core[2], r.own[3], r.own[2])

    def far(i, left, right, pumps={}):
        def body(a_ref, b_ref, out):
            pumped(pumps)
            far_tile(a_ref, b_ref, out)

        pltpu.emit_pipeline(
            body,
            grid=(right.shape[1] // tile,),
            in_specs=[pl.BlockSpec((total, half), lambda j: (0, 1)), pl.BlockSpec((total, tile), lambda j: (0, j))],
            out_specs=[pl.BlockSpec((half, tile), lambda j: (0, j))],
        )(left, right, r.far[i])

    def near(i, left, right, pumps={}):
        def body(a_ref, b_ref, received, own):
            pumped(pumps)
            near_tile(a_ref, b_ref, received, own, stays(i), pl.program_id(0))

        pltpu.emit_pipeline(
            body,
            grid=(right.shape[1] // tile,),
            in_specs=[
                pl.BlockSpec((total, half), lambda j: (0, 0)),
                pl.BlockSpec((total, tile), lambda j: (0, j)),
                pl.BlockSpec((half, tile), lambda j: (0, j)),
            ],
            out_specs=[pl.BlockSpec((half // 4, tile), lambda j: (0, j))],
        )(left, right, r.core[i], r.own[i])

    def pack_pairs():
        def body(*args):
            pack_block(pl.program_id(0), pl.program_id(1), r, *args)

        pltpu.emit_pipeline(
            body,
            grid=(heads, 2),
            in_specs=[pl.BlockSpec((prompt, head), lambda h, b: (b, h)), pl.BlockSpec((prompt, 384), lambda h, b: (b, 0))],
            out_specs=[pl.BlockSpec((prompt, 3 * head), lambda h, b: (b, h))],
        )(r.grad_q, r.table, r.grad_flat)

    def unit_pair(step, pumps={}):
        chunks = [(t + 2 * ring - 1 - step - i) % ring for i in range(2)]
        spans = [pl.ds(chunk * rows, rows) for chunk in chunks]

        def body(wa_ref, we_ref, gain_ref, *args):
            pumped(pumps)
            j = pl.program_id(0)
            cols = pl.ds(pl.multiple_of(j * tile, tile), tile)
            sums = [0.0] * 4
            for i in range(2):
                gp_ref, gh_ref, x_ref, stat_ref = args[4 * i : 4 * i + 4]
                one = mul(gp_ref[...], wa_ref[...], NT)
                two = mul(gh_ref[...], we_ref[...], NT)
                r.unit[spans[i], cols] = (one * gain_ref[0:1] + two * gain_ref[2:3]).astype(BF16)
                scaled = (x_ref[...].astype(F32) - stat_ref[:, 0:1]) * stat_ref[:, 1:2]
                for k, v in enumerate((one * scaled, one, two * scaled, two)):
                    sums[k] += jnp.sum(v, 0, keepdims=True)
            for k in range(4):
                r.vec[k : k + 1, cols] += sums[k]

        deep, deeper = r.grad_flat.shape[1], r.grad_pre.shape[1]
        rows_specs = [
            pl.BlockSpec((rows, deep), lambda j: (0, 0)),
            pl.BlockSpec((rows, deeper), lambda j: (0, 0)),
            pl.BlockSpec((rows, tile), lambda j: (0, j)),
            pl.BlockSpec((rows, 128), lambda j: (0, 0)),
        ]
        pltpu.emit_pipeline(
            body,
            grid=(width // tile,),
            in_specs=[
                pl.BlockSpec((tile, deep), lambda j: (j, 0)),
                pl.BlockSpec((tile, deeper), lambda j: (j, 0)),
                pl.BlockSpec((8, tile), lambda j: (0, j)),
                *rows_specs,
                *rows_specs,
            ],
            out_specs=[],
        )(
            r.attend_all, r.expand_all, r.gains,
            *(ref.at[at] for at in spans for ref in (r.grad_flat, r.grad_pre, r.rows_in, r.stat)),
        )

    def vectors_begin():
        size = width // len(places)
        for i, place in enumerate(places):
            to = pl.ds(pl.multiple_of(place() * size, size), size)
            r.vals[0, 0:4, to] = r.vec[0:4, i * size : (i + 1) * size]
            r.vals[0, 4:5, to] = r.held_sum[0:1, i * size : (i + 1) * size]
        start(vector_hops[:1])

    def vectors_on(i):
        arrive([vector_hops[i]])
        n = 16 if i < 3 else 8
        r.vals[i + 1, pl.ds(0, n), :] = r.vals[i, pl.ds(0, n), :] + r.got[i, pl.ds(0, n), :]
        if n < 16:
            r.vals[i + 1, pl.ds(8, 8), :] = r.vals[i, pl.ds(8, 8), :]
        start(vector_hops[i + 1 : i + 2] or [vectors_out])

    c, o, e, a = (grads[w] for w in "coea")
    hops.greet()
    start([grad_load])
    sum_out.begin()
    start([sum_load, *small])
    r.vals[0, :, :] = jnp.zeros_like(r.vals[0, :, :])
    r.vec[...] = jnp.zeros_like(r.vec)
    grad_load.wait()
    sum_load.wait()
    for copy in small:
        copy.wait()
    r.segc[...] = down(r.held_seg[0:1, pl.ds(pl.multiple_of(seq_start, 128), cont)])

    far_both()
    back_to_rows()
    sum_out.pump(1, 0)
    near_both({4: lambda: sum_out.pump(1, 1)})
    start(c.corner + o.corner + c.plain[:1] + o.plain[:1])
    attention({(1, 0): lambda: sum_out.pump(2, 0), (1, 1): lambda: pair_on(0), (1, 3): lambda: sum_out.pump(2, 1)})
    pair_on(1)
    hidden()
    arrive(pair_y)
    start(c.plain[1:] + o.plain[1:])
    pack_pairs()
    c.merge()
    o.merge()
    unit_pair(0)
    sum_unit.begin()
    far(1, r.second, r.grad_pre)
    start([e.core])
    far(0, r.first, r.grad_flat, {1: lambda: sum_unit.pump(1, 0)})
    start([a.core])
    arrive([e.core])
    near(1, r.second, r.grad_pre, {1: lambda: sum_unit.pump(1, 1)})
    start(e.corner + e.plain)
    unit_pair(2)
    sum_unit.pump(2, 0)
    vectors_begin()
    e.merge()
    arrive([a.core])
    near(0, r.first, r.grad_flat, {0: lambda: vectors_on(0), 1: lambda: sum_unit.pump(2, 1)})
    start(a.corner + a.plain)
    for i in range(1, 4):
        vectors_on(i)
    vectors_on(4)
    for h in range(2):
        sum_out.finish(h)
    a.merge()
    for w in "coea":
        grads[w].finish()
    here = pl.ds(t * rows, rows)
    own_unit = local_copy(r.unit.at[here], r.unit_own)
    start([own_unit])
    for h in range(2):
        sum_unit.finish(h)
    vectors_out.wait()
    own_unit.wait()
    hops.end()


def pack_block(h, block, r, q_ref, table_ref, o_ref):
    tq, head = q_ref.shape
    theirs = r.pair_recv[h].astype(F32) + r.pair_core[h, :tq, :].astype(F32)
    own = r.pair_own[h, pl.ds(pl.multiple_of(block * tq, tq), tq), :]
    both = own + jnp.where(block == 0, theirs, 0.0)
    out = [q_ref[...], turn(both[:, :head], table_ref[...], -1.0).astype(BF16), both[:, head:].astype(BF16)]
    for i, part in enumerate(out):
        o_ref[:, i * head : (i + 1) * head] = part
        at = pl.ds(pl.multiple_of((h * 3 + i) * head, head), head)
        r.vals[0, 8:9, at] += jnp.sum(part.astype(F32), 0, keepdims=True)


def backward_pass(places, prompt, values, segments, positions):
    total, width = values["rows_grad"].shape
    ring = lax.axis_size("tp")
    rows = total // ring
    heads, _, _ = values["row_sums"].shape
    head = HEAD
    cont = total - prompt
    far = values["pairs_far"].shape[0]
    inputs = dict(values, segments=segments, positions=positions)
    hidden = values["slope"].shape[1]
    columns = [3 * heads * head, hidden, heads * head, hidden]
    half, size = width // 2, width // 8
    outs = {
        "out_recv": shape(rows, width),
        "unit_recv": shape(rows, width),
        "unit_own": shape(rows, width),
        "vectors": shape(16, width, kind=F32),
        "grad_att": shape(total, heads * head),
        "grad_q": shape(total, heads * head),
        "grad_flat": shape(total, 3 * heads * head),
        "grad_pre": shape(total, hidden),
    }
    stay = {}
    for i, cols in enumerate(columns):
        outs[f"own{i}"] = shape(size, cols, kind=F32)
        for name, n in (("far", half), ("core", half), ("from_x", size), ("from_y", size)):
            outs[f"{name}{i}"] = shape(n, cols)
        for name, n in (("to_x", size), ("to_y", size), ("corner", size), ("via_x", size // 2), ("via_y", size // 2)):
            stay[f"{name}{i}"] = pltpu.VMEM((n, cols), BF16)
    copies = 4 * (ring - 1) + 2 * heads + 7 * len(columns) + 5
    block = pltpu.VMEM((rows, width), BF16)
    scratch = {
        "send": pltpu.SemaphoreType.DMA((copies,)),
        "recv": pltpu.SemaphoreType.DMA((copies,)),
        "local": pltpu.SemaphoreType.DMA((2 * (ring - 2) + 6,)),
        "held_seg": pltpu.VMEM(segments.shape, jnp.int32),
        "held_pos": pltpu.VMEM(positions.shape, jnp.int32),
        "segc": pltpu.VMEM((cont, 128), jnp.int32),
        "grad": pltpu.VMEM((total, width), BF16),
        "unit": pltpu.VMEM((total, width), BF16),
        "pair_own": pltpu.VMEM((heads, total, 2 * head), F32),
        "pair_near": pltpu.VMEM((heads, prompt, 2 * head), BF16),
        "pair_far": pltpu.VMEM((heads, 2 * prompt, 2 * head), BF16),
        "pair_core": pltpu.VMEM((heads, 2 * prompt, 2 * head), BF16),
        "pair_recv": pltpu.VMEM((heads, prompt, 2 * head), BF16),
        **stay,
        "acc_k": pltpu.VMEM((total + far, head), F32),
        "acc_v": pltpu.VMEM((total + far, head), F32),
        "vals": pltpu.VMEM((6, 16, width), F32),
        "got": pltpu.VMEM((5, 16, width), F32),
        "vec": pltpu.VMEM((8, width), F32),
        "held_sum": pltpu.VMEM((8, width), F32),
    }
    for name in ("land_out", "held_out", "land_unit"):
        for i in range(ring - 2):
            scratch[f"{name}{i}"] = block
    names = [*inputs, *outs, *scratch]
    ref = pl.BlockSpec(memory_space=pl.ANY)
    result = pl.pallas_call(
        partial(backward_kernel, names, places, prompt),
        in_specs=[ref] * len(inputs),
        out_specs=[ref] * len(outs),
        out_shape=list(outs.values()),
        scratch_shapes=list(scratch.values()),
        compiler_params=pltpu.CompilerParams(collective_id=1, has_side_effects=True, vmem_limit_bytes=60 * 2**20),
        cost_estimate=pl.CostEstimate(flops=60 * 10**9, bytes_accessed=200 * 2**20, transcendentals=10**7),
        name="backward_pass",
    )(*inputs.values())
    return dict(zip(outs, result))


class SquareLinks:
    order = ((0, 0, 0), (1, 0, 0), (0, 1, 0), (1, 1, 0), (0, 0, 1), (1, 0, 1), (0, 1, 1), (1, 1, 1))

    def place(self, bits):
        f, c = lax.axis_index("fsdp"), lax.axis_index("ctx")
        a, b, d = bits
        return ((f ^ a) * 2 + ((c // 2) ^ b)) * 2 + ((c % 2) ^ d)

    def spot(self, p):
        f, c = lax.axis_index("fsdp"), lax.axis_index("ctx")
        a, b, d = f ^ (p // 4), (c // 2) ^ (p // 2 % 2), (c % 2) ^ (p % 2)
        return d * 4 + b * 2 + a

    def places(self):
        return [partial(self.place, bits) for bits in self.order]

    def spots(self):
        return [partial(self.spot, p) for p in range(8)]


class AnyLinks:
    def places(self):
        return [lambda: 0]

    def spots(self):
        return [lambda: 0]

    def gather(self, block):
        return lax.all_gather(block, ("fsdp", "ctx"), axis=0, tiled=True)

    def scatter(self, whole):
        return lax.psum_scatter(whole, ("fsdp", "ctx"), scatter_dimension=0, tiled=True).astype(F32)

    def others(self, v):
        return jnp.roll(v, -lax.axis_index("ctx"), 0)[1:]

    def gather_others(self, block):
        rows = block.shape[0]
        whole = lax.all_gather(block, "ctx", axis=0, tiled=True)
        return jnp.roll(whole, -rows * lax.axis_index("ctx"), 0)[rows:]

    def scatter_others(self, near, far):
        rows = near.shape[0]
        whole = jnp.concatenate([jnp.zeros_like(near), near, far], 0)
        whole = jnp.roll(whole, rows * lax.axis_index("ctx"), 0)
        return lax.psum_scatter(whole, "ctx", scatter_dimension=0, tiled=True)


def end_kernel(spots, x_ref, g_ref, m_ref, o_ref, e_ref, f_ref, b_ref, out_ref, grad_ref, e_whole):
    size = x_ref.shape[1] // len(spots)
    for i, spot in enumerate(spots):
        at, to = pl.ds(pl.multiple_of(spot() * size, size), size), pl.ds(i * size, size)
        branches = m_ref[:, at].astype(F32) + o_ref[:, at].astype(F32)
        out_ref[:, to] = (x_ref[:, to].astype(F32) + branches + b_ref[:1, to]).astype(BF16)
        e_whole[:, to] = e_ref[:, at].astype(F32) + f_ref[:, at].astype(F32)
    x = x_ref[...].astype(F32)
    center = x - jnp.mean(x, -1, keepdims=True)
    scale = lax.rsqrt(jnp.mean(center * center, -1, keepdims=True) + EPS)
    unit = center * scale
    e = e_whole[...]
    rest = e - jnp.mean(e, -1, keepdims=True) - unit * jnp.mean(e * unit, -1, keepdims=True)
    grad_ref[...] = g_ref[...].astype(F32) + scale * rest


def row_results(x, g, mixed, mixed_own, unit, unit_own, bias, spots):
    rows, width = x.shape
    block = pl.BlockSpec((64, width), lambda i: (i, 0))
    own = pl.BlockSpec((64, width), lambda i: (lax.axis_index("tp") * (rows // 64) + i, 0))
    return call(
        partial(end_kernel, spots),
        (rows // 64,),
        [block] * 3 + [own, block, block, pl.BlockSpec((1, width), lambda i: (0, 0))],
        [block, block],
        [shape(rows, width), shape(rows, width, kind=F32)],
        15 * x.size,
        18 * x.size,
        scratch=[pltpu.VMEM((64, width), F32)],
        name="row_results",
    )(x, g, mixed, mixed_own, unit, unit_own, bias[None])


def shards(
    stream_in,
    stream_grad,
    segments,
    positions,
    first_gain,
    first_shift,
    second_gain,
    second_shift,
    attend_weight,
    attend_bias,
    output_weight,
    expand_weight,
    expand_bias,
    contract_weight,
    output_bias,
):
    square = (lax.axis_size("fsdp"), lax.axis_size("ctx"), lax.axis_size("tp")) == (2, 4, 4)
    links = SquareLinks() if square else AnyLinks()
    local_rows = attend_weight.shape[0]
    heads = attend_bias.shape[0]
    holders = lax.axis_size("ctx")
    holder = lax.axis_index("ctx")
    prompt = PROMPT // holders

    row_count = stream_in.shape[0] * lax.axis_size("tp")
    weights = (attend_weight.reshape(local_rows, -1), expand_weight, output_weight, contract_weight)

    forward_names = (
        "rows_in",
        "rows_grad",
        "gains",
        "attend_all",
        "expand_all",
        "output_all",
        "contract_all",
        "first",
        "second",
        "stat",
        "table",
        "queries",
        "pairs",
        "pairs_far",
        "activated",
        "slope",
        "attended",
        "row_sums",
        "mixed",
        "grad_sum",
    )
    if square:
        rows_of = (v[None] for v in (first_gain, first_shift, second_gain, second_shift))
        made = forward_pass(
            links.places(), prompt, heads, stream_in, stream_grad, weights, [*rows_of], attend_bias.reshape(1, -1),
            expand_bias[None], segments[None], positions[None],
        )
        values = dict(zip(forward_names, made))
        back = backward_pass(links.places(), prompt, values, segments[None], positions[None])
        sums = (back["out_recv"], values["mixed"], back["unit_recv"], back["unit_own"])
        weight_grads = [
            back[f"own{i}"] + back[f"from_x{i}"].astype(F32) + back[f"from_y{i}"].astype(F32) for i in range(4)
        ]
        vectors = back["vectors"]
        norm_sums = [vectors[i] for i in range(5)]
        bias_sums = [vectors[8, : attend_bias.size], vectors[9]]
    else:
        gains = jnp.concatenate([jnp.stack([first_gain, first_shift, second_gain, second_shift]), jnp.zeros((4, first_gain.shape[0]), F32)])
        row_pos = lax.dynamic_slice_in_dim(positions, holder * row_count, row_count)
        row_seg = lax.dynamic_slice_in_dim(segments, holder * row_count, row_count)
        starts = positions.reshape(holders, row_count)[:, 0]
        bias = jnp.where(links.others(starts) < row_pos[0], 0.0, -1e30).astype(F32)
        bias = jnp.broadcast_to(jnp.pad(bias, (0, 8 - bias.shape[0]))[:, None], (8, 128))
        rows_in, rows_grad = (lax.all_gather(v, "tp", axis=0, tiled=True) for v in (stream_in, stream_grad))
        attend_all, expand_all, output_all, contract_all = (links.gather(v) for v in weights)
        table = turn_table(row_pos)
        first, second, rows_in, stat = norms(rows_in, gains, links.places())
        queries, pairs = project(first, attend_all, attend_bias.reshape(-1), table, heads)
        pairs_far = links.gather_others(pairs[:prompt])
        activated, slope = expand(second, expand_all, expand_bias)
        attended, row_sums = attend(queries, pairs, pairs_far, bias, row_seg, prompt)
        mixed = mixed_sum(attended, activated, output_all, contract_all)
        branches = lax.psum_scatter(mixed, "tp", scatter_dimension=0, tiled=True)
        grad_attended = attended_grads(rows_grad, output_all)
        grad_queries, pair_own, pair_near, pair_far = attend_back(
            queries, grad_attended, attended, row_sums, pairs, pairs_far, bias, row_seg, prompt, table
        )
        theirs = links.scatter_others(pair_near, pair_far)
        grad_pre, expand_sums = hidden_grads(rows_grad, contract_all, slope)
        grad_flat, attend_sums = pack(grad_queries, pair_own, theirs, jnp.zeros_like(theirs), table, prompt)
        unit, vector_parts = unit_grads(grad_flat, grad_pre, attend_all, expand_all, rows_in, stat, gains)
        unit_part = lax.psum_scatter(unit, "tp", scatter_dimension=0, tiled=True)
        weight_grads = [
            links.scatter(jnp.einsum("tc,tk->ck", left, right, preferred_element_type=F32).astype(BF16))
            for left, right in ((first, grad_flat), (second, grad_pre), (rows_grad, attended), (rows_grad, activated))
        ]
        row_sum = jnp.sum(stream_grad.astype(F32), 0)
        norm_sums = lax.psum([*vector_parts[:4], row_sum], ("fsdp", "ctx", "tp"))
        bias_sums = lax.psum([attend_sums[0], expand_sums[0]], ("fsdp", "ctx"))
        sums = (branches, jnp.zeros((row_count, stream_in.shape[1]), BF16), unit_part, jnp.zeros_like(unit_part))
    stream_out, input_grad = row_results(stream_in, stream_grad, *sums, output_bias, links.spots())
    return (
        stream_out,
        input_grad,
        *norm_sums[:4],
        weight_grads[0].reshape(attend_weight.shape),
        bias_sums[0].reshape(attend_bias.shape),
        weight_grads[2],
        weight_grads[1],
        bias_sums[1],
        weight_grads[3],
        norm_sums[4],
    )


def solution(mesh):
    tokens = P(("fsdp", "ctx", "tp"), None)
    weight = P(("fsdp", "ctx"), "tp")
    heads = P(("fsdp", "ctx"), "tp", None)
    return jax.shard_map(
        shards,
        mesh=mesh,
        in_specs=(
            tokens,
            tokens,
            P("fsdp"),
            P("fsdp"),
            P(),
            P(),
            P(),
            P(),
            heads,
            P("tp", None),
            weight,
            weight,
            P("tp"),
            weight,
            P(),
        ),
        out_specs=(
            tokens,
            tokens,
            P(),
            P(),
            P(),
            P(),
            heads,
            P("tp", None),
            weight,
            weight,
            P("tp"),
            weight,
            P(),
        ),
        check_vma=False,
    )
```

```python
from functools import partial, reduce
import math
from types import SimpleNamespace

import jax
import jax.numpy as jnp
import numpy as np
from jax import lax
from jax.experimental import pallas as pl
from jax.experimental.pallas import tpu as pltpu
from jax.sharding import PartitionSpec as P

ROT = 64
PROMPT = 2048
EPS = 1e-05
F32 = jnp.float32
BF16 = jnp.bfloat16
ROWS = 256
HEAD = 256
NN = (((1,), (0,)), ((), ()))
NT = (((1,), (1,)), ((), ()))
TN = (((0,), (0,)), ((), ()))


def mul(a, b, dims):
    return lax.dot_general(a, b, dims, preferred_element_type=F32)


def call(kernel, grid, in_specs, out_specs, out_shape, flops, moved, exps=0, scratch=(), mib=48, name=None):
    return pl.pallas_call(
        kernel,
        grid=grid,
        in_specs=in_specs,
        out_specs=out_specs,
        out_shape=out_shape,
        scratch_shapes=scratch,
        compiler_params=pltpu.CompilerParams(vmem_limit_bytes=mib * 2**20),
        cost_estimate=pl.CostEstimate(flops=flops, bytes_accessed=moved, transcendentals=exps),
        name=name,
    )


def shape(*dims, kind=BF16):
    return jax.ShapeDtypeStruct(dims, kind)


def wide(row):
    return jnp.broadcast_to(row[None], (8, row.shape[0]))


def turn(v, table, sign):
    head = v[:, :128]
    other = pltpu.roll(head, 96, 1) * table[:, 128:256] + pltpu.roll(head, 32, 1) * table[:, 256:]
    return jnp.concatenate([head * table[:, :128] + sign * other, v[:, 128:]], 1)


def turn_table(where_at):
    half = ROT // 2
    frequency = jnp.exp(jnp.arange(half, dtype=F32) * (-2.0 * math.log(10000.0) / ROT))
    angles = where_at.astype(F32)[:, None] * frequency[None, :]
    c, s = jnp.cos(angles), jnp.sin(angles)
    rows = where_at.shape[0]
    one, none = jnp.ones((rows, 128 - ROT), F32), jnp.zeros((rows, 128 - half), F32)
    return jnp.concatenate([c, c, one, -s, none, none[:, :half], s, none[:, : 128 - ROT]], 1)


def norm_kernel(places, x_ref, gain_ref, first_ref, second_ref, x_out, stat_ref):
    x = x_ref[...].astype(F32)
    mean = jnp.mean(x, -1, keepdims=True)
    center = x - mean
    scale = lax.rsqrt(jnp.mean(center * center, -1, keepdims=True) + EPS)
    size = x_ref.shape[1] // len(places)
    for i, place in enumerate(places):
        at, to = pl.ds(pl.multiple_of(place() * size, size), size), pl.ds(i * size, size)
        part = x_ref[:, at]
        x_out[:, to] = part
        unit = (part.astype(F32) - mean) * scale
        first_ref[:, to] = (unit * gain_ref[0:1, at] + gain_ref[1:2, at]).astype(BF16)
        second_ref[:, to] = (unit * gain_ref[2:3, at] + gain_ref[3:4, at]).astype(BF16)
    lane = lax.broadcasted_iota(jnp.int32, stat_ref.shape, 1)
    stat_ref[...] = jnp.where(lane == 0, mean, scale)


def norms(x, gains, places):
    rows, width = x.shape
    block = pl.BlockSpec((128, width), lambda i: (i, 0))
    return call(
        partial(norm_kernel, places),
        (rows // 128,),
        [block, pl.BlockSpec((8, width), lambda i: (0, 0))],
        [block, block, block, pl.BlockSpec((128, 128), lambda i: (i, 0))],
        [shape(rows, width)] * 3 + [shape(rows, 128, kind=F32)],
        10 * rows * width,
        8 * rows * width,
        name="norms",
    )(x, gains)


def project_kernel(n_ref, w_ref, b_ref, table_ref, q_ref, kv_ref):
    head = q_ref.shape[1]
    for i in range(n_ref.shape[0] // ROWS):
        at = pl.ds(i * ROWS, ROWS)
        out = mul(n_ref[at, :], w_ref[...], NN) + b_ref[:1]
        q_ref[at, :] = turn(out[:, :head], table_ref[at, :], 1.0).astype(BF16)
        kv_ref[at, :head] = turn(out[:, head : 2 * head], table_ref[at, :], 1.0).astype(BF16)
        kv_ref[at, head:] = out[:, 2 * head :].astype(BF16)


def project(n, w, bias, table, heads):
    rows, depth = n.shape
    width = w.shape[1] // heads
    head = width // 3
    return call(
        project_kernel,
        (heads,),
        [
            pl.BlockSpec((rows, depth), lambda h: (0, 0)),
            pl.BlockSpec((depth, width), lambda h: (0, h)),
            pl.BlockSpec((8, width), lambda h: (0, h)),
            pl.BlockSpec((rows, 384), lambda h: (0, 0)),
        ],
        [pl.BlockSpec((rows, head), lambda h: (0, h)), pl.BlockSpec((rows, 2 * head), lambda h: (0, h))],
        [shape(rows, heads * head), shape(rows, heads * 2 * head)],
        2 * rows * depth * w.shape[1],
        2 * (rows * depth + w.size + rows * w.shape[1]),
        name="project",
    )(n, w, wide(bias), table)


def expand_kernel(n_ref, w_ref, b_ref, h_ref, d_ref):
    for i in range(n_ref.shape[0] // ROWS):
        at = pl.ds(i * ROWS, ROWS)
        pre = mul(n_ref[at, :], w_ref[...], NN) + b_ref[:1]
        below = 0.5 + 0.5 * lax.erf(pre * math.sqrt(0.5))
        h_ref[at, :] = (pre * below).astype(BF16)
        d_ref[at, :] = (below + pre * jnp.exp(-0.5 * pre * pre) * (1.0 / math.sqrt(2 * math.pi))).astype(BF16)


def expand(n, w, bias, tile=512):
    rows, depth = n.shape
    cols = w.shape[1]
    out = pl.BlockSpec((rows, tile), lambda j: (0, j))
    return call(
        expand_kernel,
        (cols // tile,),
        [
            pl.BlockSpec((rows, depth), lambda j: (0, 0)),
            pl.BlockSpec((depth, tile), lambda j: (0, j)),
            pl.BlockSpec((8, tile), lambda j: (0, j)),
        ],
        [out, out],
        [shape(rows, cols), shape(rows, cols)],
        2 * rows * depth * cols,
        2 * (rows * depth + w.size + 2 * rows * cols),
        2 * rows * cols,
        name="expand",
    )(n, w, wide(bias))


def attend_block(prompt, block, allow, segc_ref, segr, q_ref, ko, vo, kt, vt, o_ref, stat_ref):
    tq = q_ref.shape[0]
    first_cont = prompt // tq
    cont = ko.shape[0] - prompt
    q = q_ref[...] * BF16(1.0 / math.sqrt(q_ref.shape[1]))
    rows = lax.broadcasted_iota(jnp.int32, (tq, 1), 0)

    def finish(scores, values):
        top = reduce(jnp.maximum, [jnp.max(s, -1, keepdims=True) for s in scores])
        exps = [jnp.exp(s - top) for s in scores]
        total = sum(jnp.sum(e, -1, keepdims=True) for e in exps)
        out = sum(mul(e.astype(BF16), v, NN) for e, v in zip(exps, values))
        o_ref[...] = (out / total).astype(BF16)
        stat_ref[0] = jnp.transpose(jnp.broadcast_to(top + jnp.log(total), (tq, 128)))[:8]

    @pl.when(block < first_cont)
    def _():
        cols = lax.broadcasted_iota(jnp.int32, (1, prompt), 1)
        own = jnp.where(cols <= rows + block * tq, mul(q, ko[:prompt], NT), -1e30)
        spans = [pl.ds(i * prompt, prompt) for i in range(len(allow))]
        far = [mul(q, kt[at, :], NT) + add for at, add in zip(spans, allow)]
        finish([own, *far], [vo[:prompt], *(vt[at, :] for at in spans)])

    @pl.when(block >= first_cont)
    def _():
        cols = lax.broadcasted_iota(jnp.int32, (1, cont), 1)
        own = mul(q, ko[:prompt], NT)
        at = jnp.maximum(block - first_cont, 0) * tq
        segc = segc_ref[pl.ds(pl.multiple_of(at, tq), tq), :1]
        follow = jnp.where((cols <= rows + at) & (segc == segr), mul(q, ko[prompt:], NT), -1e30)
        far = mul(q, kt[...], NT)
        finish([own, follow, far], [vo[:prompt], vo[prompt:], vt[...]])


def sequence_places(prompt, holder, places_ref, rows):
    own = places_ref[0:1, pl.ds(pl.multiple_of(holder * rows, 128), 128)][:, :1]

    def allow(other):
        start = places_ref[0:1, pl.ds(pl.multiple_of(other * rows, 128), 128)][:, :1]
        return jnp.where(start < own, 0.0, -1e30)

    return allow


def down(row):
    return jnp.transpose(jnp.broadcast_to(row, (128, row.shape[1])))


def attend_kernel(prompt, bias_ref, segc_ref, segr_ref, *refs):
    allow = [bias_ref[i : i + 1, :1] for i in range(refs[3].shape[0] // prompt)]
    attend_block(prompt, pl.program_id(1), allow, segc_ref, segr_ref[:1], *refs)


def attend(q, kv, kv_far, bias, seg, prompt):
    rows, width = q.shape
    head = HEAD
    heads = width // head
    far = kv_far.shape[0]
    cont = rows - prompt
    tq = ROWS
    return call(
        partial(attend_kernel, prompt),
        (heads, rows // tq),
        [
            pl.BlockSpec((8, 128), lambda h, b: (0, 0)),
            pl.BlockSpec((cont, 128), lambda h, b: (0, 0)),
            pl.BlockSpec((8, cont), lambda h, b: (0, 0)),
            pl.BlockSpec((tq, head), lambda h, b: (b, h)),
            pl.BlockSpec((rows, head), lambda h, b: (0, 2 * h)),
            pl.BlockSpec((rows, head), lambda h, b: (0, 2 * h + 1)),
            pl.BlockSpec((far, head), lambda h, b: (0, 2 * h)),
            pl.BlockSpec((far, head), lambda h, b: (0, 2 * h + 1)),
        ],
        [pl.BlockSpec((tq, head), lambda h, b: (b, h)), pl.BlockSpec((1, 8, tq), lambda h, b: (h, 0, b))],
        [shape(rows, width), shape(heads, 8, rows, kind=F32)],
        4 * rows * (rows + far) * width,
        2 * (2 * q.size + kv.size + kv_far.size),
        rows * (rows + far) * heads,
        name="attend",
    )(bias, jnp.broadcast_to(seg[prompt:, None], (cont, 128)), wide(seg[prompt:]), q, kv, kv, kv_far, kv_far)


def attend_back_block(
    prompt, block, last, allow, segc, segr, q_ref, do_ref, o_ref, stat_ref, ko, vo, kt, vt, table_ref,
    dq_ref, own_ref, near_ref, far_ref, acc_k, acc_v,
):
    tq, head = q_ref.shape
    first_cont = prompt // tq
    scale = 1.0 / math.sqrt(head)
    q = q_ref[...] * BF16(scale)
    do = do_ref[...]
    inner = jnp.sum(do.astype(F32) * o_ref[...].astype(F32), -1, keepdims=True)
    inner = jnp.transpose(jnp.broadcast_to(inner, (tq, 128)))[:1]
    stat = stat_ref[0, :1]
    cols = lax.broadcasted_iota(jnp.int32, (1, tq), 1)

    @pl.when(block == 0)
    def _():
        acc_k[...] = jnp.zeros_like(acc_k)
        acc_v[...] = jnp.zeros_like(acc_v)

    def part(keys, values, at, seen):
        probs = jnp.exp(seen(mul(keys, q, NT)) - stat)
        grads = (probs * (mul(values, do, NT) - inner)).astype(BF16)
        acc_v[at, :] += mul(probs.astype(BF16), do, NN)
        acc_k[at, :] += mul(grads, q, NN)
        return mul(grads, keys, TN)

    def far_parts(total, seen):
        for i in range(kt.shape[0] // prompt):
            at = pl.ds(i * prompt, prompt)
            total += part(kt[at, :], vt[at, :], pl.ds(ko.shape[0] + i * prompt, prompt), partial(seen, i))
        dq_ref[...] = turn(total * scale, table_ref[...], -1.0).astype(BF16)

    @pl.when(block < first_cont)
    def _():
        rows = lax.broadcasted_iota(jnp.int32, (prompt, 1), 0)
        total = part(
            ko[:prompt], vo[:prompt], pl.ds(0, prompt), lambda s: jnp.where(rows <= cols + block * tq, s, -1e30)
        )
        far_parts(total, lambda i, s: s + allow[i])

    @pl.when(block >= first_cont)
    def _():
        cont = ko.shape[0] - prompt
        rows = lax.broadcasted_iota(jnp.int32, (cont, 1), 0)
        total = part(ko[:prompt], vo[:prompt], pl.ds(0, prompt), lambda s: s)
        read = (rows <= cols + (block - first_cont) * tq) & (segc() == segr())
        total += part(ko[prompt:], vo[prompt:], pl.ds(prompt, cont), lambda s: jnp.where(read, s, -1e30))
        far_parts(total, lambda i, s: s)

    @pl.when(block == last)
    def _():
        start = 0
        for ref in (own_ref, near_ref, far_ref):
            at = pl.ds(start, ref.shape[0])
            ref[:, :head] = acc_k[at, :].astype(ref.dtype)
            ref[:, head:] = acc_v[at, :].astype(ref.dtype)
            start += ref.shape[0]


def attend_back_kernel(prompt, bias_ref, segc_ref, segr_ref, *refs):
    allow = [bias_ref[i : i + 1, :1] for i in range(refs[6].shape[0] // prompt)]
    last = pl.num_programs(1) - 1
    attend_back_block(prompt, pl.program_id(1), last, allow, lambda: segc_ref[:, :1], lambda: segr_ref[:1], *refs)


def attend_back(q, do, o, stat, kv, kv_far, bias, seg, prompt, table):
    rows, width = q.shape
    head = HEAD
    heads = width // head
    far = kv_far.shape[0]
    cont = rows - prompt
    tq = ROWS
    first = prompt // tq
    row = pl.BlockSpec((tq, head), lambda h, b: (b, h))

    def column(n, odd):
        return pl.BlockSpec((n, head), lambda h, b: (0, 2 * h + odd))

    def pair(n):
        return pl.BlockSpec((n, 2 * head), lambda h, b: (0, h))

    return call(
        partial(attend_back_kernel, prompt),
        (heads, rows // tq),
        [
            pl.BlockSpec((8, 128), lambda h, b: (0, 0)),
            pl.BlockSpec((cont, 128), lambda h, b: (0, 0)),
            pl.BlockSpec((8, tq), lambda h, b: (0, jnp.maximum(b - first, 0))),
            row,
            row,
            row,
            pl.BlockSpec((1, 8, tq), lambda h, b: (h, 0, b)),
            column(rows, 0),
            column(rows, 1),
            column(far, 0),
            column(far, 1),
            pl.BlockSpec((tq, 384), lambda h, b: (b, 0)),
        ],
        [row, pair(rows), pair(prompt), pair(far - prompt)],
        [
            shape(rows, width),
            shape(rows, 2 * width, kind=F32),
            shape(prompt, 2 * width),
            shape(far - prompt, 2 * width),
        ],
        10 * rows * (rows + far) * width,
        2 * (4 * q.size + 4 * kv.size + 2 * kv_far.size),
        rows * (rows + far) * heads,
        [pltpu.VMEM((rows + far, head), F32), pltpu.VMEM((rows + far, head), F32)],
        name="attend_back",
    )(
        bias, jnp.broadcast_to(seg[prompt:, None], (cont, 128)), wide(seg[prompt:]),
        q, do, o, stat, kv, kv, kv_far, kv_far, table,
    )


def mixed_kernel(a_ref, h_ref, wa_ref, wh_ref, o_ref):
    for i in range(a_ref.shape[0] // ROWS):
        at = pl.ds(i * ROWS, ROWS)
        o_ref[at, :] = (mul(a_ref[at, :], wa_ref[...], NT) + mul(h_ref[at, :], wh_ref[...], NT)).astype(BF16)


def mixed_sum(attended, activated, w_out, w_contract, tile=512):
    rows = attended.shape[0]
    deep, deeper = attended.shape[1], activated.shape[1]
    width = w_out.shape[0]
    return call(
        mixed_kernel,
        (width // tile,),
        [
            pl.BlockSpec((rows, deep), lambda j: (0, 0)),
            pl.BlockSpec((rows, deeper), lambda j: (0, 0)),
            pl.BlockSpec((tile, deep), lambda j: (j, 0)),
            pl.BlockSpec((tile, deeper), lambda j: (j, 0)),
        ],
        pl.BlockSpec((rows, tile), lambda j: (0, j)),
        shape(rows, width),
        2 * rows * width * (deep + deeper),
        2 * (rows + width) * (deep + deeper) + 2 * rows * width,
        name="mixed_sum",
    )(attended, activated, w_out, w_contract)


def attended_grad_kernel(g_ref, w_ref, o_ref):
    for i in range(g_ref.shape[0] // ROWS):
        at = pl.ds(i * ROWS, ROWS)
        o_ref[at, :] = mul(g_ref[at, :], w_ref[...], NN).astype(BF16)


def attended_grads(g, w, tile=256):
    rows, depth = g.shape
    cols = w.shape[1]
    return call(
        attended_grad_kernel,
        (cols // tile,),
        [pl.BlockSpec((rows, depth), lambda j: (0, 0)), pl.BlockSpec((depth, tile), lambda j: (0, j))],
        pl.BlockSpec((rows, tile), lambda j: (0, j)),
        shape(rows, cols),
        2 * rows * depth * cols,
        2 * (rows * depth + w.size + rows * cols),
        name="attended_grads",
    )(g, w)


def hidden_grad_kernel(g_ref, w_ref, d_ref, gp_ref, sum_ref):
    total = 0.0
    for i in range(g_ref.shape[0] // ROWS):
        at = pl.ds(i * ROWS, ROWS)
        grad = (mul(g_ref[at, :], w_ref[...], NN) * d_ref[at, :].astype(F32)).astype(BF16)
        gp_ref[at, :] = grad
        total += jnp.sum(grad.astype(F32), 0, keepdims=True)
    sum_ref[...] = jnp.broadcast_to(total, sum_ref.shape)


def hidden_grads(g, w, slope, tile=512):
    rows, depth = g.shape
    cols = w.shape[1]
    tall = pl.BlockSpec((rows, tile), lambda j: (0, j))
    return call(
        hidden_grad_kernel,
        (cols // tile,),
        [pl.BlockSpec((rows, depth), lambda j: (0, 0)), pl.BlockSpec((depth, tile), lambda j: (0, j)), tall],
        [tall, pl.BlockSpec((8, tile), lambda j: (0, j))],
        [shape(rows, cols), shape(8, cols, kind=F32)],
        2 * rows * depth * cols,
        2 * (rows * depth + w.size + 2 * rows * cols),
        name="hidden_grads",
    )(g, w, slope)


def pack_kernel(prompt_blocks, q_ref, own_ref, near_ref, far_ref, table_ref, o_ref, sum_ref):
    block = pl.program_id(1)
    head = q_ref.shape[1]
    theirs = near_ref[...].astype(F32) + far_ref[...].astype(F32)
    both = own_ref[...] + jnp.where(block < prompt_blocks, theirs, 0.0)
    out = [q_ref[...], turn(both[:, :head], table_ref[...], -1.0).astype(BF16), both[:, head:].astype(BF16)]

    @pl.when(block == 0)
    def _():
        sum_ref[...] = jnp.zeros_like(sum_ref)

    for i, part in enumerate(out):
        o_ref[:, i * head : (i + 1) * head] = part
        sum_ref[:, i * head : (i + 1) * head] += jnp.sum(part.astype(F32), 0, keepdims=True)


def pack(dq, own, near, far, table, prompt):
    rows, width = dq.shape
    head = HEAD
    heads = width // head
    tq = ROWS
    blocks = prompt // tq
    theirs = pl.BlockSpec((tq, 2 * head), lambda h, b: (jnp.minimum(b, blocks - 1), h))
    return call(
        partial(pack_kernel, blocks),
        (heads, rows // tq),
        [
            pl.BlockSpec((tq, head), lambda h, b: (b, h)),
            pl.BlockSpec((tq, 2 * head), lambda h, b: (b, h)),
            theirs,
            theirs,
            pl.BlockSpec((tq, 384), lambda h, b: (b, 0)),
        ],
        [pl.BlockSpec((tq, 3 * head), lambda h, b: (b, h)), pl.BlockSpec((8, 3 * head), lambda h, b: (0, h))],
        [shape(rows, 3 * width), shape(8, 3 * width, kind=F32)],
        10 * rows * width,
        16 * rows * width,
        name="pack",
    )(dq, own, near, far, table)


def unit_grad_kernel(gp_ref, gh_ref, wa_ref, we_ref, x_ref, stat_ref, gain_ref, e_ref, sum_ref):
    sums = [0.0] * 4
    for i in range(gp_ref.shape[0] // ROWS):
        at = pl.ds(i * ROWS, ROWS)
        first = mul(gp_ref[at, :], wa_ref[...], NT)
        second = mul(gh_ref[at, :], we_ref[...], NT)
        e_ref[at, :] = (first * gain_ref[0:1] + second * gain_ref[2:3]).astype(BF16)
        unit = (x_ref[at, :].astype(F32) - stat_ref[at, 0:1]) * stat_ref[at, 1:2]
        for j, v in enumerate((first * unit, first, second * unit, second)):
            sums[j] += jnp.sum(v, 0, keepdims=True)
    for j in range(4):
        sum_ref[j : j + 1] = sums[j]
    sum_ref[4:] = jnp.zeros_like(sum_ref[4:])


def unit_grads(gp, gh, w_attend, w_expand, x, stat, gains, tile=512):
    rows, width = x.shape
    deep, deeper = gp.shape[1], gh.shape[1]
    col = pl.BlockSpec((rows, tile), lambda j: (0, j))
    row = pl.BlockSpec((8, tile), lambda j: (0, j))
    return call(
        unit_grad_kernel,
        (width // tile,),
        [
            pl.BlockSpec((rows, deep), lambda j: (0, 0)),
            pl.BlockSpec((rows, deeper), lambda j: (0, 0)),
            pl.BlockSpec((tile, deep), lambda j: (j, 0)),
            pl.BlockSpec((tile, deeper), lambda j: (j, 0)),
            col,
            pl.BlockSpec((rows, 128), lambda j: (0, 0)),
            row,
        ],
        [col, row],
        [shape(rows, width), shape(8, width, kind=F32)],
        2 * rows * width * (deep + deeper),
        2 * (rows + width) * (deep + deeper) + 4 * rows * width,
        name="unit_grads",
    )(gp, gh, w_attend, w_expand, x, stat, gains)


def far_kernel(a_ref, b_ref, o_ref):
    for i in range(o_ref.shape[0] // ROWS):
        o_ref[pl.ds(i * ROWS, ROWS), :] = mul(a_ref[:, pl.ds(i * ROWS, ROWS)], b_ref[...], TN).astype(BF16)


def near_kernel(a_ref, b_ref, r_ref, *outs):
    size = a_ref.shape[1] // len(outs)
    for i, out in enumerate(outs):
        at = pl.ds(i * size, size)
        out[...] = (mul(a_ref[:, at], b_ref[...], TN) + r_ref[at, :].astype(F32)).astype(out.dtype)


class Hops:
    def __init__(self, send, recv, pairs=False):
        self.send, self.recv, self.made = send, recv, []
        f, c, t = (lax.axis_index(a) for a in ("fsdp", "ctx", "tp"))
        ring = lax.axis_size("tp")
        self.to = {
            "x": {"fsdp": 1 - f},
            "y": {"ctx": (c + 2) % 4},
            "core": {"ctx": c + 1 - 2 * (c % 2)},
            "up": {"tp": (t + 1) % ring},
        }
        self.back = {"tp": (t + ring - 1) % ring}
        if pairs:
            self.to["t1"] = {"tp": t + 1 - 2 * (t % 2)}
            self.to["t2"] = {"tp": t + 2 - 4 * (t // 2 % 2)}

    def greet(self):
        barrier = pltpu.get_barrier_semaphore()
        near = [*self.to.values(), self.back]
        for device in near:
            pl.semaphore_signal(barrier, inc=1, device_id=device, device_id_type=pl.DeviceIdType.MESH)
        pl.semaphore_wait(barrier, len(near))

    def copy(self, way, src, dst):
        i = len(self.made)
        self.made.append(
            pltpu.make_async_remote_copy(
                src,
                dst,
                self.send.at[i],
                self.recv.at[i],
                device_id=self.to[way],
                device_id_type=pl.DeviceIdType.MESH,
            )
        )
        return self.made[-1]

    def end(self):
        for copy in self.made:
            copy.wait_send()


class Block:
    def __init__(self, hops, part, whole, halves=1):
        size = part.shape[0]
        half, piece = size // 2, size // halves

        def at(slot, start=0, rows=size):
            return whole.at[pl.ds(slot * size + start, rows)]

        self.first = [
            [
                hops.copy(way, part.at[pl.ds(i * piece, piece)], at(slot, i * piece, piece))
                for way, slot in (("x", 1), ("y", 2))
            ]
            for i in range(halves)
        ]
        self.corner = [
            hops.copy("x", at(2, 0, half), at(3, 0, half)),
            hops.copy("y", at(1, half, half), at(3, half, half)),
        ]
        self.core = [hops.copy("core", part if slot == 0 else at(slot), at(4 + slot)) for slot in range(4)]


def start(copies):
    for copy in copies:
        copy.start()


def arrive(copies):
    for copy in copies:
        copy.wait_recv()


def table_kernel(pos_ref, freq_ref, o_ref):
    angle = down(pos_ref[...].astype(F32)) * freq_ref[:1]
    c, s = jnp.cos(angle), jnp.sin(angle)
    lane = lax.broadcasted_iota(jnp.int32, angle.shape, 1)
    half = ROT // 2
    o_ref[:, :128] = jnp.where(lane < ROT, c, 1.0)
    o_ref[:, 128:256] = jnp.where(lane < half, -s, 0.0)
    o_ref[:, 256:] = jnp.where((lane >= half) & (lane < ROT), s, 0.0)


def norm_block_kernel(x_ref, gain_ref, first_ref, second_ref, stat_ref):
    x = x_ref[...].astype(F32)
    mean = jnp.mean(x, -1, keepdims=True)
    center = x - mean
    scale = lax.rsqrt(jnp.mean(center * center, -1, keepdims=True) + EPS)
    unit = center * scale
    first_ref[...] = (unit * gain_ref[0:1] + gain_ref[1:2]).astype(BF16)
    second_ref[...] = (unit * gain_ref[2:3] + gain_ref[3:4]).astype(BF16)
    lane = lax.broadcasted_iota(jnp.int32, stat_ref.shape, 1)
    stat_ref[...] = jnp.where(lane == 0, mean, scale)


def project_block_kernel(n_ref, w_ref, b_ref, table_ref, q_ref, kv_ref):
    head = q_ref.shape[1]
    out = mul(n_ref[...], w_ref[...], NN) + b_ref[:1]
    q_ref[...] = turn(out[:, :head], table_ref[...], 1.0).astype(BF16)
    kv_ref[:, :head] = turn(out[:, head : 2 * head], table_ref[...], 1.0).astype(BF16)
    kv_ref[:, head:] = out[:, 2 * head :].astype(BF16)


def expand_block_kernel(n_ref, w_ref, b_ref, h_ref, d_ref):
    pre = mul(n_ref[...], w_ref[...], NN) + b_ref[:1]
    below = 0.5 + 0.5 * lax.erf(pre * math.sqrt(0.5))
    h_ref[...] = (pre * below).astype(BF16)
    d_ref[...] = (below + pre * jnp.exp(-0.5 * pre * pre) * (1.0 / math.sqrt(2 * math.pi))).astype(BF16)


def forward_kernel(places, prompt, *refs):
    (
        x_ref, g_ref, wa, we, wo, wc, gain_1, gain_2, gain_3, gain_4, bias_a, bias_e, seg_ref, pos_ref, freq_ref,
        rows_in, rows_grad, gains, attend_all, expand_all, output_all, contract_all,
        first, second, stat, table, queries, pairs, pairs_far, activated, slope, attended, row_sums, mixed, grad_sum,
        send, recv, local, held_x, held_g, held_gains, held_sum, held_seg, held_pos, segc, gain_rows, *held,
    ) = refs
    hops = Hops(send, recv)
    t, ring = lax.axis_index("tp"), lax.axis_size("tp")
    rows, width = x_ref.shape
    total = rows * ring
    block = width // len(places)
    chunk = rows // 2

    here = pl.ds(t * rows, rows)
    moves = [(x_ref, held_x, rows_in.at[here]), (g_ref, held_g, rows_grad.at[here])]
    loads, stores, count = [], [], 0
    for src, mid, dst in moves:
        loads.append([])
        for i, place in enumerate(places):
            at = pl.ds(pl.multiple_of(place() * block, block), block)
            loads[-1].append(pltpu.make_async_copy(src.at[:, at], mid.at[:, pl.ds(i * block, block)], local.at[count]))
            count += 1
        stores.append(pltpu.make_async_copy(mid, dst, local.at[count]))
        count += 1
    small = [pltpu.make_async_copy(seg_ref, held_seg, local.at[count]), pltpu.make_async_copy(pos_ref, held_pos, local.at[count + 1])]
    count += 2
    for i, src in enumerate((gain_1, gain_2, gain_3, gain_4)):
        small.append(pltpu.make_async_copy(src, gain_rows.at[i], local.at[count]))
        count += 1
    for src, mid, whole in zip((wa, we, wo, wc), held, (attend_all, expand_all, output_all, contract_all)):
        loads.append([pltpu.make_async_copy(src, mid, local.at[count])])
        stores.append(pltpu.make_async_copy(mid, whole.at[pl.ds(0, src.shape[0])], local.at[count + 1]))
        count += 2

    def rings(ref, held_rows):
        made = {}
        for step in range(ring - 1):
            for half in range(2):
                at = ref.at[pl.ds(((t + ring - step) % ring) * rows + half * chunk, chunk)]
                src = held_rows.at[pl.ds(half * chunk, chunk)] if step == 0 else at
                made[step, half] = hops.copy("up", src, at)
        return made

    ring_x, ring_g = rings(rows_in, held_x), rings(rows_grad, held_g)
    a, e, o = (Block(hops, part, whole) for part, whole in ((wa, attend_all), (we, expand_all), (wo, output_all)))
    c = Block(hops, wc, contract_all, 2)
    own_pairs = pairs.at[pl.ds(0, prompt)]
    far = [pairs_far.at[pl.ds(i * prompt, prompt)] for i in range(3)]
    pair_y, pair_core = hops.copy("y", own_pairs, far[0]), hops.copy("core", own_pairs, far[1])
    pair_corner = hops.copy("core", far[0], far[2])

    def forward(copies, step, half):
        arrive([copies[step, half]])
        if step < ring - 2:
            start([copies[step + 1, half]])

    head = HEAD
    heads = queries.shape[1] // head

    def span(step):
        return pl.ds(((t + ring - step) % ring) * rows, rows)

    def norm(step):
        tile = 128
        row = pl.BlockSpec((tile, width), lambda i: (i, 0))
        pltpu.emit_pipeline(
            norm_block_kernel,
            grid=(rows // tile,),
            in_specs=[row, pl.BlockSpec((8, width), lambda i: (0, 0))],
            out_specs=[row, row, pl.BlockSpec((tile, 128), lambda i: (i, 0))],
        )(rows_in.at[span(step)], gains, first.at[span(step)], second.at[span(step)], stat.at[span(step)])

    def project(step):
        pltpu.emit_pipeline(
            project_block_kernel,
            grid=(heads,),
            in_specs=[
                pl.BlockSpec((rows, width), lambda h: (0, 0)),
                pl.BlockSpec((width, 3 * head), lambda h: (0, h)),
                pl.BlockSpec((1, 3 * head), lambda h: (0, h)),
                pl.BlockSpec((rows, 384), lambda h: (0, 0)),
            ],
            out_specs=[pl.BlockSpec((rows, head), lambda h: (0, h)), pl.BlockSpec((rows, 2 * head), lambda h: (0, h))],
        )(first.at[span(step)], attend_all, bias_a, table.at[span(step)], queries.at[span(step)], pairs.at[span(step)])

    def expand(pumps):
        tile = 512
        out = pl.BlockSpec((total, tile), lambda j: (0, j))

        def body(n_ref, w_ref, b_ref, h_ref, d_ref):
            for when, pump in pumps.items():
                pl.when(pl.program_id(0) == when)(pump)
            for i in range(ring):
                at = pl.ds(i * rows, rows)
                expand_block_kernel(n_ref.at[at], w_ref, b_ref, h_ref.at[at], d_ref.at[at])

        pltpu.emit_pipeline(
            body,
            grid=(expand_all.shape[1] // tile,),
            in_specs=[
                pl.BlockSpec((total, width), lambda j: (0, 0)),
                pl.BlockSpec((width, tile), lambda j: (0, j)),
                pl.BlockSpec((1, tile), lambda j: (0, j)),
            ],
            out_specs=[out, out],
        )(second, expand_all, bias_e, activated, slope)

    for load in loads:
        start(load)
    start(small)
    hops.greet()
    start(a.first[0])
    start([a.core[0]])
    for i, (load, store) in enumerate(zip(loads, stores)):
        for copy in load:
            copy.wait()
        store.start()
        if i == 0:
            start([ring_x[0, 0], ring_x[0, 1], e.core[0]])
    for copy in small:
        copy.wait()
    held_gains[...] = jnp.zeros_like(held_gains)
    for i, place in enumerate(places):
        at = pl.ds(pl.multiple_of(place() * block, block), block)
        for k in range(4):
            held_gains[k : k + 1, i * block : (i + 1) * block] = gain_rows[k, :, at]
    gains_out = pltpu.make_async_copy(held_gains, gains, local.at[count + 1])
    gains_out.start()
    holder = lax.axis_index("ctx")
    after_prompt = pl.ds(pl.multiple_of(holder * total + prompt, 128), total - prompt)
    segc[...] = down(held_seg[0:1, after_prompt])
    allow_of = sequence_places(prompt, holder, held_pos, total)
    c_bits = holder // 2, holder % 2
    others = [((c_bits[0] + b) % 2) * 2 + (c_bits[1] + d) % 2 for b, d in ((1, 0), (0, 1), (1, 1))]
    held_sum[...] = jnp.broadcast_to(jnp.sum(held_g[...].astype(F32), 0, keepdims=True), held_sum.shape)
    sum_out = pltpu.make_async_copy(held_sum, grad_sum, local.at[count])
    sum_out.start()
    for store in stores + [sum_out, gains_out]:
        store.wait()
    pltpu.emit_pipeline(
        table_kernel,
        grid=(total // rows,),
        in_specs=[pl.BlockSpec((1, rows), lambda i: (0, holder * ring + i)), pl.BlockSpec((8, 128), lambda i: (0, 0))],
        out_specs=[pl.BlockSpec((rows, 384), lambda i: (i, 0))],
    )(pos_ref, freq_ref, table)
    norm(0)
    forward(ring_x, 0, 0)
    start(e.first[0])
    arrive(a.first[0])
    start(a.corner + a.core[1:3])
    forward(ring_x, 0, 1)
    norm(1)
    forward(ring_x, 1, 0)
    arrive(a.corner)
    start([a.core[3]])
    arrive(e.first[0])
    start(e.corner + e.core[1:3] + o.first[0] + [o.core[0]] + c.first[0] + c.first[1] + [c.core[0]])
    forward(ring_x, 1, 1)
    start([ring_g[0, 0], ring_g[0, 1]])
    norm(2)
    arrive(a.core)
    project(0)
    forward(ring_x, 2, 0)
    arrive(e.corner)
    start([e.core[3]])
    project(1)
    project(2)
    arrive(o.first[0])
    start(o.core[1:3])
    forward(ring_x, 2, 1)
    norm(3)
    project(3)
    start([pair_y, pair_core])
    arrive(e.core)

    def others_on():
        for copies in c.first:
            arrive(copies)
        start(c.core[1:3])

    expand({0: lambda: forward(ring_g, 0, 0), 2: others_on, 3: lambda: forward(ring_g, 0, 1)})
    arrive([pair_y])
    start([pair_corner] + o.corner + c.corner)
    arrive([pair_core, pair_corner])

    def attend_step(*args):
        step = pl.program_id(0) * pl.num_programs(1) + pl.program_id(1)
        pl.when(step == 1)(lambda: forward(ring_g, 1, 0))
        pl.when(step == 6)(lambda: forward(ring_g, 1, 1))
        attend_block(prompt, pl.program_id(1), [allow_of(i) for i in others], segc, held_seg[0:1, after_prompt], *args)

    tq = ROWS
    n_far = pairs_far.shape[0]
    pltpu.emit_pipeline(
        attend_step,
        grid=(heads, total // tq),
        in_specs=[
            pl.BlockSpec((tq, head), lambda h, b: (b, h)),
            pl.BlockSpec((total, head), lambda h, b: (0, 2 * h)),
            pl.BlockSpec((total, head), lambda h, b: (0, 2 * h + 1)),
            pl.BlockSpec((n_far, head), lambda h, b: (0, 2 * h)),
            pl.BlockSpec((n_far, head), lambda h, b: (0, 2 * h + 1)),
        ],
        out_specs=[pl.BlockSpec((tq, head), lambda h, b: (b, h)), pl.BlockSpec((1, 8, tq), lambda h, b: (h, 0, b))],
    )(queries, pairs, pairs, pairs_far, pairs_far, attended, row_sums)

    arrive(o.corner + c.corner)
    start([o.core[3], c.core[3]])
    forward(ring_g, 2, 0)
    arrive(o.core + c.core)
    tile = 512
    pltpu.emit_pipeline(
        mixed_kernel,
        grid=(width // tile,),
        in_specs=[
            pl.BlockSpec((total, attended.shape[1]), lambda j: (0, 0)),
            pl.BlockSpec((total, activated.shape[1]), lambda j: (0, 0)),
            pl.BlockSpec((tile, attended.shape[1]), lambda j: (j, 0)),
            pl.BlockSpec((tile, activated.shape[1]), lambda j: (j, 0)),
        ],
        out_specs=[pl.BlockSpec((total, tile), lambda j: (0, j))],
    )(attended, activated, output_all, contract_all, mixed)
    forward(ring_g, 2, 1)
    hops.end()


def forward_pass(places, prompt, heads, x, g, weights, gains, bias_a, bias_e, segments, positions):
    ring = lax.axis_size("tp")
    rows, width = x.shape
    total = ring * rows
    wa, we, wo, wc = weights
    head = HEAD
    hidden = we.shape[1]
    freq = 10000.0 ** (-2.0 * (np.arange(128) % (ROT // 2)) / ROT)
    freq = jnp.asarray(np.tile(freq.astype(np.float32)[None], (8, 1)))
    inputs = [x, g, wa, we, wo, wc, *gains, bias_a, bias_e, segments, positions, freq]
    outs = [
        shape(total, width), shape(total, width), shape(8, width, kind=F32),
        *(shape(8 * w.shape[0], w.shape[1]) for w in (wa, we, wo, wc)),
        shape(total, width), shape(total, width), shape(total, 128, kind=F32), shape(total, 384, kind=F32),
        shape(total, heads * head), shape(total, 2 * heads * head), shape(3 * prompt, 2 * heads * head),
        shape(total, hidden), shape(total, hidden), shape(total, heads * head), shape(heads, 8, total, kind=F32),
        shape(total, width), shape(8, width, kind=F32),
    ]
    copies = 4 * (ring - 1) + 34 + 3
    ref = pl.BlockSpec(memory_space=pl.ANY)
    return pl.pallas_call(
        partial(forward_kernel, places, prompt),
        in_specs=[ref] * len(inputs),
        out_specs=[ref] * len(outs),
        out_shape=outs,
        scratch_shapes=[
            pltpu.SemaphoreType.DMA((copies,)),
            pltpu.SemaphoreType.DMA((copies,)),
            pltpu.SemaphoreType.DMA((2 * len(places) + 18,)),
            pltpu.VMEM(x.shape, BF16),
            pltpu.VMEM(g.shape, BF16),
            pltpu.VMEM((8, width), F32),
            pltpu.VMEM((8, width), F32),
            pltpu.VMEM(segments.shape, jnp.int32),
            pltpu.VMEM(positions.shape, jnp.int32),
            pltpu.VMEM((total - prompt, 128), jnp.int32),
            pltpu.VMEM((4, 1, width), F32),
            *(pltpu.VMEM(w.shape, BF16) for w in weights),
        ],
        compiler_params=pltpu.CompilerParams(collective_id=0, has_side_effects=True, vmem_limit_bytes=56 * 2**20),
        cost_estimate=pl.CostEstimate(flops=40 * 10**9, bytes_accessed=200 * 2**20, transcendentals=10**7),
        name="forward_pass",
    )(*inputs)


class RingSum:
    def __init__(self, hops, copies, source, landing, held, last):
        t, ring = lax.axis_index("tp"), lax.axis_size("tp")
        rows = last.shape[0]
        half = rows // 2
        self.sends, self.loads, self.adds = {}, {}, {}
        for h in range(2):
            part = pl.ds(h * half, half)
            for step in range(ring - 1):
                mine = source.at[pl.ds(((t + 2 * ring - 1 - step) % ring) * rows + h * half, half)]
                src = landing[step - 1].at[part] if step else mine
                if step:
                    if held:
                        self.loads[step, h] = copies(mine, held[step - 1].at[part])
                        mine = held[step - 1].at[part]
                    self.adds[step, h] = (src, mine)
                dst = landing[step].at[part] if step < ring - 2 else last.at[part]
                self.sends[step, h] = hops.copy("up", src, dst)

    def begin(self):
        start(self.sends[0, h] for h in range(2))
        start(self.loads.values())

    def pump(self, step, h):
        arrive([self.sends[step - 1, h]])
        if self.loads:
            self.loads[step, h].wait()
        here, own = self.adds[step, h]
        here[...] = (here[...].astype(F32) + own[...].astype(F32)).astype(BF16)
        start([self.sends[step, h]])

    def finish(self, h):
        arrive([self.sends[max(step for step, _ in self.sends), h]])


class Sums:
    def __init__(self, hops, r, i):
        to_x, to_y, corner = r.to_x[i], r.to_y[i], r.corner[i]
        half = corner.shape[0] // 2
        top, low = pl.ds(0, half), pl.ds(half, half)
        self.core = hops.copy("core", r.far[i], r.core[i])
        self.corner = [hops.copy("x", corner.at[top], r.via_x[i]), hops.copy("y", corner.at[low], r.via_y[i])]
        self.plain = [hops.copy("x", to_x.at[top], r.from_x[i].at[top]), hops.copy("y", to_y.at[low], r.from_y[i].at[low])]
        self.merged = [hops.copy("x", to_x.at[low], r.from_x[i].at[low]), hops.copy("y", to_y.at[top], r.from_y[i].at[top])]
        self.pairs = [
            (self.corner[1], to_x.at[low], r.via_y[i], self.merged[0]),
            (self.corner[0], to_y.at[top], r.via_x[i], self.merged[1]),
        ]

    def merge(self):
        for came, mine, theirs, send in self.pairs:
            arrive([came])
            mine[...] = (mine[...].astype(F32) + theirs[...].astype(F32)).astype(BF16)
            start([send])

    def finish(self):
        arrive(self.plain + self.merged)


def backward_kernel(names, places, prompt, *refs):
    r = SimpleNamespace()
    for name, ref in zip(names, refs):
        if name[-1].isdigit():
            getattr(r, name[:-1]).append(ref) if hasattr(r, name[:-1]) else setattr(r, name[:-1], [ref])
        else:
            setattr(r, name, ref)
    hops = Hops(r.send, r.recv, True)
    made = []

    def local_copy(src, dst):
        made.append(pltpu.make_async_copy(src, dst, r.local.at[len(made)]))
        return made[-1]

    t, ring = lax.axis_index("tp"), lax.axis_size("tp")
    total, width = r.rows_grad.shape
    rows = total // ring
    head = HEAD
    heads = r.queries.shape[1] // head
    tq = ROWS
    cont = total - prompt
    n_far = r.pairs_far.shape[0]
    first_cont = prompt // tq
    blocks = total // tq
    holder = lax.axis_index("ctx")
    c_bits = holder // 2, holder % 2
    others = [((c_bits[0] + b) % 2) * 2 + (c_bits[1] + d) % 2 for b, d in ((1, 0), (0, 1), (1, 1))]
    seq_start = holder * total + prompt

    sum_out = RingSum(hops, local_copy, r.mixed, r.land_out, r.held_out, r.out_recv)
    sum_unit = RingSum(hops, local_copy, r.unit, r.land_unit, None, r.unit_recv)
    pair_core = [hops.copy("core", r.pair_far.at[h], r.pair_core.at[h]) for h in range(heads)]
    pair_y = [hops.copy("y", r.pair_near.at[h], r.pair_recv.at[h]) for h in range(heads)]
    grads = {w: Sums(hops, r, i) for i, w in enumerate("aeoc")}
    vector_hops = [
        hops.copy(way, r.vals.at[i, pl.ds(0, n)], r.got.at[i, pl.ds(0, n)])
        for i, (way, n) in enumerate((("core", 8), ("x", 8), ("y", 8), ("t1", 8), ("t2", 8)))
    ]
    vectors_out = local_copy(r.vals.at[len(vector_hops)], r.vectors)
    sum_load = local_copy(r.grad_sum, r.held_sum)
    grad_load = local_copy(r.rows_grad, r.grad)
    small = [local_copy(r.segments, r.held_seg), local_copy(r.positions, r.held_pos)]
    half = width // 2
    tile = 512

    def pumped(pumps):
        for when, pump in pumps.items():
            pl.when(pl.program_id(0) == when)(pump)

    def back_to_rows():
        cols = 256

        def body(w_ref, o_ref):
            for i in range(total // ROWS):
                at = pl.ds(i * ROWS, ROWS)
                o_ref[at, :] = mul(r.grad[at, :], w_ref[...], NN).astype(BF16)

        pltpu.emit_pipeline(
            body,
            grid=(heads * head // cols,),
            in_specs=[pl.BlockSpec((width, cols), lambda j: (0, j))],
            out_specs=[pl.BlockSpec((total, cols), lambda j: (0, j))],
        )(r.output_all, r.grad_att)

    def attention(pumps):
        def body(*args):
            h, block = pl.program_id(0), pl.program_id(1)
            for (at_h, at_b), pump in pumps.items():
                pl.when((h == at_h) & (block == at_b))(pump)
            outs = (r.pair_own.at[h], r.pair_near.at[h], r.pair_far.at[h])
            at = pl.multiple_of(seq_start + jnp.maximum(block - first_cont, 0) * tq, 128)
            allow_of = sequence_places(prompt, holder, r.held_pos, total)
            attend_back_block(
                prompt, block, blocks - 1, [allow_of(i) for i in others], lambda: r.segc[:, :1],
                lambda: r.held_seg[0:1, pl.ds(at, tq)], *args, *outs, r.acc_k, r.acc_v,
            )
            for k in range(heads):
                pl.when((h == k) & (block == blocks - 1))(lambda: start([pair_core[k]]))

        row = pl.BlockSpec((tq, head), lambda h, b: (b, h))

        def column(n, odd):
            return pl.BlockSpec((n, head), lambda h, b: (0, 2 * h + odd))

        pltpu.emit_pipeline(
            body,
            grid=(heads, blocks),
            in_specs=[
                row,
                row,
                row,
                pl.BlockSpec((1, 8, tq), lambda h, b: (h, 0, b)),
                column(total, 0),
                column(total, 1),
                column(n_far, 0),
                column(n_far, 1),
                pl.BlockSpec((tq, 384), lambda h, b: (b, 0)),
            ],
            out_specs=[row],
        )(
            r.queries, r.grad_att, r.attended, r.row_sums, r.pairs, r.pairs, r.pairs_far, r.pairs_far, r.table, r.grad_q,
        )

    def pair_on(h):
        arrive([pair_core[h]])
        near, theirs = r.pair_near.at[h], r.pair_core.at[h, pl.ds(prompt, prompt)]
        near[...] = (near[...].astype(F32) + theirs[...].astype(F32)).astype(BF16)
        start([pair_y[h]])

    def hidden(pumps={}):
        def body(w_ref, d_ref, gp_ref):
            pumped(pumps)
            j = pl.program_id(0)
            sums = 0.0
            for i in range(total // ROWS):
                at = pl.ds(i * ROWS, ROWS)
                grad = (mul(r.grad[at, :], w_ref[...], NN) * d_ref[at, :].astype(F32)).astype(BF16)
                gp_ref[at, :] = grad
                sums += jnp.sum(grad.astype(F32), 0, keepdims=True)
            r.vals[0, 6:7, pl.ds(pl.multiple_of(j * tile, tile), tile)] = sums

        tall = pl.BlockSpec((total, tile), lambda j: (0, j))
        pltpu.emit_pipeline(
            body,
            grid=(r.grad_pre.shape[1] // tile,),
            in_specs=[pl.BlockSpec((width, tile), lambda j: (0, j)), tall],
            out_specs=[tall],
        )(r.contract_all, r.slope, r.grad_pre)

    def far_tile(left, right, out):
        for i in range(half // ROWS):
            out[pl.ds(i * ROWS, ROWS), :] = mul(left[:, pl.ds(i * ROWS, ROWS)], right[...], TN).astype(BF16)

    def near_tile(left, right, received, own, outs, j):
        size = half // 4
        cols = pl.ds(pl.multiple_of(j * tile, tile), tile)
        for i in range(4):
            at = pl.ds(i * size, size)
            out = mul(left[:, at], right[...], TN) + received[at, :].astype(F32)
            if i:
                outs[i - 1][:, cols] = out.astype(BF16)
            else:
                own[...] = out

    def stays(i):
        return (r.to_x[i], r.to_y[i], r.corner[i])

    def far_both(pumps={}):
        steps = r.activated.shape[1] // tile

        def body(h_ref, a_ref, c_out, o_out):
            pumped(pumps)
            j = pl.program_id(0)
            left = r.grad.at[:, pl.ds(half, half)]
            pl.when(j < steps)(lambda: far_tile(left, h_ref, c_out))
            pl.when(j == steps)(lambda: far_tile(left, a_ref, o_out))

        pltpu.emit_pipeline(
            body,
            grid=(steps + 1,),
            in_specs=[
                pl.BlockSpec((total, tile), lambda j: (0, jnp.minimum(j, steps - 1))),
                pl.BlockSpec((total, tile), lambda j: (0, 0)),
            ],
            out_specs=[
                pl.BlockSpec((half, tile), lambda j: (0, jnp.minimum(j, steps - 1))),
                pl.BlockSpec((half, tile), lambda j: (0, 0)),
            ],
        )(r.activated, r.attended, r.far[3], r.far[2])
        start([grads["c"].core, grads["o"].core])

    def near_both(pumps={}):
        steps = r.activated.shape[1] // tile
        arrive([grads["c"].core, grads["o"].core])

        def body(h_ref, a_ref, c_in, o_in, c_own, o_own):
            pumped(pumps)
            j = pl.program_id(0)
            left = r.grad.at[:, pl.ds(0, half)]
            pl.when(j < steps)(lambda: near_tile(left, h_ref, c_in, c_own, stays(3), jnp.minimum(j, steps - 1)))
            pl.when(j == steps)(lambda: near_tile(left, a_ref, o_in, o_own, stays(2), 0))

        def wide_tile(rows):
            return pl.BlockSpec((rows, tile), lambda j: (0, jnp.minimum(j, steps - 1)))

        def one_tile(rows):
            return pl.BlockSpec((rows, tile), lambda j: (0, 0))

        pltpu.emit_pipeline(
            body,
            grid=(steps + 1,),
            in_specs=[wide_tile(total), one_tile(total), wide_tile(half), one_tile(half)],
            out_specs=[wide_tile(half // 4), one_tile(half // 4)],
        )(r.activated, r.attended, r.core[3], r.core[2], r.own[3], r.own[2])

    def far(i, left, right, pumps={}):
        def body(a_ref, b_ref, out):
            pumped(pumps)
            far_tile(a_ref, b_ref, out)

        pltpu.emit_pipeline(
            body,
            grid=(right.shape[1] // tile,),
            in_specs=[pl.BlockSpec((total, half), lambda j: (0, 1)), pl.BlockSpec((total, tile), lambda j: (0, j))],
            out_specs=[pl.BlockSpec((half, tile), lambda j: (0, j))],
        )(left, right, r.far[i])

    def near(i, left, right, pumps={}):
        def body(a_ref, b_ref, received, own):
            pumped(pumps)
            near_tile(a_ref, b_ref, received, own, stays(i), pl.program_id(0))

        pltpu.emit_pipeline(
            body,
            grid=(right.shape[1] // tile,),
            in_specs=[
                pl.BlockSpec((total, half), lambda j: (0, 0)),
                pl.BlockSpec((total, tile), lambda j: (0, j)),
                pl.BlockSpec((half, tile), lambda j: (0, j)),
            ],
            out_specs=[pl.BlockSpec((half // 4, tile), lambda j: (0, j))],
        )(left, right, r.core[i], r.own[i])

    def pack_pairs():
        def body(*args):
            pack_block(pl.program_id(0), pl.program_id(1), r, *args)

        pltpu.emit_pipeline(
            body,
            grid=(heads, 2),
            in_specs=[pl.BlockSpec((prompt, head), lambda h, b: (b, h)), pl.BlockSpec((prompt, 384), lambda h, b: (b, 0))],
            out_specs=[pl.BlockSpec((prompt, 3 * head), lambda h, b: (b, h))],
        )(r.grad_q, r.table, r.grad_flat)

    def unit_pair(step, pumps={}):
        chunks = [(t + 2 * ring - 1 - step - i) % ring for i in range(2)]
        spans = [pl.ds(chunk * rows, rows) for chunk in chunks]

        def body(wa_ref, we_ref, gain_ref, *args):
            pumped(pumps)
            j = pl.program_id(0)
            cols = pl.ds(pl.multiple_of(j * tile, tile), tile)
            sums = [0.0] * 4
            for i in range(2):
                gp_ref, gh_ref, x_ref, stat_ref = args[4 * i : 4 * i + 4]
                one = mul(gp_ref[...], wa_ref[...], NT)
                two = mul(gh_ref[...], we_ref[...], NT)
                r.unit[spans[i], cols] = (one * gain_ref[0:1] + two * gain_ref[2:3]).astype(BF16)
                scaled = (x_ref[...].astype(F32) - stat_ref[:, 0:1]) * stat_ref[:, 1:2]
                for k, v in enumerate((one * scaled, one, two * scaled, two)):
                    sums[k] += jnp.sum(v, 0, keepdims=True)
            for k in range(4):
                r.vec[k : k + 1, cols] += sums[k]

        deep, deeper = r.grad_flat.shape[1], r.grad_pre.shape[1]
        rows_specs = [
            pl.BlockSpec((rows, deep), lambda j: (0, 0)),
            pl.BlockSpec((rows, deeper), lambda j: (0, 0)),
            pl.BlockSpec((rows, tile), lambda j: (0, j)),
            pl.BlockSpec((rows, 128), lambda j: (0, 0)),
        ]
        pltpu.emit_pipeline(
            body,
            grid=(width // tile,),
            in_specs=[
                pl.BlockSpec((tile, deep), lambda j: (j, 0)),
                pl.BlockSpec((tile, deeper), lambda j: (j, 0)),
                pl.BlockSpec((8, tile), lambda j: (0, j)),
                *rows_specs,
                *rows_specs,
            ],
            out_specs=[],
        )(
            r.attend_all, r.expand_all, r.gains,
            *(ref.at[at] for at in spans for ref in (r.grad_flat, r.grad_pre, r.rows_in, r.stat)),
        )

    def vectors_begin():
        size = width // len(places)
        for i, place in enumerate(places):
            to = pl.ds(pl.multiple_of(place() * size, size), size)
            r.vals[0, 0:4, to] = r.vec[0:4, i * size : (i + 1) * size]
            r.vals[0, 4:5, to] = r.held_sum[0:1, i * size : (i + 1) * size]
        start(vector_hops[:1])

    def vectors_on(i):
        arrive([vector_hops[i]])
        n = 8 if i < 3 else 5
        r.vals[i + 1, :, :] = r.vals[i, :, :]
        r.vals[i + 1, 0:n, :] += r.got[i, 0:n, :]
        start(vector_hops[i + 1 : i + 2] or [vectors_out])

    c, o, e, a = (grads[w] for w in "coea")
    hops.greet()
    start([grad_load])
    sum_out.begin()
    start([sum_load, *small])
    r.vals[0, :, :] = jnp.zeros_like(r.vals[0, :, :])
    r.vec[...] = jnp.zeros_like(r.vec)
    grad_load.wait()
    sum_load.wait()
    for copy in small:
        copy.wait()
    r.segc[...] = down(r.held_seg[0:1, pl.ds(pl.multiple_of(seq_start, 128), cont)])

    far_both()
    back_to_rows()
    sum_out.pump(1, 0)
    near_both({4: lambda: sum_out.pump(1, 1)})
    start(c.corner + o.corner + c.plain[:1] + o.plain[:1])
    attention({(1, 0): lambda: sum_out.pump(2, 0), (1, 1): lambda: pair_on(0), (1, 3): lambda: sum_out.pump(2, 1)})
    pair_on(1)
    hidden()
    arrive(pair_y)
    start(c.plain[1:] + o.plain[1:])
    pack_pairs()
    c.merge()
    o.merge()
    far(1, r.second, r.grad_pre)
    start([e.core])
    unit_pair(0)
    sum_unit.begin()
    arrive([e.core])
    near(1, r.second, r.grad_pre)
    start(e.corner + e.plain)
    unit_pair(2, {1: lambda: sum_unit.pump(1, 0), 2: lambda: sum_unit.pump(1, 1), 3: e.merge})
    vectors_begin()
    far(0, r.first, r.grad_flat, {2: lambda: vectors_on(0)})
    start([a.core])
    sum_unit.pump(2, 0)
    arrive([a.core])
    near(0, r.first, r.grad_flat, {1: lambda: sum_unit.pump(2, 1), 2: lambda: vectors_on(1)})
    start(a.corner + a.plain)
    vectors_on(2)
    vectors_on(3)
    a.merge()
    vectors_on(4)
    for h in range(2):
        sum_out.finish(h)
    for w in "coea":
        grads[w].finish()
    here = pl.ds(t * rows, rows)
    own_unit = local_copy(r.unit.at[here], r.unit_own)
    start([own_unit])
    for h in range(2):
        sum_unit.finish(h)
    vectors_out.wait()
    own_unit.wait()
    hops.end()


def pack_block(h, block, r, q_ref, table_ref, o_ref):
    tq, head = q_ref.shape
    theirs = r.pair_recv[h].astype(F32) + r.pair_core[h, :tq, :].astype(F32)
    own = r.pair_own[h, pl.ds(pl.multiple_of(block * tq, tq), tq), :]
    both = own + jnp.where(block == 0, theirs, 0.0)
    out = [q_ref[...], turn(both[:, :head], table_ref[...], -1.0).astype(BF16), both[:, head:].astype(BF16)]
    for i, part in enumerate(out):
        o_ref[:, i * head : (i + 1) * head] = part
        at = pl.ds(pl.multiple_of((h * 3 + i) * head, head), head)
        r.vals[0, 5:6, at] += jnp.sum(part.astype(F32), 0, keepdims=True)


def backward_pass(places, prompt, values, segments, positions):
    total, width = values["rows_grad"].shape
    ring = lax.axis_size("tp")
    rows = total // ring
    heads, _, _ = values["row_sums"].shape
    head = HEAD
    cont = total - prompt
    far = values["pairs_far"].shape[0]
    inputs = dict(values, segments=segments, positions=positions)
    hidden = values["slope"].shape[1]
    columns = [3 * heads * head, hidden, heads * head, hidden]
    half, size = width // 2, width // 8
    outs = {
        "out_recv": shape(rows, width),
        "unit_recv": shape(rows, width),
        "unit_own": shape(rows, width),
        "vectors": shape(8, width, kind=F32),
        "grad_att": shape(total, heads * head),
        "grad_q": shape(total, heads * head),
        "grad_flat": shape(total, 3 * heads * head),
        "grad_pre": shape(total, hidden),
    }
    stay = {}
    for i, cols in enumerate(columns):
        outs[f"own{i}"] = shape(size, cols, kind=F32)
        for name, n in (("far", half), ("core", half), ("from_x", size), ("from_y", size)):
            outs[f"{name}{i}"] = shape(n, cols)
        for name, n in (("to_x", size), ("to_y", size), ("corner", size), ("via_x", size // 2), ("via_y", size // 2)):
            stay[f"{name}{i}"] = pltpu.VMEM((n, cols), BF16)
    copies = 4 * (ring - 1) + 2 * heads + 7 * len(columns) + 5
    block = pltpu.VMEM((rows, width), BF16)
    scratch = {
        "send": pltpu.SemaphoreType.DMA((copies,)),
        "recv": pltpu.SemaphoreType.DMA((copies,)),
        "local": pltpu.SemaphoreType.DMA((2 * (ring - 2) + 6,)),
        "held_seg": pltpu.VMEM(segments.shape, jnp.int32),
        "held_pos": pltpu.VMEM(positions.shape, jnp.int32),
        "segc": pltpu.VMEM((cont, 128), jnp.int32),
        "grad": pltpu.VMEM((total, width), BF16),
        "unit": pltpu.VMEM((total, width), BF16),
        "pair_own": pltpu.VMEM((heads, total, 2 * head), F32),
        "pair_near": pltpu.VMEM((heads, prompt, 2 * head), BF16),
        "pair_far": pltpu.VMEM((heads, 2 * prompt, 2 * head), BF16),
        "pair_core": pltpu.VMEM((heads, 2 * prompt, 2 * head), BF16),
        "pair_recv": pltpu.VMEM((heads, prompt, 2 * head), BF16),
        **stay,
        "acc_k": pltpu.VMEM((total + far, head), F32),
        "acc_v": pltpu.VMEM((total + far, head), F32),
        "vals": pltpu.VMEM((6, 8, width), F32),
        "got": pltpu.VMEM((5, 8, width), F32),
        "vec": pltpu.VMEM((8, width), F32),
        "held_sum": pltpu.VMEM((8, width), F32),
    }
    for name in ("land_out", "held_out", "land_unit"):
        for i in range(ring - 2):
            scratch[f"{name}{i}"] = block
    names = [*inputs, *outs, *scratch]
    ref = pl.BlockSpec(memory_space=pl.ANY)
    result = pl.pallas_call(
        partial(backward_kernel, names, places, prompt),
        in_specs=[ref] * len(inputs),
        out_specs=[ref] * len(outs),
        out_shape=list(outs.values()),
        scratch_shapes=list(scratch.values()),
        compiler_params=pltpu.CompilerParams(collective_id=1, has_side_effects=True, vmem_limit_bytes=60 * 2**20),
        cost_estimate=pl.CostEstimate(flops=60 * 10**9, bytes_accessed=200 * 2**20, transcendentals=10**7),
        name="backward_pass",
    )(*inputs.values())
    return dict(zip(outs, result))


class SquareLinks:
    order = ((0, 0, 0), (1, 0, 0), (0, 1, 0), (1, 1, 0), (0, 0, 1), (1, 0, 1), (0, 1, 1), (1, 1, 1))

    def place(self, bits):
        f, c = lax.axis_index("fsdp"), lax.axis_index("ctx")
        a, b, d = bits
        return ((f ^ a) * 2 + ((c // 2) ^ b)) * 2 + ((c % 2) ^ d)

    def spot(self, p):
        f, c = lax.axis_index("fsdp"), lax.axis_index("ctx")
        a, b, d = f ^ (p // 4), (c // 2) ^ (p // 2 % 2), (c % 2) ^ (p % 2)
        return d * 4 + b * 2 + a

    def places(self):
        return [partial(self.place, bits) for bits in self.order]

    def spots(self):
        return [partial(self.spot, p) for p in range(8)]


class AnyLinks:
    def places(self):
        return [lambda: 0]

    def spots(self):
        return [lambda: 0]

    def gather(self, block):
        return lax.all_gather(block, ("fsdp", "ctx"), axis=0, tiled=True)

    def scatter(self, whole):
        return lax.psum_scatter(whole, ("fsdp", "ctx"), scatter_dimension=0, tiled=True).astype(F32)

    def others(self, v):
        return jnp.roll(v, -lax.axis_index("ctx"), 0)[1:]

    def gather_others(self, block):
        rows = block.shape[0]
        whole = lax.all_gather(block, "ctx", axis=0, tiled=True)
        return jnp.roll(whole, -rows * lax.axis_index("ctx"), 0)[rows:]

    def scatter_others(self, near, far):
        rows = near.shape[0]
        whole = jnp.concatenate([jnp.zeros_like(near), near, far], 0)
        whole = jnp.roll(whole, rows * lax.axis_index("ctx"), 0)
        return lax.psum_scatter(whole, "ctx", scatter_dimension=0, tiled=True)


def end_kernel(spots, n, x_ref, g_ref, m_ref, o_ref, e_ref, f_ref, b_ref, *refs):
    parts, outs, e_whole = refs[: 3 * n], refs[3 * n : -1], refs[-1]
    out_ref, grad_ref, sums = outs[0], outs[1], outs[2:]
    size = x_ref.shape[1] // len(spots)
    for i, spot in enumerate(spots):
        at, to = pl.ds(pl.multiple_of(spot() * size, size), size), pl.ds(i * size, size)
        branches = m_ref[:, at].astype(F32) + o_ref[:, at].astype(F32)
        out_ref[:, to] = (x_ref[:, to].astype(F32) + branches + b_ref[:1, to]).astype(BF16)
        e_whole[:, to] = e_ref[:, at].astype(F32) + f_ref[:, at].astype(F32)
    x = x_ref[...].astype(F32)
    center = x - jnp.mean(x, -1, keepdims=True)
    scale = lax.rsqrt(jnp.mean(center * center, -1, keepdims=True) + EPS)
    unit = center * scale
    e = e_whole[...]
    rest = e - jnp.mean(e, -1, keepdims=True) - unit * jnp.mean(e * unit, -1, keepdims=True)
    grad_ref[...] = g_ref[...].astype(F32) + scale * rest
    for i, out in enumerate(sums):
        own, one, two = parts[3 * i : 3 * i + 3]
        total = own[...] + one[...].astype(F32) + two[...].astype(F32)
        if len(out.shape) == 3:
            for h in range(out.shape[1]):
                out[:, h, :] = total[:, h * out.shape[2] : (h + 1) * out.shape[2]]
        else:
            out[...] = total


def row_results(x, g, mixed, mixed_own, unit, unit_own, bias, spots, weights=(), shapes=()):
    rows, width = x.shape
    tile = 64

    def block(dims):
        return pl.BlockSpec((tile, *dims[1:]), lambda i: (i,) + (0,) * (len(dims) - 1))

    own = pl.BlockSpec((tile, width), lambda i: (lax.axis_index("tp") * (rows // tile) + i, 0))
    parts = [part for weight in weights for part in weight]
    outs = [shape(rows, width), shape(rows, width, kind=F32)] + [shape(*dims, kind=F32) for dims in shapes]
    return call(
        partial(end_kernel, spots, len(weights)),
        (rows // tile,),
        [block(x.shape)] * 3 + [own] + [block(x.shape)] * 2 + [pl.BlockSpec((1, width), lambda i: (0, 0))] + [block(p.shape) for p in parts],
        [block(out.shape) for out in outs],
        outs,
        15 * x.size,
        18 * x.size + 12 * sum(p.size for p in parts),
        scratch=[pltpu.VMEM((tile, width), F32)],
        mib=60,
        name="row_results",
    )(x, g, mixed, mixed_own, unit, unit_own, bias[None], *parts)


def shards(
    stream_in,
    stream_grad,
    segments,
    positions,
    first_gain,
    first_shift,
    second_gain,
    second_shift,
    attend_weight,
    attend_bias,
    output_weight,
    expand_weight,
    expand_bias,
    contract_weight,
    output_bias,
):
    square = (lax.axis_size("fsdp"), lax.axis_size("ctx"), lax.axis_size("tp")) == (2, 4, 4)
    links = SquareLinks() if square else AnyLinks()
    local_rows = attend_weight.shape[0]
    heads = attend_bias.shape[0]
    holders = lax.axis_size("ctx")
    holder = lax.axis_index("ctx")
    prompt = PROMPT // holders

    row_count = stream_in.shape[0] * lax.axis_size("tp")
    weights = (attend_weight.reshape(local_rows, -1), expand_weight, output_weight, contract_weight)

    forward_names = (
        "rows_in",
        "rows_grad",
        "gains",
        "attend_all",
        "expand_all",
        "output_all",
        "contract_all",
        "first",
        "second",
        "stat",
        "table",
        "queries",
        "pairs",
        "pairs_far",
        "activated",
        "slope",
        "attended",
        "row_sums",
        "mixed",
        "grad_sum",
    )
    weight_grads = None
    if square:
        rows_of = (v[None] for v in (first_gain, first_shift, second_gain, second_shift))
        made = forward_pass(
            links.places(), prompt, heads, stream_in, stream_grad, weights, [*rows_of], attend_bias.reshape(1, -1),
            expand_bias[None], segments[None], positions[None],
        )
        values = dict(zip(forward_names, made))
        back = backward_pass(links.places(), prompt, values, segments[None], positions[None])
        sums = (back["out_recv"], values["mixed"], back["unit_recv"], back["unit_own"])
        parts = [(back[f"own{i}"], back[f"from_x{i}"], back[f"from_y{i}"]) for i in range(4)]
        shapes = [w.shape for w in (attend_weight, expand_weight, output_weight, contract_weight)]
        vectors = back["vectors"]
        norm_sums = [vectors[i] for i in range(5)]
        bias_sums = [vectors[5, : attend_bias.size], vectors[6]]
    else:
        gains = jnp.concatenate([jnp.stack([first_gain, first_shift, second_gain, second_shift]), jnp.zeros((4, first_gain.shape[0]), F32)])
        row_pos = lax.dynamic_slice_in_dim(positions, holder * row_count, row_count)
        row_seg = lax.dynamic_slice_in_dim(segments, holder * row_count, row_count)
        starts = positions.reshape(holders, row_count)[:, 0]
        bias = jnp.where(links.others(starts) < row_pos[0], 0.0, -1e30).astype(F32)
        bias = jnp.broadcast_to(jnp.pad(bias, (0, 8 - bias.shape[0]))[:, None], (8, 128))
        rows_in, rows_grad = (lax.all_gather(v, "tp", axis=0, tiled=True) for v in (stream_in, stream_grad))
        attend_all, expand_all, output_all, contract_all = (links.gather(v) for v in weights)
        table = turn_table(row_pos)
        first, second, rows_in, stat = norms(rows_in, gains, links.places())
        queries, pairs = project(first, attend_all, attend_bias.reshape(-1), table, heads)
        pairs_far = links.gather_others(pairs[:prompt])
        activated, slope = expand(second, expand_all, expand_bias)
        attended, row_sums = attend(queries, pairs, pairs_far, bias, row_seg, prompt)
        mixed = mixed_sum(attended, activated, output_all, contract_all)
        branches = lax.psum_scatter(mixed, "tp", scatter_dimension=0, tiled=True)
        grad_attended = attended_grads(rows_grad, output_all)
        grad_queries, pair_own, pair_near, pair_far = attend_back(
            queries, grad_attended, attended, row_sums, pairs, pairs_far, bias, row_seg, prompt, table
        )
        theirs = links.scatter_others(pair_near, pair_far)
        grad_pre, expand_sums = hidden_grads(rows_grad, contract_all, slope)
        grad_flat, attend_sums = pack(grad_queries, pair_own, theirs, jnp.zeros_like(theirs), table, prompt)
        unit, vector_parts = unit_grads(grad_flat, grad_pre, attend_all, expand_all, rows_in, stat, gains)
        unit_part = lax.psum_scatter(unit, "tp", scatter_dimension=0, tiled=True)
        weight_grads = [
            links.scatter(jnp.einsum("tc,tk->ck", left, right, preferred_element_type=F32).astype(BF16))
            for left, right in ((first, grad_flat), (second, grad_pre), (rows_grad, attended), (rows_grad, activated))
        ]
        row_sum = jnp.sum(stream_grad.astype(F32), 0)
        norm_sums = lax.psum([*vector_parts[:4], row_sum], ("fsdp", "ctx", "tp"))
        bias_sums = lax.psum([attend_sums[0], expand_sums[0]], ("fsdp", "ctx"))
        parts, shapes = (), ()
        sums = (branches, jnp.zeros((row_count, stream_in.shape[1]), BF16), unit_part, jnp.zeros_like(unit_part))
    stream_out, input_grad, *summed = row_results(
        stream_in, stream_grad, *sums, output_bias, links.spots(), parts, shapes
    )
    weight_grads = summed or weight_grads
    return (
        stream_out,
        input_grad,
        *norm_sums[:4],
        weight_grads[0].reshape(attend_weight.shape),
        bias_sums[0].reshape(attend_bias.shape),
        weight_grads[2],
        weight_grads[1],
        bias_sums[1],
        weight_grads[3],
        norm_sums[4],
    )


def solution(mesh):
    tokens = P(("fsdp", "ctx", "tp"), None)
    weight = P(("fsdp", "ctx"), "tp")
    heads = P(("fsdp", "ctx"), "tp", None)
    return jax.shard_map(
        shards,
        mesh=mesh,
        in_specs=(
            tokens,
            tokens,
            P("fsdp"),
            P("fsdp"),
            P(),
            P(),
            P(),
            P(),
            heads,
            P("tp", None),
            weight,
            weight,
            P("tp"),
            weight,
            P(),
        ),
        out_specs=(
            tokens,
            tokens,
            P(),
            P(),
            P(),
            P(),
            heads,
            P("tp", None),
            weight,
            weight,
            P("tp"),
            weight,
            P(),
        ),
        check_vma=False,
    )
```

```python
from functools import partial, reduce
import math
from types import SimpleNamespace

import jax
import jax.numpy as jnp
import numpy as np
from jax import lax
from jax.experimental import pallas as pl
from jax.experimental.pallas import tpu as pltpu
from jax.sharding import PartitionSpec as P

ROT = 64
PROMPT = 2048
EPS = 1e-05
F32 = jnp.float32
BF16 = jnp.bfloat16
ROWS = 256
HEAD = 256
NN = (((1,), (0,)), ((), ()))
NT = (((1,), (1,)), ((), ()))
TN = (((0,), (0,)), ((), ()))


def mul(a, b, dims):
    return lax.dot_general(a, b, dims, preferred_element_type=F32)


def call(kernel, grid, in_specs, out_specs, out_shape, flops, moved, exps=0, scratch=(), mib=48, name=None):
    return pl.pallas_call(
        kernel,
        grid=grid,
        in_specs=in_specs,
        out_specs=out_specs,
        out_shape=out_shape,
        scratch_shapes=scratch,
        compiler_params=pltpu.CompilerParams(vmem_limit_bytes=mib * 2**20),
        cost_estimate=pl.CostEstimate(flops=flops, bytes_accessed=moved, transcendentals=exps),
        name=name,
    )


def shape(*dims, kind=BF16):
    return jax.ShapeDtypeStruct(dims, kind)


def wide(row):
    return jnp.broadcast_to(row[None], (8, row.shape[0]))


def turn(v, table, sign):
    head = v[:, :128]
    other = pltpu.roll(head, 96, 1) * table[:, 128:256] + pltpu.roll(head, 32, 1) * table[:, 256:]
    return jnp.concatenate([head * table[:, :128] + sign * other, v[:, 128:]], 1)


def turn_table(where_at):
    half = ROT // 2
    frequency = jnp.exp(jnp.arange(half, dtype=F32) * (-2.0 * math.log(10000.0) / ROT))
    angles = where_at.astype(F32)[:, None] * frequency[None, :]
    c, s = jnp.cos(angles), jnp.sin(angles)
    rows = where_at.shape[0]
    one, none = jnp.ones((rows, 128 - ROT), F32), jnp.zeros((rows, 128 - half), F32)
    return jnp.concatenate([c, c, one, -s, none, none[:, :half], s, none[:, : 128 - ROT]], 1)


def norm_kernel(places, x_ref, gain_ref, first_ref, second_ref, x_out, stat_ref):
    x = x_ref[...].astype(F32)
    mean = jnp.mean(x, -1, keepdims=True)
    center = x - mean
    scale = lax.rsqrt(jnp.mean(center * center, -1, keepdims=True) + EPS)
    size = x_ref.shape[1] // len(places)
    for i, place in enumerate(places):
        at, to = pl.ds(pl.multiple_of(place() * size, size), size), pl.ds(i * size, size)
        part = x_ref[:, at]
        x_out[:, to] = part
        unit = (part.astype(F32) - mean) * scale
        first_ref[:, to] = (unit * gain_ref[0:1, at] + gain_ref[1:2, at]).astype(BF16)
        second_ref[:, to] = (unit * gain_ref[2:3, at] + gain_ref[3:4, at]).astype(BF16)
    lane = lax.broadcasted_iota(jnp.int32, stat_ref.shape, 1)
    stat_ref[...] = jnp.where(lane == 0, mean, scale)


def norms(x, gains, places):
    rows, width = x.shape
    block = pl.BlockSpec((128, width), lambda i: (i, 0))
    return call(
        partial(norm_kernel, places),
        (rows // 128,),
        [block, pl.BlockSpec((8, width), lambda i: (0, 0))],
        [block, block, block, pl.BlockSpec((128, 128), lambda i: (i, 0))],
        [shape(rows, width)] * 3 + [shape(rows, 128, kind=F32)],
        10 * rows * width,
        8 * rows * width,
        name="norms",
    )(x, gains)


def project_kernel(n_ref, w_ref, b_ref, table_ref, q_ref, kv_ref):
    head = q_ref.shape[1]
    for i in range(n_ref.shape[0] // ROWS):
        at = pl.ds(i * ROWS, ROWS)
        out = mul(n_ref[at, :], w_ref[...], NN) + b_ref[:1]
        q_ref[at, :] = turn(out[:, :head], table_ref[at, :], 1.0).astype(BF16)
        kv_ref[at, :head] = turn(out[:, head : 2 * head], table_ref[at, :], 1.0).astype(BF16)
        kv_ref[at, head:] = out[:, 2 * head :].astype(BF16)


def project(n, w, bias, table, heads):
    rows, depth = n.shape
    width = w.shape[1] // heads
    head = width // 3
    return call(
        project_kernel,
        (heads,),
        [
            pl.BlockSpec((rows, depth), lambda h: (0, 0)),
            pl.BlockSpec((depth, width), lambda h: (0, h)),
            pl.BlockSpec((8, width), lambda h: (0, h)),
            pl.BlockSpec((rows, 384), lambda h: (0, 0)),
        ],
        [pl.BlockSpec((rows, head), lambda h: (0, h)), pl.BlockSpec((rows, 2 * head), lambda h: (0, h))],
        [shape(rows, heads * head), shape(rows, heads * 2 * head)],
        2 * rows * depth * w.shape[1],
        2 * (rows * depth + w.size + rows * w.shape[1]),
        name="project",
    )(n, w, wide(bias), table)


def expand_kernel(n_ref, w_ref, b_ref, h_ref, d_ref):
    for i in range(n_ref.shape[0] // ROWS):
        at = pl.ds(i * ROWS, ROWS)
        pre = mul(n_ref[at, :], w_ref[...], NN) + b_ref[:1]
        below = 0.5 + 0.5 * lax.erf(pre * math.sqrt(0.5))
        h_ref[at, :] = (pre * below).astype(BF16)
        d_ref[at, :] = (below + pre * jnp.exp(-0.5 * pre * pre) * (1.0 / math.sqrt(2 * math.pi))).astype(BF16)


def expand(n, w, bias, tile=512):
    rows, depth = n.shape
    cols = w.shape[1]
    out = pl.BlockSpec((rows, tile), lambda j: (0, j))
    return call(
        expand_kernel,
        (cols // tile,),
        [
            pl.BlockSpec((rows, depth), lambda j: (0, 0)),
            pl.BlockSpec((depth, tile), lambda j: (0, j)),
            pl.BlockSpec((8, tile), lambda j: (0, j)),
        ],
        [out, out],
        [shape(rows, cols), shape(rows, cols)],
        2 * rows * depth * cols,
        2 * (rows * depth + w.size + 2 * rows * cols),
        2 * rows * cols,
        name="expand",
    )(n, w, wide(bias))


def attend_block(prompt, block, allow, segc_ref, segr, q_ref, ko, vo, kt, vt, o_ref, stat_ref):
    tq = q_ref.shape[0]
    first_cont = prompt // tq
    cont = ko.shape[0] - prompt
    q = q_ref[...] * BF16(1.0 / math.sqrt(q_ref.shape[1]))
    rows = lax.broadcasted_iota(jnp.int32, (tq, 1), 0)

    def finish(scores, values):
        top = reduce(jnp.maximum, [jnp.max(s, -1, keepdims=True) for s in scores])
        exps = [jnp.exp(s - top) for s in scores]
        total = sum(jnp.sum(e, -1, keepdims=True) for e in exps)
        out = sum(mul(e.astype(BF16), v, NN) for e, v in zip(exps, values))
        o_ref[...] = (out / total).astype(BF16)
        stat_ref[0] = jnp.transpose(jnp.broadcast_to(top + jnp.log(total), (tq, 128)))[:8]

    @pl.when(block < first_cont)
    def _():
        cols = lax.broadcasted_iota(jnp.int32, (1, prompt), 1)
        own = jnp.where(cols <= rows + block * tq, mul(q, ko[:prompt], NT), -1e30)
        spans = [pl.ds(i * prompt, prompt) for i in range(len(allow))]
        far = [mul(q, kt[at, :], NT) + add for at, add in zip(spans, allow)]
        finish([own, *far], [vo[:prompt], *(vt[at, :] for at in spans)])

    @pl.when(block >= first_cont)
    def _():
        cols = lax.broadcasted_iota(jnp.int32, (1, cont), 1)
        own = mul(q, ko[:prompt], NT)
        at = jnp.maximum(block - first_cont, 0) * tq
        segc = segc_ref[pl.ds(pl.multiple_of(at, tq), tq), :1]
        follow = jnp.where((cols <= rows + at) & (segc == segr), mul(q, ko[prompt:], NT), -1e30)
        far = mul(q, kt[...], NT)
        finish([own, follow, far], [vo[:prompt], vo[prompt:], vt[...]])


def sequence_places(prompt, holder, places_ref, rows):
    own = places_ref[0:1, pl.ds(pl.multiple_of(holder * rows, 128), 128)][:, :1]

    def allow(other):
        start = places_ref[0:1, pl.ds(pl.multiple_of(other * rows, 128), 128)][:, :1]
        return jnp.where(start < own, 0.0, -1e30)

    return allow


def down(row):
    return jnp.transpose(jnp.broadcast_to(row, (128, row.shape[1])))


def attend_kernel(prompt, bias_ref, segc_ref, segr_ref, *refs):
    allow = [bias_ref[i : i + 1, :1] for i in range(refs[3].shape[0] // prompt)]
    attend_block(prompt, pl.program_id(1), allow, segc_ref, segr_ref[:1], *refs)


def attend(q, kv, kv_far, bias, seg, prompt):
    rows, width = q.shape
    head = HEAD
    heads = width // head
    far = kv_far.shape[0]
    cont = rows - prompt
    tq = ROWS
    return call(
        partial(attend_kernel, prompt),
        (heads, rows // tq),
        [
            pl.BlockSpec((8, 128), lambda h, b: (0, 0)),
            pl.BlockSpec((cont, 128), lambda h, b: (0, 0)),
            pl.BlockSpec((8, cont), lambda h, b: (0, 0)),
            pl.BlockSpec((tq, head), lambda h, b: (b, h)),
            pl.BlockSpec((rows, head), lambda h, b: (0, 2 * h)),
            pl.BlockSpec((rows, head), lambda h, b: (0, 2 * h + 1)),
            pl.BlockSpec((far, head), lambda h, b: (0, 2 * h)),
            pl.BlockSpec((far, head), lambda h, b: (0, 2 * h + 1)),
        ],
        [pl.BlockSpec((tq, head), lambda h, b: (b, h)), pl.BlockSpec((1, 8, tq), lambda h, b: (h, 0, b))],
        [shape(rows, width), shape(heads, 8, rows, kind=F32)],
        4 * rows * (rows + far) * width,
        2 * (2 * q.size + kv.size + kv_far.size),
        rows * (rows + far) * heads,
        name="attend",
    )(bias, jnp.broadcast_to(seg[prompt:, None], (cont, 128)), wide(seg[prompt:]), q, kv, kv, kv_far, kv_far)


def attend_back_block(
    prompt, block, last, allow, segc, segr, q_ref, do_ref, o_ref, stat_ref, ko, vo, kt, vt, table_ref,
    dq_ref, own_ref, near_ref, far_ref, acc_k, acc_v,
):
    tq, head = q_ref.shape
    first_cont = prompt // tq
    scale = 1.0 / math.sqrt(head)
    q = q_ref[...] * BF16(scale)
    do = do_ref[...]
    inner = jnp.sum(do.astype(F32) * o_ref[...].astype(F32), -1, keepdims=True)
    inner = jnp.transpose(jnp.broadcast_to(inner, (tq, 128)))[:1]
    stat = stat_ref[0, :1]
    cols = lax.broadcasted_iota(jnp.int32, (1, tq), 1)

    @pl.when(block == 0)
    def _():
        acc_k[...] = jnp.zeros_like(acc_k)
        acc_v[...] = jnp.zeros_like(acc_v)

    def part(keys, values, at, seen):
        probs = jnp.exp(seen(mul(keys, q, NT)) - stat)
        grads = (probs * (mul(values, do, NT) - inner)).astype(BF16)
        acc_v[at, :] += mul(probs.astype(BF16), do, NN)
        acc_k[at, :] += mul(grads, q, NN)
        return mul(grads, keys, TN)

    def far_parts(total, seen):
        for i in range(kt.shape[0] // prompt):
            at = pl.ds(i * prompt, prompt)
            total += part(kt[at, :], vt[at, :], pl.ds(ko.shape[0] + i * prompt, prompt), partial(seen, i))
        dq_ref[...] = turn(total * scale, table_ref[...], -1.0).astype(BF16)

    @pl.when(block < first_cont)
    def _():
        rows = lax.broadcasted_iota(jnp.int32, (prompt, 1), 0)
        total = part(
            ko[:prompt], vo[:prompt], pl.ds(0, prompt), lambda s: jnp.where(rows <= cols + block * tq, s, -1e30)
        )
        far_parts(total, lambda i, s: s + allow[i])

    @pl.when(block >= first_cont)
    def _():
        cont = ko.shape[0] - prompt
        rows = lax.broadcasted_iota(jnp.int32, (cont, 1), 0)
        total = part(ko[:prompt], vo[:prompt], pl.ds(0, prompt), lambda s: s)
        read = (rows <= cols + (block - first_cont) * tq) & (segc() == segr())
        total += part(ko[prompt:], vo[prompt:], pl.ds(prompt, cont), lambda s: jnp.where(read, s, -1e30))
        far_parts(total, lambda i, s: s)

    @pl.when(block == last)
    def _():
        start = 0
        for ref in (own_ref, near_ref, far_ref):
            at = pl.ds(start, ref.shape[0])
            ref[:, :head] = acc_k[at, :].astype(ref.dtype)
            ref[:, head:] = acc_v[at, :].astype(ref.dtype)
            start += ref.shape[0]


def attend_back_kernel(prompt, bias_ref, segc_ref, segr_ref, *refs):
    allow = [bias_ref[i : i + 1, :1] for i in range(refs[6].shape[0] // prompt)]
    last = pl.num_programs(1) - 1
    attend_back_block(prompt, pl.program_id(1), last, allow, lambda: segc_ref[:, :1], lambda: segr_ref[:1], *refs)


def attend_back(q, do, o, stat, kv, kv_far, bias, seg, prompt, table):
    rows, width = q.shape
    head = HEAD
    heads = width // head
    far = kv_far.shape[0]
    cont = rows - prompt
    tq = ROWS
    first = prompt // tq
    row = pl.BlockSpec((tq, head), lambda h, b: (b, h))

    def column(n, odd):
        return pl.BlockSpec((n, head), lambda h, b: (0, 2 * h + odd))

    def pair(n):
        return pl.BlockSpec((n, 2 * head), lambda h, b: (0, h))

    return call(
        partial(attend_back_kernel, prompt),
        (heads, rows // tq),
        [
            pl.BlockSpec((8, 128), lambda h, b: (0, 0)),
            pl.BlockSpec((cont, 128), lambda h, b: (0, 0)),
            pl.BlockSpec((8, tq), lambda h, b: (0, jnp.maximum(b - first, 0))),
            row,
            row,
            row,
            pl.BlockSpec((1, 8, tq), lambda h, b: (h, 0, b)),
            column(rows, 0),
            column(rows, 1),
            column(far, 0),
            column(far, 1),
            pl.BlockSpec((tq, 384), lambda h, b: (b, 0)),
        ],
        [row, pair(rows), pair(prompt), pair(far - prompt)],
        [
            shape(rows, width),
            shape(rows, 2 * width, kind=F32),
            shape(prompt, 2 * width),
            shape(far - prompt, 2 * width),
        ],
        10 * rows * (rows + far) * width,
        2 * (4 * q.size + 4 * kv.size + 2 * kv_far.size),
        rows * (rows + far) * heads,
        [pltpu.VMEM((rows + far, head), F32), pltpu.VMEM((rows + far, head), F32)],
        name="attend_back",
    )(
        bias, jnp.broadcast_to(seg[prompt:, None], (cont, 128)), wide(seg[prompt:]),
        q, do, o, stat, kv, kv, kv_far, kv_far, table,
    )


def mixed_kernel(a_ref, h_ref, wa_ref, wh_ref, o_ref):
    for i in range(a_ref.shape[0] // ROWS):
        at = pl.ds(i * ROWS, ROWS)
        o_ref[at, :] = (mul(a_ref[at, :], wa_ref[...], NT) + mul(h_ref[at, :], wh_ref[...], NT)).astype(BF16)


def mixed_sum(attended, activated, w_out, w_contract, tile=512):
    rows = attended.shape[0]
    deep, deeper = attended.shape[1], activated.shape[1]
    width = w_out.shape[0]
    return call(
        mixed_kernel,
        (width // tile,),
        [
            pl.BlockSpec((rows, deep), lambda j: (0, 0)),
            pl.BlockSpec((rows, deeper), lambda j: (0, 0)),
            pl.BlockSpec((tile, deep), lambda j: (j, 0)),
            pl.BlockSpec((tile, deeper), lambda j: (j, 0)),
        ],
        pl.BlockSpec((rows, tile), lambda j: (0, j)),
        shape(rows, width),
        2 * rows * width * (deep + deeper),
        2 * (rows + width) * (deep + deeper) + 2 * rows * width,
        name="mixed_sum",
    )(attended, activated, w_out, w_contract)


def attended_grad_kernel(g_ref, w_ref, o_ref):
    for i in range(g_ref.shape[0] // ROWS):
        at = pl.ds(i * ROWS, ROWS)
        o_ref[at, :] = mul(g_ref[at, :], w_ref[...], NN).astype(BF16)


def attended_grads(g, w, tile=256):
    rows, depth = g.shape
    cols = w.shape[1]
    return call(
        attended_grad_kernel,
        (cols // tile,),
        [pl.BlockSpec((rows, depth), lambda j: (0, 0)), pl.BlockSpec((depth, tile), lambda j: (0, j))],
        pl.BlockSpec((rows, tile), lambda j: (0, j)),
        shape(rows, cols),
        2 * rows * depth * cols,
        2 * (rows * depth + w.size + rows * cols),
        name="attended_grads",
    )(g, w)


def hidden_grad_kernel(g_ref, w_ref, d_ref, gp_ref, sum_ref):
    total = 0.0
    for i in range(g_ref.shape[0] // ROWS):
        at = pl.ds(i * ROWS, ROWS)
        grad = (mul(g_ref[at, :], w_ref[...], NN) * d_ref[at, :].astype(F32)).astype(BF16)
        gp_ref[at, :] = grad
        total += jnp.sum(grad.astype(F32), 0, keepdims=True)
    sum_ref[...] = jnp.broadcast_to(total, sum_ref.shape)


def hidden_grads(g, w, slope, tile=512):
    rows, depth = g.shape
    cols = w.shape[1]
    tall = pl.BlockSpec((rows, tile), lambda j: (0, j))
    return call(
        hidden_grad_kernel,
        (cols // tile,),
        [pl.BlockSpec((rows, depth), lambda j: (0, 0)), pl.BlockSpec((depth, tile), lambda j: (0, j)), tall],
        [tall, pl.BlockSpec((8, tile), lambda j: (0, j))],
        [shape(rows, cols), shape(8, cols, kind=F32)],
        2 * rows * depth * cols,
        2 * (rows * depth + w.size + 2 * rows * cols),
        name="hidden_grads",
    )(g, w, slope)


def pack_kernel(prompt_blocks, q_ref, own_ref, near_ref, far_ref, table_ref, o_ref, sum_ref):
    block = pl.program_id(1)
    head = q_ref.shape[1]
    theirs = near_ref[...].astype(F32) + far_ref[...].astype(F32)
    both = own_ref[...] + jnp.where(block < prompt_blocks, theirs, 0.0)
    out = [q_ref[...], turn(both[:, :head], table_ref[...], -1.0).astype(BF16), both[:, head:].astype(BF16)]

    @pl.when(block == 0)
    def _():
        sum_ref[...] = jnp.zeros_like(sum_ref)

    for i, part in enumerate(out):
        o_ref[:, i * head : (i + 1) * head] = part
        sum_ref[:, i * head : (i + 1) * head] += jnp.sum(part.astype(F32), 0, keepdims=True)


def pack(dq, own, near, far, table, prompt):
    rows, width = dq.shape
    head = HEAD
    heads = width // head
    tq = ROWS
    blocks = prompt // tq
    theirs = pl.BlockSpec((tq, 2 * head), lambda h, b: (jnp.minimum(b, blocks - 1), h))
    return call(
        partial(pack_kernel, blocks),
        (heads, rows // tq),
        [
            pl.BlockSpec((tq, head), lambda h, b: (b, h)),
            pl.BlockSpec((tq, 2 * head), lambda h, b: (b, h)),
            theirs,
            theirs,
            pl.BlockSpec((tq, 384), lambda h, b: (b, 0)),
        ],
        [pl.BlockSpec((tq, 3 * head), lambda h, b: (b, h)), pl.BlockSpec((8, 3 * head), lambda h, b: (0, h))],
        [shape(rows, 3 * width), shape(8, 3 * width, kind=F32)],
        10 * rows * width,
        16 * rows * width,
        name="pack",
    )(dq, own, near, far, table)


def unit_grad_kernel(gp_ref, gh_ref, wa_ref, we_ref, x_ref, stat_ref, gain_ref, e_ref, sum_ref):
    sums = [0.0] * 4
    for i in range(gp_ref.shape[0] // ROWS):
        at = pl.ds(i * ROWS, ROWS)
        first = mul(gp_ref[at, :], wa_ref[...], NT)
        second = mul(gh_ref[at, :], we_ref[...], NT)
        e_ref[at, :] = (first * gain_ref[0:1] + second * gain_ref[2:3]).astype(BF16)
        unit = (x_ref[at, :].astype(F32) - stat_ref[at, 0:1]) * stat_ref[at, 1:2]
        for j, v in enumerate((first * unit, first, second * unit, second)):
            sums[j] += jnp.sum(v, 0, keepdims=True)
    for j in range(4):
        sum_ref[j : j + 1] = sums[j]
    sum_ref[4:] = jnp.zeros_like(sum_ref[4:])


def unit_grads(gp, gh, w_attend, w_expand, x, stat, gains, tile=512):
    rows, width = x.shape
    deep, deeper = gp.shape[1], gh.shape[1]
    col = pl.BlockSpec((rows, tile), lambda j: (0, j))
    row = pl.BlockSpec((8, tile), lambda j: (0, j))
    return call(
        unit_grad_kernel,
        (width // tile,),
        [
            pl.BlockSpec((rows, deep), lambda j: (0, 0)),
            pl.BlockSpec((rows, deeper), lambda j: (0, 0)),
            pl.BlockSpec((tile, deep), lambda j: (j, 0)),
            pl.BlockSpec((tile, deeper), lambda j: (j, 0)),
            col,
            pl.BlockSpec((rows, 128), lambda j: (0, 0)),
            row,
        ],
        [col, row],
        [shape(rows, width), shape(8, width, kind=F32)],
        2 * rows * width * (deep + deeper),
        2 * (rows + width) * (deep + deeper) + 4 * rows * width,
        name="unit_grads",
    )(gp, gh, w_attend, w_expand, x, stat, gains)


def far_kernel(a_ref, b_ref, o_ref):
    for i in range(o_ref.shape[0] // ROWS):
        o_ref[pl.ds(i * ROWS, ROWS), :] = mul(a_ref[:, pl.ds(i * ROWS, ROWS)], b_ref[...], TN).astype(BF16)


def near_kernel(a_ref, b_ref, r_ref, *outs):
    size = a_ref.shape[1] // len(outs)
    for i, out in enumerate(outs):
        at = pl.ds(i * size, size)
        out[...] = (mul(a_ref[:, at], b_ref[...], TN) + r_ref[at, :].astype(F32)).astype(out.dtype)


class Hops:
    def __init__(self, send, recv, pairs=False):
        self.send, self.recv, self.made = send, recv, []
        f, c, t = (lax.axis_index(a) for a in ("fsdp", "ctx", "tp"))
        ring = lax.axis_size("tp")
        self.to = {
            "x": {"fsdp": 1 - f},
            "y": {"ctx": (c + 2) % 4},
            "core": {"ctx": c + 1 - 2 * (c % 2)},
            "up": {"tp": (t + 1) % ring},
        }
        self.back = {"tp": (t + ring - 1) % ring}
        if pairs:
            self.to["t1"] = {"tp": t + 1 - 2 * (t % 2)}
            self.to["t2"] = {"tp": t + 2 - 4 * (t // 2 % 2)}

    def greet(self):
        barrier = pltpu.get_barrier_semaphore()
        near = [*self.to.values(), self.back]
        for device in near:
            pl.semaphore_signal(barrier, inc=1, device_id=device, device_id_type=pl.DeviceIdType.MESH)
        pl.semaphore_wait(barrier, len(near))

    def copy(self, way, src, dst):
        i = len(self.made)
        self.made.append(
            pltpu.make_async_remote_copy(
                src,
                dst,
                self.send.at[i],
                self.recv.at[i],
                device_id=self.to[way],
                device_id_type=pl.DeviceIdType.MESH,
            )
        )
        return self.made[-1]

    def end(self):
        for copy in self.made:
            copy.wait_send()


class Block:
    def __init__(self, hops, part, whole, halves=1):
        size = part.shape[0]
        half, piece = size // 2, size // halves

        def at(slot, start=0, rows=size):
            return whole.at[pl.ds(slot * size + start, rows)]

        self.first = [
            [
                hops.copy(way, part.at[pl.ds(i * piece, piece)], at(slot, i * piece, piece))
                for way, slot in (("x", 1), ("y", 2))
            ]
            for i in range(halves)
        ]
        self.corner = [
            hops.copy("x", at(2, 0, half), at(3, 0, half)),
            hops.copy("y", at(1, half, half), at(3, half, half)),
        ]
        self.core = [hops.copy("core", part if slot == 0 else at(slot), at(4 + slot)) for slot in range(4)]


def start(copies):
    for copy in copies:
        copy.start()


def arrive(copies):
    for copy in copies:
        copy.wait_recv()


def table_kernel(pos_ref, freq_ref, o_ref):
    angle = down(pos_ref[...].astype(F32)) * freq_ref[:1]
    c, s = jnp.cos(angle), jnp.sin(angle)
    lane = lax.broadcasted_iota(jnp.int32, angle.shape, 1)
    half = ROT // 2
    o_ref[:, :128] = jnp.where(lane < ROT, c, 1.0)
    o_ref[:, 128:256] = jnp.where(lane < half, -s, 0.0)
    o_ref[:, 256:] = jnp.where((lane >= half) & (lane < ROT), s, 0.0)


def norm_block_kernel(x_ref, gain_ref, first_ref, second_ref, stat_ref):
    x = x_ref[...].astype(F32)
    mean = jnp.mean(x, -1, keepdims=True)
    center = x - mean
    scale = lax.rsqrt(jnp.mean(center * center, -1, keepdims=True) + EPS)
    unit = center * scale
    first_ref[...] = (unit * gain_ref[0:1] + gain_ref[1:2]).astype(BF16)
    second_ref[...] = (unit * gain_ref[2:3] + gain_ref[3:4]).astype(BF16)
    lane = lax.broadcasted_iota(jnp.int32, stat_ref.shape, 1)
    stat_ref[...] = jnp.where(lane == 0, mean, scale)


def project_block_kernel(n_ref, w_ref, b_ref, table_ref, q_ref, kv_ref):
    head = q_ref.shape[1]
    out = mul(n_ref[...], w_ref[...], NN) + b_ref[:1]
    q_ref[...] = turn(out[:, :head], table_ref[...], 1.0).astype(BF16)
    kv_ref[:, :head] = turn(out[:, head : 2 * head], table_ref[...], 1.0).astype(BF16)
    kv_ref[:, head:] = out[:, 2 * head :].astype(BF16)


def expand_block_kernel(n_ref, w_ref, b_ref, h_ref, d_ref):
    pre = mul(n_ref[...], w_ref[...], NN) + b_ref[:1]
    below = 0.5 + 0.5 * lax.erf(pre * math.sqrt(0.5))
    h_ref[...] = (pre * below).astype(BF16)
    d_ref[...] = (below + pre * jnp.exp(-0.5 * pre * pre) * (1.0 / math.sqrt(2 * math.pi))).astype(BF16)


def forward_kernel(places, prompt, *refs):
    (
        x_ref, g_ref, wa, we, wo, wc, gain_1, gain_2, gain_3, gain_4, bias_a, bias_e, seg_ref, pos_ref, freq_ref,
        rows_in, rows_grad, gains, attend_all, expand_all, output_all, contract_all,
        first, second, stat, table, queries, pairs, pairs_far, activated, slope, attended, row_sums, mixed, grad_sum,
        send, recv, local, held_x, held_g, held_gains, held_sum, held_seg, held_pos, segc, gain_rows, *held,
    ) = refs
    hops = Hops(send, recv)
    t, ring = lax.axis_index("tp"), lax.axis_size("tp")
    rows, width = x_ref.shape
    total = rows * ring
    block = width // len(places)
    chunk = rows // 2

    here = pl.ds(t * rows, rows)
    moves = [(x_ref, held_x, rows_in.at[here]), (g_ref, held_g, rows_grad.at[here])]
    loads, stores, count = [], [], 0
    for src, mid, dst in moves:
        loads.append([])
        for i, place in enumerate(places):
            at = pl.ds(pl.multiple_of(place() * block, block), block)
            loads[-1].append(pltpu.make_async_copy(src.at[:, at], mid.at[:, pl.ds(i * block, block)], local.at[count]))
            count += 1
        stores.append(pltpu.make_async_copy(mid, dst, local.at[count]))
        count += 1
    small = [pltpu.make_async_copy(seg_ref, held_seg, local.at[count]), pltpu.make_async_copy(pos_ref, held_pos, local.at[count + 1])]
    count += 2
    for i, src in enumerate((gain_1, gain_2, gain_3, gain_4)):
        small.append(pltpu.make_async_copy(src, gain_rows.at[i], local.at[count]))
        count += 1
    for src, mid, whole in zip((wa, we, wo, wc), held, (attend_all, expand_all, output_all, contract_all)):
        loads.append([pltpu.make_async_copy(src, mid, local.at[count])])
        stores.append(pltpu.make_async_copy(mid, whole.at[pl.ds(0, src.shape[0])], local.at[count + 1]))
        count += 2

    def rings(ref, held_rows):
        made = {}
        for step in range(ring - 1):
            for half in range(2):
                at = ref.at[pl.ds(((t + ring - step) % ring) * rows + half * chunk, chunk)]
                src = held_rows.at[pl.ds(half * chunk, chunk)] if step == 0 else at
                made[step, half] = hops.copy("up", src, at)
        return made

    ring_x, ring_g = rings(rows_in, held_x), rings(rows_grad, held_g)
    a, e, o = (Block(hops, part, whole) for part, whole in ((wa, attend_all), (we, expand_all), (wo, output_all)))
    c = Block(hops, wc, contract_all, 2)
    own_pairs = pairs.at[pl.ds(0, prompt)]
    far = [pairs_far.at[pl.ds(i * prompt, prompt)] for i in range(3)]
    pair_y, pair_core = hops.copy("y", own_pairs, far[0]), hops.copy("core", own_pairs, far[1])
    pair_corner = hops.copy("core", far[0], far[2])

    def forward(copies, step, half):
        arrive([copies[step, half]])
        if step < ring - 2:
            start([copies[step + 1, half]])

    head = HEAD
    heads = queries.shape[1] // head

    def span(step):
        return pl.ds(((t + ring - step) % ring) * rows, rows)

    def norm(step):
        tile = 128
        row = pl.BlockSpec((tile, width), lambda i: (i, 0))
        pltpu.emit_pipeline(
            norm_block_kernel,
            grid=(rows // tile,),
            in_specs=[row, pl.BlockSpec((8, width), lambda i: (0, 0))],
            out_specs=[row, row, pl.BlockSpec((tile, 128), lambda i: (i, 0))],
        )(rows_in.at[span(step)], gains, first.at[span(step)], second.at[span(step)], stat.at[span(step)])

    def project(step):
        pltpu.emit_pipeline(
            project_block_kernel,
            grid=(heads,),
            in_specs=[
                pl.BlockSpec((rows, width), lambda h: (0, 0)),
                pl.BlockSpec((width, 3 * head), lambda h: (0, h)),
                pl.BlockSpec((1, 3 * head), lambda h: (0, h)),
                pl.BlockSpec((rows, 384), lambda h: (0, 0)),
            ],
            out_specs=[pl.BlockSpec((rows, head), lambda h: (0, h)), pl.BlockSpec((rows, 2 * head), lambda h: (0, h))],
        )(first.at[span(step)], attend_all, bias_a, table.at[span(step)], queries.at[span(step)], pairs.at[span(step)])

    def expand(pumps):
        tile = 512
        out = pl.BlockSpec((total, tile), lambda j: (0, j))

        def body(n_ref, w_ref, b_ref, h_ref, d_ref):
            for when, pump in pumps.items():
                pl.when(pl.program_id(0) == when)(pump)
            for i in range(ring):
                at = pl.ds(i * rows, rows)
                expand_block_kernel(n_ref.at[at], w_ref, b_ref, h_ref.at[at], d_ref.at[at])

        pltpu.emit_pipeline(
            body,
            grid=(expand_all.shape[1] // tile,),
            in_specs=[
                pl.BlockSpec((total, width), lambda j: (0, 0)),
                pl.BlockSpec((width, tile), lambda j: (0, j)),
                pl.BlockSpec((1, tile), lambda j: (0, j)),
            ],
            out_specs=[out, out],
        )(second, expand_all, bias_e, activated, slope)

    for load in loads:
        start(load)
    start(small)
    hops.greet()
    start(a.first[0])
    start([a.core[0]])
    for i, (load, store) in enumerate(zip(loads, stores)):
        for copy in load:
            copy.wait()
        store.start()
        if i == 0:
            start([ring_x[0, 0], ring_x[0, 1], e.core[0]])
    for copy in small:
        copy.wait()
    held_gains[...] = jnp.zeros_like(held_gains)
    for i, place in enumerate(places):
        at = pl.ds(pl.multiple_of(place() * block, block), block)
        for k in range(4):
            held_gains[k : k + 1, i * block : (i + 1) * block] = gain_rows[k, :, at]
    gains_out = pltpu.make_async_copy(held_gains, gains, local.at[count + 1])
    gains_out.start()
    holder = lax.axis_index("ctx")
    after_prompt = pl.ds(pl.multiple_of(holder * total + prompt, 128), total - prompt)
    segc[...] = down(held_seg[0:1, after_prompt])
    allow_of = sequence_places(prompt, holder, held_pos, total)
    c_bits = holder // 2, holder % 2
    others = [((c_bits[0] + b) % 2) * 2 + (c_bits[1] + d) % 2 for b, d in ((1, 0), (0, 1), (1, 1))]
    held_sum[...] = jnp.broadcast_to(jnp.sum(held_g[...].astype(F32), 0, keepdims=True), held_sum.shape)
    sum_out = pltpu.make_async_copy(held_sum, grad_sum, local.at[count])
    sum_out.start()
    for store in stores + [sum_out, gains_out]:
        store.wait()
    pltpu.emit_pipeline(
        table_kernel,
        grid=(total // rows,),
        in_specs=[pl.BlockSpec((1, rows), lambda i: (0, holder * ring + i)), pl.BlockSpec((8, 128), lambda i: (0, 0))],
        out_specs=[pl.BlockSpec((rows, 384), lambda i: (i, 0))],
    )(pos_ref, freq_ref, table)
    norm(0)
    forward(ring_x, 0, 0)
    start(e.first[0])
    arrive(a.first[0])
    start(a.corner + a.core[1:3])
    forward(ring_x, 0, 1)
    norm(1)
    forward(ring_x, 1, 0)
    arrive(a.corner)
    start([a.core[3]])
    arrive(e.first[0])
    start(e.corner + e.core[1:3] + o.first[0] + [o.core[0]] + c.first[0] + c.first[1] + [c.core[0]])
    forward(ring_x, 1, 1)
    start([ring_g[0, 0], ring_g[0, 1]])
    norm(2)
    arrive(a.core)
    project(0)
    forward(ring_x, 2, 0)
    arrive(e.corner)
    start([e.core[3]])
    project(1)
    project(2)
    arrive(o.first[0])
    start(o.core[1:3])
    forward(ring_x, 2, 1)
    norm(3)
    project(3)
    start([pair_y, pair_core])
    arrive(e.core)

    def others_on():
        for copies in c.first:
            arrive(copies)
        start(c.core[1:3])

    expand({0: lambda: forward(ring_g, 0, 0), 2: others_on, 3: lambda: forward(ring_g, 0, 1)})
    arrive([pair_y])
    start([pair_corner] + o.corner + c.corner)
    arrive([pair_core, pair_corner])

    def attend_step(*args):
        step = pl.program_id(0) * pl.num_programs(1) + pl.program_id(1)
        pl.when(step == 1)(lambda: forward(ring_g, 1, 0))
        pl.when(step == 6)(lambda: forward(ring_g, 1, 1))
        attend_block(prompt, pl.program_id(1), [allow_of(i) for i in others], segc, held_seg[0:1, after_prompt], *args)

    tq = ROWS
    n_far = pairs_far.shape[0]
    pltpu.emit_pipeline(
        attend_step,
        grid=(heads, total // tq),
        in_specs=[
            pl.BlockSpec((tq, head), lambda h, b: (b, h)),
            pl.BlockSpec((total, head), lambda h, b: (0, 2 * h)),
            pl.BlockSpec((total, head), lambda h, b: (0, 2 * h + 1)),
            pl.BlockSpec((n_far, head), lambda h, b: (0, 2 * h)),
            pl.BlockSpec((n_far, head), lambda h, b: (0, 2 * h + 1)),
        ],
        out_specs=[pl.BlockSpec((tq, head), lambda h, b: (b, h)), pl.BlockSpec((1, 8, tq), lambda h, b: (h, 0, b))],
    )(queries, pairs, pairs, pairs_far, pairs_far, attended, row_sums)

    arrive(o.corner + c.corner)
    start([o.core[3], c.core[3]])
    forward(ring_g, 2, 0)
    arrive(o.core + c.core)
    tile = 512
    pltpu.emit_pipeline(
        mixed_kernel,
        grid=(width // tile,),
        in_specs=[
            pl.BlockSpec((total, attended.shape[1]), lambda j: (0, 0)),
            pl.BlockSpec((total, activated.shape[1]), lambda j: (0, 0)),
            pl.BlockSpec((tile, attended.shape[1]), lambda j: (j, 0)),
            pl.BlockSpec((tile, activated.shape[1]), lambda j: (j, 0)),
        ],
        out_specs=[pl.BlockSpec((total, tile), lambda j: (0, j))],
    )(attended, activated, output_all, contract_all, mixed)
    forward(ring_g, 2, 1)
    hops.end()


def forward_pass(places, prompt, heads, x, g, weights, gains, bias_a, bias_e, segments, positions):
    ring = lax.axis_size("tp")
    rows, width = x.shape
    total = ring * rows
    wa, we, wo, wc = weights
    head = HEAD
    hidden = we.shape[1]
    freq = 10000.0 ** (-2.0 * (np.arange(128) % (ROT // 2)) / ROT)
    freq = jnp.asarray(np.tile(freq.astype(np.float32)[None], (8, 1)))
    inputs = [x, g, wa, we, wo, wc, *gains, bias_a, bias_e, segments, positions, freq]
    outs = [
        shape(total, width), shape(total, width), shape(8, width, kind=F32),
        *(shape(8 * w.shape[0], w.shape[1]) for w in (wa, we, wo, wc)),
        shape(total, width), shape(total, width), shape(total, 128, kind=F32), shape(total, 384, kind=F32),
        shape(total, heads * head), shape(total, 2 * heads * head), shape(3 * prompt, 2 * heads * head),
        shape(total, hidden), shape(total, hidden), shape(total, heads * head), shape(heads, 8, total, kind=F32),
        shape(total, width), shape(8, width, kind=F32),
    ]
    copies = 4 * (ring - 1) + 34 + 3
    ref = pl.BlockSpec(memory_space=pl.ANY)
    return pl.pallas_call(
        partial(forward_kernel, places, prompt),
        in_specs=[ref] * len(inputs),
        out_specs=[ref] * len(outs),
        out_shape=outs,
        scratch_shapes=[
            pltpu.SemaphoreType.DMA((copies,)),
            pltpu.SemaphoreType.DMA((copies,)),
            pltpu.SemaphoreType.DMA((2 * len(places) + 18,)),
            pltpu.VMEM(x.shape, BF16),
            pltpu.VMEM(g.shape, BF16),
            pltpu.VMEM((8, width), F32),
            pltpu.VMEM((8, width), F32),
            pltpu.VMEM(segments.shape, jnp.int32),
            pltpu.VMEM(positions.shape, jnp.int32),
            pltpu.VMEM((total - prompt, 128), jnp.int32),
            pltpu.VMEM((4, 1, width), F32),
            *(pltpu.VMEM(w.shape, BF16) for w in weights),
        ],
        compiler_params=pltpu.CompilerParams(collective_id=0, has_side_effects=True, vmem_limit_bytes=56 * 2**20),
        cost_estimate=pl.CostEstimate(flops=40 * 10**9, bytes_accessed=200 * 2**20, transcendentals=10**7),
        name="forward_pass",
    )(*inputs)


class RingSum:
    def __init__(self, hops, copies, source, landing, held, last):
        t, ring = lax.axis_index("tp"), lax.axis_size("tp")
        rows = last.shape[0]
        half = rows // 2
        self.sends, self.loads, self.adds = {}, {}, {}
        for h in range(2):
            part = pl.ds(h * half, half)
            for step in range(ring - 1):
                mine = source.at[pl.ds(((t + 2 * ring - 1 - step) % ring) * rows + h * half, half)]
                src = landing[step - 1].at[part] if step else mine
                if step:
                    if held:
                        self.loads[step, h] = copies(mine, held[step - 1].at[part])
                        mine = held[step - 1].at[part]
                    self.adds[step, h] = (src, mine)
                dst = landing[step].at[part] if step < ring - 2 else last.at[part]
                self.sends[step, h] = hops.copy("up", src, dst)

    def begin(self):
        start(self.sends[0, h] for h in range(2))
        start(self.loads.values())

    def pump(self, step, h):
        arrive([self.sends[step - 1, h]])
        if self.loads:
            self.loads[step, h].wait()
        here, own = self.adds[step, h]
        here[...] = (here[...].astype(F32) + own[...].astype(F32)).astype(BF16)
        start([self.sends[step, h]])

    def finish(self, h):
        arrive([self.sends[max(step for step, _ in self.sends), h]])


class Sums:
    def __init__(self, hops, r, i):
        to_x, to_y, corner = r.to_x[i], r.to_y[i], r.corner[i]
        half = corner.shape[0] // 2
        top, low = pl.ds(0, half), pl.ds(half, half)
        self.core = hops.copy("core", r.far[i], r.core[i])
        self.corner = [hops.copy("x", corner.at[top], r.via_x[i]), hops.copy("y", corner.at[low], r.via_y[i])]
        self.plain = [hops.copy("x", to_x.at[top], r.from_x[i].at[top]), hops.copy("y", to_y.at[low], r.from_y[i].at[low])]
        self.merged = [hops.copy("x", to_x.at[low], r.from_x[i].at[low]), hops.copy("y", to_y.at[top], r.from_y[i].at[top])]
        self.pairs = [
            (self.corner[1], to_x.at[low], r.via_y[i], self.merged[0]),
            (self.corner[0], to_y.at[top], r.via_x[i], self.merged[1]),
        ]

    def merge(self):
        for came, mine, theirs, send in self.pairs:
            arrive([came])
            mine[...] = (mine[...].astype(F32) + theirs[...].astype(F32)).astype(BF16)
            start([send])

    def finish(self):
        arrive(self.plain + self.merged)


def backward_kernel(names, places, prompt, *refs):
    r = SimpleNamespace()
    for name, ref in zip(names, refs):
        if name[-1].isdigit():
            getattr(r, name[:-1]).append(ref) if hasattr(r, name[:-1]) else setattr(r, name[:-1], [ref])
        else:
            setattr(r, name, ref)
    hops = Hops(r.send, r.recv, True)
    made = []

    def local_copy(src, dst):
        made.append(pltpu.make_async_copy(src, dst, r.local.at[len(made)]))
        return made[-1]

    t, ring = lax.axis_index("tp"), lax.axis_size("tp")
    total, width = r.rows_grad.shape
    rows = total // ring
    head = HEAD
    heads = r.queries.shape[1] // head
    tq = ROWS
    cont = total - prompt
    n_far = r.pairs_far.shape[0]
    first_cont = prompt // tq
    blocks = total // tq
    holder = lax.axis_index("ctx")
    c_bits = holder // 2, holder % 2
    others = [((c_bits[0] + b) % 2) * 2 + (c_bits[1] + d) % 2 for b, d in ((1, 0), (0, 1), (1, 1))]
    seq_start = holder * total + prompt

    sum_out = RingSum(hops, local_copy, r.mixed, r.land_out, r.held_out, r.out_recv)
    sum_unit = RingSum(hops, local_copy, r.unit, r.land_unit, None, r.unit_recv)
    pair_core = [hops.copy("core", r.pair_far.at[h], r.pair_core.at[h]) for h in range(heads)]
    pair_y = [hops.copy("y", r.pair_near.at[h], r.pair_recv.at[h]) for h in range(heads)]
    grads = {w: Sums(hops, r, i) for i, w in enumerate("aeoc")}
    vector_hops = [
        hops.copy(way, r.vals.at[i, pl.ds(0, n)], r.got.at[i, pl.ds(0, n)])
        for i, (way, n) in enumerate((("core", 8), ("x", 8), ("y", 8), ("t1", 8), ("t2", 8)))
    ]
    vectors_out = local_copy(r.vals.at[len(vector_hops)], r.vectors)
    sum_load = local_copy(r.grad_sum, r.held_sum)
    grad_load = local_copy(r.rows_grad, r.grad)
    small = [local_copy(r.segments, r.held_seg), local_copy(r.positions, r.held_pos)]
    half = width // 2
    tile = 512

    def pumped(pumps):
        for when, pump in pumps.items():
            pl.when(pl.program_id(0) == when)(pump)

    def back_to_rows():
        cols = 256

        def body(w_ref, o_ref):
            for i in range(total // ROWS):
                at = pl.ds(i * ROWS, ROWS)
                o_ref[at, :] = mul(r.grad[at, :], w_ref[...], NN).astype(BF16)

        pltpu.emit_pipeline(
            body,
            grid=(heads * head // cols,),
            in_specs=[pl.BlockSpec((width, cols), lambda j: (0, j))],
            out_specs=[pl.BlockSpec((total, cols), lambda j: (0, j))],
        )(r.output_all, r.grad_att)

    def attention(pumps):
        def body(*args):
            h, block = pl.program_id(0), pl.program_id(1)
            for (at_h, at_b), pump in pumps.items():
                pl.when((h == at_h) & (block == at_b))(pump)
            outs = (r.pair_own.at[h], r.pair_near.at[h], r.pair_far.at[h])
            at = pl.multiple_of(seq_start + jnp.maximum(block - first_cont, 0) * tq, 128)
            allow_of = sequence_places(prompt, holder, r.held_pos, total)
            attend_back_block(
                prompt, block, blocks - 1, [allow_of(i) for i in others], lambda: r.segc[:, :1],
                lambda: r.held_seg[0:1, pl.ds(at, tq)], *args, *outs, r.acc_k, r.acc_v,
            )
            for k in range(heads):
                pl.when((h == k) & (block == blocks - 1))(lambda: start([pair_core[k]]))

        row = pl.BlockSpec((tq, head), lambda h, b: (b, h))

        def column(n, odd):
            return pl.BlockSpec((n, head), lambda h, b: (0, 2 * h + odd))

        pltpu.emit_pipeline(
            body,
            grid=(heads, blocks),
            in_specs=[
                row,
                row,
                row,
                pl.BlockSpec((1, 8, tq), lambda h, b: (h, 0, b)),
                column(total, 0),
                column(total, 1),
                column(n_far, 0),
                column(n_far, 1),
                pl.BlockSpec((tq, 384), lambda h, b: (b, 0)),
            ],
            out_specs=[row],
        )(
            r.queries, r.grad_att, r.attended, r.row_sums, r.pairs, r.pairs, r.pairs_far, r.pairs_far, r.table, r.grad_q,
        )

    def pair_on(h):
        arrive([pair_core[h]])
        near, theirs = r.pair_near.at[h], r.pair_core.at[h, pl.ds(prompt, prompt)]
        near[...] = (near[...].astype(F32) + theirs[...].astype(F32)).astype(BF16)
        start([pair_y[h]])

    def hidden(pumps={}):
        def body(w_ref, d_ref, gp_ref):
            pumped(pumps)
            j = pl.program_id(0)
            sums = 0.0
            for i in range(total // ROWS):
                at = pl.ds(i * ROWS, ROWS)
                grad = (mul(r.grad[at, :], w_ref[...], NN) * d_ref[at, :].astype(F32)).astype(BF16)
                gp_ref[at, :] = grad
                sums += jnp.sum(grad.astype(F32), 0, keepdims=True)
            r.vals[0, 6:7, pl.ds(pl.multiple_of(j * tile, tile), tile)] = sums

        tall = pl.BlockSpec((total, tile), lambda j: (0, j))
        pltpu.emit_pipeline(
            body,
            grid=(r.grad_pre.shape[1] // tile,),
            in_specs=[pl.BlockSpec((width, tile), lambda j: (0, j)), tall],
            out_specs=[tall],
        )(r.contract_all, r.slope, r.grad_pre)

    def far_tile(left, right, out):
        for i in range(half // ROWS):
            out[pl.ds(i * ROWS, ROWS), :] = mul(left[:, pl.ds(i * ROWS, ROWS)], right[...], TN).astype(BF16)

    def near_tile(left, right, received, own, outs, j):
        size = half // 4
        cols = pl.ds(pl.multiple_of(j * tile, tile), tile)
        for i in range(4):
            at = pl.ds(i * size, size)
            out = mul(left[:, at], right[...], TN) + received[at, :].astype(F32)
            if i:
                outs[i - 1][:, cols] = out.astype(BF16)
            else:
                own[...] = out

    def stays(i):
        return (r.to_x[i], r.to_y[i], r.corner[i])

    def far_both(pumps={}):
        steps = r.activated.shape[1] // tile

        def body(h_ref, a_ref, c_out, o_out):
            pumped(pumps)
            j = pl.program_id(0)
            left = r.grad.at[:, pl.ds(half, half)]
            pl.when(j < steps)(lambda: far_tile(left, h_ref, c_out))
            pl.when(j == steps)(lambda: far_tile(left, a_ref, o_out))

        pltpu.emit_pipeline(
            body,
            grid=(steps + 1,),
            in_specs=[
                pl.BlockSpec((total, tile), lambda j: (0, jnp.minimum(j, steps - 1))),
                pl.BlockSpec((total, tile), lambda j: (0, 0)),
            ],
            out_specs=[
                pl.BlockSpec((half, tile), lambda j: (0, jnp.minimum(j, steps - 1))),
                pl.BlockSpec((half, tile), lambda j: (0, 0)),
            ],
        )(r.activated, r.attended, r.far[3], r.far[2])
        start([grads["c"].core, grads["o"].core])

    def near_both(pumps={}):
        steps = r.activated.shape[1] // tile
        arrive([grads["c"].core, grads["o"].core])

        def body(h_ref, a_ref, c_in, o_in, c_own, o_own):
            pumped(pumps)
            j = pl.program_id(0)
            left = r.grad.at[:, pl.ds(0, half)]
            pl.when(j < steps)(lambda: near_tile(left, h_ref, c_in, c_own, stays(3), jnp.minimum(j, steps - 1)))
            pl.when(j == steps)(lambda: near_tile(left, a_ref, o_in, o_own, stays(2), 0))

        def wide_tile(rows):
            return pl.BlockSpec((rows, tile), lambda j: (0, jnp.minimum(j, steps - 1)))

        def one_tile(rows):
            return pl.BlockSpec((rows, tile), lambda j: (0, 0))

        pltpu.emit_pipeline(
            body,
            grid=(steps + 1,),
            in_specs=[wide_tile(total), one_tile(total), wide_tile(half), one_tile(half)],
            out_specs=[wide_tile(half // 4), one_tile(half // 4)],
        )(r.activated, r.attended, r.core[3], r.core[2], r.own[3], r.own[2])

    def far(i, left, right, pumps={}):
        def body(a_ref, b_ref, out):
            pumped(pumps)
            far_tile(a_ref, b_ref, out)

        pltpu.emit_pipeline(
            body,
            grid=(right.shape[1] // tile,),
            in_specs=[pl.BlockSpec((total, half), lambda j: (0, 1)), pl.BlockSpec((total, tile), lambda j: (0, j))],
            out_specs=[pl.BlockSpec((half, tile), lambda j: (0, j))],
        )(left, right, r.far[i])

    def near(i, left, right, pumps={}):
        def body(a_ref, b_ref, received, own):
            pumped(pumps)
            near_tile(a_ref, b_ref, received, own, stays(i), pl.program_id(0))

        pltpu.emit_pipeline(
            body,
            grid=(right.shape[1] // tile,),
            in_specs=[
                pl.BlockSpec((total, half), lambda j: (0, 0)),
                pl.BlockSpec((total, tile), lambda j: (0, j)),
                pl.BlockSpec((half, tile), lambda j: (0, j)),
            ],
            out_specs=[pl.BlockSpec((half // 4, tile), lambda j: (0, j))],
        )(left, right, r.core[i], r.own[i])

    def pack_pairs():
        def body(*args):
            pack_block(pl.program_id(0), pl.program_id(1), r, *args)

        pltpu.emit_pipeline(
            body,
            grid=(heads, 2),
            in_specs=[pl.BlockSpec((prompt, head), lambda h, b: (b, h)), pl.BlockSpec((prompt, 384), lambda h, b: (b, 0))],
            out_specs=[pl.BlockSpec((prompt, 3 * head), lambda h, b: (b, h))],
        )(r.grad_q, r.table, r.grad_flat)

    def unit_pair(step, pumps={}):
        chunks = [(t + 2 * ring - 1 - step - i) % ring for i in range(2)]
        spans = [pl.ds(chunk * rows, rows) for chunk in chunks]

        def body(wa_ref, we_ref, gain_ref, *args):
            pumped(pumps)
            j = pl.program_id(0)
            cols = pl.ds(pl.multiple_of(j * tile, tile), tile)
            sums = [0.0] * 4
            for i in range(2):
                gp_ref, gh_ref, x_ref, stat_ref = args[4 * i : 4 * i + 4]
                one = mul(gp_ref[...], wa_ref[...], NT)
                two = mul(gh_ref[...], we_ref[...], NT)
                r.unit[spans[i], cols] = (one * gain_ref[0:1] + two * gain_ref[2:3]).astype(BF16)
                scaled = (x_ref[...].astype(F32) - stat_ref[:, 0:1]) * stat_ref[:, 1:2]
                for k, v in enumerate((one * scaled, one, two * scaled, two)):
                    sums[k] += jnp.sum(v, 0, keepdims=True)
            for k in range(4):
                r.vec[k : k + 1, cols] += sums[k]

        deep, deeper = r.grad_flat.shape[1], r.grad_pre.shape[1]
        rows_specs = [
            pl.BlockSpec((rows, deep), lambda j: (0, 0)),
            pl.BlockSpec((rows, deeper), lambda j: (0, 0)),
            pl.BlockSpec((rows, tile), lambda j: (0, j)),
            pl.BlockSpec((rows, 128), lambda j: (0, 0)),
        ]
        pltpu.emit_pipeline(
            body,
            grid=(width // tile,),
            in_specs=[
                pl.BlockSpec((tile, deep), lambda j: (j, 0)),
                pl.BlockSpec((tile, deeper), lambda j: (j, 0)),
                pl.BlockSpec((8, tile), lambda j: (0, j)),
                *rows_specs,
                *rows_specs,
            ],
            out_specs=[],
        )(
            r.attend_all, r.expand_all, r.gains,
            *(ref.at[at] for at in spans for ref in (r.grad_flat, r.grad_pre, r.rows_in, r.stat)),
        )

    def vectors_begin():
        size = width // len(places)
        for i, place in enumerate(places):
            to = pl.ds(pl.multiple_of(place() * size, size), size)
            r.vals[0, 0:4, to] = r.vec[0:4, i * size : (i + 1) * size]
            r.vals[0, 4:5, to] = r.held_sum[0:1, i * size : (i + 1) * size]
        start(vector_hops[:1])

    def vectors_on(i):
        arrive([vector_hops[i]])
        n = 8 if i < 3 else 5
        r.vals[i + 1, :, :] = r.vals[i, :, :]
        r.vals[i + 1, 0:n, :] += r.got[i, 0:n, :]
        start(vector_hops[i + 1 : i + 2] or [vectors_out])

    c, o, e, a = (grads[w] for w in "coea")
    hops.greet()
    start([grad_load])
    sum_out.begin()
    start([sum_load, *small])
    r.vals[0, :, :] = jnp.zeros_like(r.vals[0, :, :])
    r.vec[...] = jnp.zeros_like(r.vec)
    grad_load.wait()
    sum_load.wait()
    for copy in small:
        copy.wait()
    r.segc[...] = down(r.held_seg[0:1, pl.ds(pl.multiple_of(seq_start, 128), cont)])

    far_both()
    back_to_rows()
    sum_out.pump(1, 0)
    near_both({4: lambda: sum_out.pump(1, 1)})
    start(c.corner + o.corner + c.plain[:1] + o.plain[:1])
    attention({(1, 0): lambda: sum_out.pump(2, 0), (1, 1): lambda: pair_on(0), (1, 3): lambda: sum_out.pump(2, 1)})
    pair_on(1)
    hidden()
    arrive(pair_y)
    start(c.plain[1:] + o.plain[1:])
    pack_pairs()
    c.merge()
    o.merge()
    far(1, r.second, r.grad_pre)
    start([e.core])
    unit_pair(0)
    sum_unit.begin()
    arrive([e.core])
    near(1, r.second, r.grad_pre)
    start(e.corner + e.plain)
    unit_pair(2, {1: lambda: sum_unit.pump(1, 0), 2: lambda: sum_unit.pump(1, 1), 3: e.merge})
    vectors_begin()
    far(0, r.first, r.grad_flat, {2: lambda: vectors_on(0)})
    start([a.core])
    sum_unit.pump(2, 0)
    arrive([a.core])
    near(0, r.first, r.grad_flat, {1: lambda: sum_unit.pump(2, 1), 2: lambda: vectors_on(1)})
    start(a.corner + a.plain)
    vectors_on(2)
    vectors_on(3)
    a.merge()
    vectors_on(4)
    for h in range(2):
        sum_out.finish(h)
    for w in "coea":
        grads[w].finish()
    here = pl.ds(t * rows, rows)
    own_unit = local_copy(r.unit.at[here], r.unit_own)
    start([own_unit])
    for h in range(2):
        sum_unit.finish(h)
    vectors_out.wait()
    own_unit.wait()
    hops.end()


def pack_block(h, block, r, q_ref, table_ref, o_ref):
    tq, head = q_ref.shape
    theirs = r.pair_recv[h].astype(F32) + r.pair_core[h, :tq, :].astype(F32)
    own = r.pair_own[h, pl.ds(pl.multiple_of(block * tq, tq), tq), :]
    both = own + jnp.where(block == 0, theirs, 0.0)
    out = [q_ref[...], turn(both[:, :head], table_ref[...], -1.0).astype(BF16), both[:, head:].astype(BF16)]
    for i, part in enumerate(out):
        o_ref[:, i * head : (i + 1) * head] = part
        at = pl.ds(pl.multiple_of((h * 3 + i) * head, head), head)
        r.vals[0, 5:6, at] += jnp.sum(part.astype(F32), 0, keepdims=True)


def backward_pass(places, prompt, values, segments, positions):
    total, width = values["rows_grad"].shape
    ring = lax.axis_size("tp")
    rows = total // ring
    heads, _, _ = values["row_sums"].shape
    head = HEAD
    cont = total - prompt
    far = values["pairs_far"].shape[0]
    inputs = dict(values, segments=segments, positions=positions)
    hidden = values["slope"].shape[1]
    columns = [3 * heads * head, hidden, heads * head, hidden]
    half, size = width // 2, width // 8
    outs = {
        "out_recv": shape(rows, width),
        "unit_recv": shape(rows, width),
        "unit_own": shape(rows, width),
        "vectors": shape(8, width, kind=F32),
        "grad_att": shape(total, heads * head),
        "grad_q": shape(total, heads * head),
        "grad_flat": shape(total, 3 * heads * head),
        "grad_pre": shape(total, hidden),
    }
    stay = {}
    for i, cols in enumerate(columns):
        outs[f"own{i}"] = shape(size, cols, kind=F32)
        for name, n in (("far", half), ("core", half), ("from_x", size), ("from_y", size)):
            outs[f"{name}{i}"] = shape(n, cols)
        for name, n in (("to_x", size), ("to_y", size), ("corner", size), ("via_x", size // 2), ("via_y", size // 2)):
            stay[f"{name}{i}"] = pltpu.VMEM((n, cols), BF16)
    copies = 4 * (ring - 1) + 2 * heads + 7 * len(columns) + 5
    block = pltpu.VMEM((rows, width), BF16)
    scratch = {
        "send": pltpu.SemaphoreType.DMA((copies,)),
        "recv": pltpu.SemaphoreType.DMA((copies,)),
        "local": pltpu.SemaphoreType.DMA((2 * (ring - 2) + 6,)),
        "held_seg": pltpu.VMEM(segments.shape, jnp.int32),
        "held_pos": pltpu.VMEM(positions.shape, jnp.int32),
        "segc": pltpu.VMEM((cont, 128), jnp.int32),
        "grad": pltpu.VMEM((total, width), BF16),
        "unit": pltpu.VMEM((total, width), BF16),
        "pair_own": pltpu.VMEM((heads, total, 2 * head), F32),
        "pair_near": pltpu.VMEM((heads, prompt, 2 * head), BF16),
        "pair_far": pltpu.VMEM((heads, 2 * prompt, 2 * head), BF16),
        "pair_core": pltpu.VMEM((heads, 2 * prompt, 2 * head), BF16),
        "pair_recv": pltpu.VMEM((heads, prompt, 2 * head), BF16),
        **stay,
        "acc_k": pltpu.VMEM((total + far, head), F32),
        "acc_v": pltpu.VMEM((total + far, head), F32),
        "vals": pltpu.VMEM((6, 8, width), F32),
        "got": pltpu.VMEM((5, 8, width), F32),
        "vec": pltpu.VMEM((8, width), F32),
        "held_sum": pltpu.VMEM((8, width), F32),
    }
    for name in ("land_out", "held_out", "land_unit"):
        for i in range(ring - 2):
            scratch[f"{name}{i}"] = block
    names = [*inputs, *outs, *scratch]
    ref = pl.BlockSpec(memory_space=pl.ANY)
    result = pl.pallas_call(
        partial(backward_kernel, names, places, prompt),
        in_specs=[ref] * len(inputs),
        out_specs=[ref] * len(outs),
        out_shape=list(outs.values()),
        scratch_shapes=list(scratch.values()),
        compiler_params=pltpu.CompilerParams(collective_id=1, has_side_effects=True, vmem_limit_bytes=60 * 2**20),
        cost_estimate=pl.CostEstimate(flops=60 * 10**9, bytes_accessed=200 * 2**20, transcendentals=10**7),
        name="backward_pass",
    )(*inputs.values())
    return dict(zip(outs, result))


class SquareLinks:
    order = ((0, 0, 0), (1, 0, 0), (0, 1, 0), (1, 1, 0), (0, 0, 1), (1, 0, 1), (0, 1, 1), (1, 1, 1))

    def place(self, bits):
        f, c = lax.axis_index("fsdp"), lax.axis_index("ctx")
        a, b, d = bits
        return ((f ^ a) * 2 + ((c // 2) ^ b)) * 2 + ((c % 2) ^ d)

    def spot(self, p):
        f, c = lax.axis_index("fsdp"), lax.axis_index("ctx")
        a, b, d = f ^ (p // 4), (c // 2) ^ (p // 2 % 2), (c % 2) ^ (p % 2)
        return d * 4 + b * 2 + a

    def places(self):
        return [partial(self.place, bits) for bits in self.order]

    def spots(self):
        return [partial(self.spot, p) for p in range(8)]


class AnyLinks:
    def places(self):
        return [lambda: 0]

    def spots(self):
        return [lambda: 0]

    def gather(self, block):
        return lax.all_gather(block, ("fsdp", "ctx"), axis=0, tiled=True)

    def scatter(self, whole):
        return lax.psum_scatter(whole, ("fsdp", "ctx"), scatter_dimension=0, tiled=True).astype(F32)

    def others(self, v):
        return jnp.roll(v, -lax.axis_index("ctx"), 0)[1:]

    def gather_others(self, block):
        rows = block.shape[0]
        whole = lax.all_gather(block, "ctx", axis=0, tiled=True)
        return jnp.roll(whole, -rows * lax.axis_index("ctx"), 0)[rows:]

    def scatter_others(self, near, far):
        rows = near.shape[0]
        whole = jnp.concatenate([jnp.zeros_like(near), near, far], 0)
        whole = jnp.roll(whole, rows * lax.axis_index("ctx"), 0)
        return lax.psum_scatter(whole, "ctx", scatter_dimension=0, tiled=True)


def end_kernel(spots, n, x_ref, g_ref, m_ref, o_ref, e_ref, f_ref, b_ref, *refs):
    parts, outs, e_whole = refs[: 3 * n], refs[3 * n : -1], refs[-1]
    out_ref, grad_ref, sums = outs[0], outs[1], outs[2:]
    size = x_ref.shape[1] // len(spots)
    for i, spot in enumerate(spots):
        at, to = pl.ds(pl.multiple_of(spot() * size, size), size), pl.ds(i * size, size)
        branches = m_ref[:, at].astype(F32) + o_ref[:, at].astype(F32)
        out_ref[:, to] = (x_ref[:, to].astype(F32) + branches + b_ref[:1, to]).astype(BF16)
        e_whole[:, to] = e_ref[:, at].astype(F32) + f_ref[:, at].astype(F32)
    x = x_ref[...].astype(F32)
    center = x - jnp.mean(x, -1, keepdims=True)
    scale = lax.rsqrt(jnp.mean(center * center, -1, keepdims=True) + EPS)
    unit = center * scale
    e = e_whole[...]
    rest = e - jnp.mean(e, -1, keepdims=True) - unit * jnp.mean(e * unit, -1, keepdims=True)
    grad_ref[...] = g_ref[...].astype(F32) + scale * rest
    for i, out in enumerate(sums):
        own, one, two = parts[3 * i : 3 * i + 3]
        total = own[...] + one[...].astype(F32) + two[...].astype(F32)
        if len(out.shape) == 3:
            for h in range(out.shape[1]):
                out[:, h, :] = total[:, h * out.shape[2] : (h + 1) * out.shape[2]]
        else:
            out[...] = total


def row_results(x, g, mixed, mixed_own, unit, unit_own, bias, spots, weights=(), shapes=()):
    rows, width = x.shape
    tile = 32

    def block(dims):
        return pl.BlockSpec((tile, *dims[1:]), lambda i: (i,) + (0,) * (len(dims) - 1))

    own = pl.BlockSpec((tile, width), lambda i: (lax.axis_index("tp") * (rows // tile) + i, 0))
    parts = [part for weight in weights for part in weight]
    outs = [shape(rows, width), shape(rows, width, kind=F32)] + [shape(*dims, kind=F32) for dims in shapes]
    return call(
        partial(end_kernel, spots, len(weights)),
        (rows // tile,),
        [block(x.shape)] * 3 + [own] + [block(x.shape)] * 2 + [pl.BlockSpec((1, width), lambda i: (0, 0))] + [block(p.shape) for p in parts],
        [block(out.shape) for out in outs],
        outs,
        15 * x.size,
        18 * x.size + 12 * sum(p.size for p in parts),
        scratch=[pltpu.VMEM((tile, width), F32)],
        mib=60,
        name="row_results",
    )(x, g, mixed, mixed_own, unit, unit_own, bias[None], *parts)


def shards(
    stream_in,
    stream_grad,
    segments,
    positions,
    first_gain,
    first_shift,
    second_gain,
    second_shift,
    attend_weight,
    attend_bias,
    output_weight,
    expand_weight,
    expand_bias,
    contract_weight,
    output_bias,
):
    square = (lax.axis_size("fsdp"), lax.axis_size("ctx"), lax.axis_size("tp")) == (2, 4, 4)
    links = SquareLinks() if square else AnyLinks()
    local_rows = attend_weight.shape[0]
    heads = attend_bias.shape[0]
    holders = lax.axis_size("ctx")
    holder = lax.axis_index("ctx")
    prompt = PROMPT // holders

    row_count = stream_in.shape[0] * lax.axis_size("tp")
    weights = (attend_weight.reshape(local_rows, -1), expand_weight, output_weight, contract_weight)

    forward_names = (
        "rows_in",
        "rows_grad",
        "gains",
        "attend_all",
        "expand_all",
        "output_all",
        "contract_all",
        "first",
        "second",
        "stat",
        "table",
        "queries",
        "pairs",
        "pairs_far",
        "activated",
        "slope",
        "attended",
        "row_sums",
        "mixed",
        "grad_sum",
    )
    weight_grads = None
    if square:
        rows_of = (v[None] for v in (first_gain, first_shift, second_gain, second_shift))
        made = forward_pass(
            links.places(), prompt, heads, stream_in, stream_grad, weights, [*rows_of], attend_bias.reshape(1, -1),
            expand_bias[None], segments[None], positions[None],
        )
        values = dict(zip(forward_names, made))
        back = backward_pass(links.places(), prompt, values, segments[None], positions[None])
        sums = (back["out_recv"], values["mixed"], back["unit_recv"], back["unit_own"])
        parts = [(back[f"own{i}"], back[f"from_x{i}"], back[f"from_y{i}"]) for i in range(4)]
        shapes = [w.shape for w in (attend_weight, expand_weight, output_weight, contract_weight)]
        vectors = back["vectors"]
        norm_sums = [vectors[i] for i in range(5)]
        bias_sums = [vectors[5, : attend_bias.size], vectors[6]]
    else:
        gains = jnp.concatenate([jnp.stack([first_gain, first_shift, second_gain, second_shift]), jnp.zeros((4, first_gain.shape[0]), F32)])
        row_pos = lax.dynamic_slice_in_dim(positions, holder * row_count, row_count)
        row_seg = lax.dynamic_slice_in_dim(segments, holder * row_count, row_count)
        starts = positions.reshape(holders, row_count)[:, 0]
        bias = jnp.where(links.others(starts) < row_pos[0], 0.0, -1e30).astype(F32)
        bias = jnp.broadcast_to(jnp.pad(bias, (0, 8 - bias.shape[0]))[:, None], (8, 128))
        rows_in, rows_grad = (lax.all_gather(v, "tp", axis=0, tiled=True) for v in (stream_in, stream_grad))
        attend_all, expand_all, output_all, contract_all = (links.gather(v) for v in weights)
        table = turn_table(row_pos)
        first, second, rows_in, stat = norms(rows_in, gains, links.places())
        queries, pairs = project(first, attend_all, attend_bias.reshape(-1), table, heads)
        pairs_far = links.gather_others(pairs[:prompt])
        activated, slope = expand(second, expand_all, expand_bias)
        attended, row_sums = attend(queries, pairs, pairs_far, bias, row_seg, prompt)
        mixed = mixed_sum(attended, activated, output_all, contract_all)
        branches = lax.psum_scatter(mixed, "tp", scatter_dimension=0, tiled=True)
        grad_attended = attended_grads(rows_grad, output_all)
        grad_queries, pair_own, pair_near, pair_far = attend_back(
            queries, grad_attended, attended, row_sums, pairs, pairs_far, bias, row_seg, prompt, table
        )
        theirs = links.scatter_others(pair_near, pair_far)
        grad_pre, expand_sums = hidden_grads(rows_grad, contract_all, slope)
        grad_flat, attend_sums = pack(grad_queries, pair_own, theirs, jnp.zeros_like(theirs), table, prompt)
        unit, vector_parts = unit_grads(grad_flat, grad_pre, attend_all, expand_all, rows_in, stat, gains)
        unit_part = lax.psum_scatter(unit, "tp", scatter_dimension=0, tiled=True)
        weight_grads = [
            links.scatter(jnp.einsum("tc,tk->ck", left, right, preferred_element_type=F32).astype(BF16))
            for left, right in ((first, grad_flat), (second, grad_pre), (rows_grad, attended), (rows_grad, activated))
        ]
        row_sum = jnp.sum(stream_grad.astype(F32), 0)
        norm_sums = lax.psum([*vector_parts[:4], row_sum], ("fsdp", "ctx", "tp"))
        bias_sums = lax.psum([attend_sums[0], expand_sums[0]], ("fsdp", "ctx"))
        parts, shapes = (), ()
        sums = (branches, jnp.zeros((row_count, stream_in.shape[1]), BF16), unit_part, jnp.zeros_like(unit_part))
    stream_out, input_grad, *summed = row_results(
        stream_in, stream_grad, *sums, output_bias, links.spots(), parts, shapes
    )
    weight_grads = summed or weight_grads
    return (
        stream_out,
        input_grad,
        *norm_sums[:4],
        weight_grads[0].reshape(attend_weight.shape),
        bias_sums[0].reshape(attend_bias.shape),
        weight_grads[2],
        weight_grads[1],
        bias_sums[1],
        weight_grads[3],
        norm_sums[4],
    )


def solution(mesh):
    tokens = P(("fsdp", "ctx", "tp"), None)
    weight = P(("fsdp", "ctx"), "tp")
    heads = P(("fsdp", "ctx"), "tp", None)
    return jax.shard_map(
        shards,
        mesh=mesh,
        in_specs=(
            tokens,
            tokens,
            P("fsdp"),
            P("fsdp"),
            P(),
            P(),
            P(),
            P(),
            heads,
            P("tp", None),
            weight,
            weight,
            P("tp"),
            weight,
            P(),
        ),
        out_specs=(
            tokens,
            tokens,
            P(),
            P(),
            P(),
            P(),
            heads,
            P("tp", None),
            weight,
            weight,
            P("tp"),
            weight,
            P(),
        ),
        check_vma=False,
    )
```
